32 devices in a mesh: dp: 8 (over z, core), mp: 4 (over y, x).
Axes of the slice: x: 2, y: 2, z: 4, core: 2. Of those that a mesh axis runs over, the one named last changes fastest.
Arguments:
- inputs: bfloat16 [65536, 1024], P(('dp', 'mp')), may hold values from -6 to 6
- first_gain: bfloat16 [1024], P('mp'), may hold values from 0.5 to 1.5
- first_shift: bfloat16 [1024], P('mp'), may hold values from -2 to 2
- in_weight: bfloat16 [1024, 3072], P('mp'), may hold values from -0.1875 to 0.1875
- in_bias: bfloat16 [3072], P('mp'), may hold values from -2 to 2
- short_weight: bfloat16 [3, 3072], P(None, 'mp'), may hold values from -3 to 3
- skip_gain: bfloat16 [1024], P('mp'), may hold values from -4 to 4
- pos_weight: float32 [33, 64], replicated, may hold values from -1 to 1
- pos_bias: float32 [64], replicated, may hold values from -3.140625 to 3.140625
- mid_weight: float32 [64, 64], replicated, may hold values from -0.75 to 0.75
- mid_bias: float32 [64], replicated, may hold values from -3.140625 to 3.140625
- filter_weight: float32 [64, 1024], replicated, may hold values from -0.015625 to 0.015625
- decay_rates: float32 [1024], replicated, may hold values from 0.5 to 64
- out_weight: bfloat16 [1024, 1024], P('mp'), may hold values from -0.1875 to 0.1875
- out_bias: bfloat16 [1024], P('mp'), may hold values from -2 to 2
- second_gain: bfloat16 [1024], P('mp'), may hold values from 0.5 to 1.5
- second_shift: bfloat16 [1024], P('mp'), may hold values from -2 to 2
- up_weight: bfloat16 [1024, 4096], P('mp'), may hold values from -0.1875 to 0.1875
- up_bias: bfloat16 [4096], P('mp'), may hold values from -2 to 2
- down_weight: bfloat16 [4096, 1024], P('mp'), may hold values from -0.09375 to 0.09375
- down_bias: bfloat16 [1024], P('mp'), may hold values from -2 to 2
- cotangent: bfloat16 [65536, 1024], P(('dp', 'mp')), may hold values from -6 to 6
Outputs:
- block_out: bfloat16 [65536, 1024], P(('dp', 'mp'))
- input_grad: bfloat16 [65536, 1024], P(('dp', 'mp'))
- first_gain_grad: float32 [1024], P('mp')
- first_shift_grad: float32 [1024], P('mp')
- in_weight_grad: float32 [1024, 3072], P('mp')
- in_bias_grad: float32 [3072], P('mp')
- short_weight_grad: float32 [3, 3072], P(None, 'mp')
- skip_gain_grad: float32 [1024], P('mp')
- pos_weight_grad: float32 [33, 64], replicated
- pos_bias_grad: float32 [64], replicated
- mid_weight_grad: float32 [64, 64], replicated
- mid_bias_grad: float32 [64], replicated
- filter_weight_grad: float32 [64, 1024], replicated
- out_weight_grad: float32 [1024, 1024], P('mp')
- out_bias_grad: float32 [1024], P('mp')
- second_gain_grad: float32 [1024], P('mp')
- second_shift_grad: float32 [1024], P('mp')
- up_weight_grad: float32 [1024, 4096], P('mp')
- up_bias_grad: float32 [4096], P('mp')
- down_weight_grad: float32 [4096, 1024], P('mp')
- down_bias_grad: float32 [1024], P('mp')
The draws below stay inside these ranges and needn't reach their ends.
All inputs are finite; a program needn't handle non-finite values.
Results may differ from the reference program's by a relative error of at most 0.02.
Values may be sent and summed in bfloat16 or wider, within the bound.
A program may use at most 576 MiB of HBM per device.

```python
import math
import jax
import jax.numpy as jnp
from jax import lax

D = 1024
FF = 4096
FW = 64
BANDS = 16
FEAT = 33
L = 2048
TOKENS = 65536


def steps_of(key, extent, shards, low, largest):
    def one(position, parts):
        steps = jax.random.uniform(jax.random.fold_in(jax.random.fold_in(key, 6), position), (parts,), jnp.float32, low / len(shards), largest / len(shards))
        return jnp.repeat(jnp.exp(steps), extent[position] // parts).reshape((-1,) + (1,) * (len(extent) - position - 1))

    level = one(*shards[0])
    for cut in shards[1:]:
        level = level * one(*cut)
    return level


def gaussian(own_key, shape, deviation, bound, cuts=(), held_as=jnp.bfloat16):
    level = steps_of(own_key, shape, cuts, -0.22, 0.18) if cuts else 1.0
    entries = jax.random.normal(own_key, shape, jnp.float32) * deviation * level
    return jnp.minimum(jnp.maximum(entries, -bound), bound).astype(held_as)


def setup_inputs(seed: int = 0) -> dict:
    key_of = jax.random.split(jax.random.key(seed), 23)
    return {
        "inputs": gaussian(key_of[0], (TOKENS, D), 1.0, 6.0, ((0, 32),)),
        "first_gain": jnp.clip(1.0 + 0.1 * jax.random.normal(key_of[1], (D,), jnp.float32), 0.5, 1.5).astype(jnp.bfloat16),
        "first_shift": gaussian(key_of[2], (D,), 0.3, 2.0, ((0, 4),)),
        "in_weight": gaussian(key_of[3], (D, 3 * D), D ** -0.5, 0.1875, ((0, 4),)),
        "in_bias": gaussian(key_of[4], (3 * D,), 0.3, 2.0, ((0, 4),)),
        "short_weight": gaussian(key_of[5], (3, 3 * D), 0.6, 3.0, ((1, 4),)),
        "skip_gain": gaussian(key_of[6], (D,), 1.0, 4.0, ((0, 4),)),
        "pos_weight": gaussian(key_of[7], (FEAT, FW), FEAT ** -0.5, 1.0, (), jnp.float32),
        "pos_bias": jnp.clip(jax.random.uniform(key_of[8], (FW,), jnp.float32, -3.140625, 3.140625), -3.140625, 3.140625),
        "mid_weight": gaussian(key_of[9], (FW, FW), FW ** -0.5, 0.75, (), jnp.float32),
        "mid_bias": jnp.clip(jax.random.uniform(key_of[10], (FW,), jnp.float32, -3.140625, 3.140625), -3.140625, 3.140625),
        "filter_weight": gaussian(key_of[11], (FW, D), (FW * L) ** -0.5, 0.015625, (), jnp.float32),
        "decay_rates": jnp.clip(jnp.exp(jax.random.uniform(key_of[12], (D,), jnp.float32, math.log(0.5), math.log(64.0))), 0.5, 64.0),
        "out_weight": gaussian(key_of[13], (D, D), D ** -0.5, 0.1875, ((0, 4),)),
        "out_bias": gaussian(key_of[14], (D,), 0.3, 2.0, ((0, 4),)),
        "second_gain": jnp.clip(1.0 + 0.1 * jax.random.normal(key_of[15], (D,), jnp.float32), 0.5, 1.5).astype(jnp.bfloat16),
        "second_shift": gaussian(key_of[16], (D,), 0.3, 2.0, ((0, 4),)),
        "up_weight": gaussian(key_of[17], (D, FF), D ** -0.5, 0.1875, ((0, 4),)),
        "up_bias": gaussian(key_of[18], (FF,), 0.3, 2.0, ((0, 4),)),
        "down_weight": gaussian(key_of[19], (FF, D), FF ** -0.5, 0.09375, ((0, 4),)),
        "down_bias": gaussian(key_of[20], (D,), 0.3, 2.0, ((0, 4),)),
        "cotangent": gaussian(key_of[21], (TOKENS, D), 1.0, 6.0, ((0, 32),)),
    }


@jax.custom_vjp
def low(v):
    return lax.optimization_barrier(v.astype(jnp.bfloat16)).astype(jnp.float32)

@jax.custom_vjp
def lowered_backward(v):
    return v

def low_keep(v):
    return (low(v), None)

def low_pass(kept, grad):
    return (grad,)

def back_keep(v):
    return (v, None)

def back_low(kept, grad):
    return (low(grad),)
low.defvjp(low_keep, low_pass)
lowered_backward.defvjp(back_keep, back_low)
HIGH_ACCURACY = lax.Precision.HIGHEST
eps = 1e-05
decay_floor = 0.05

def positions_table(start, count):
    places = (start + jnp.arange(count)).astype(jnp.float32)
    harmonics = jnp.arange(1, BANDS + 1).astype(jnp.float32)
    angles = 2.0 * math.pi / L * places[:, None] * harmonics[None, :]
    return (places, jnp.concatenate([places[:, None] / L, jnp.cos(angles), jnp.sin(angles)], axis=1))

def filter_values(start, count, network, rates):
    pos_weight, pos_bias, mid_weight, mid_bias, filter_weight = network
    places, features = positions_table(start, count)
    first_layer = jnp.sin(jnp.dot(features, pos_weight, precision=HIGH_ACCURACY) + pos_bias)
    second_layer = jnp.sin(jnp.dot(first_layer, mid_weight, precision=HIGH_ACCURACY) + mid_bias)
    shaped = jnp.dot(second_layer, filter_weight, precision=HIGH_ACCURACY)
    return shaped * (jnp.exp(-rates[None, :] * places[:, None] / L) + decay_floor)

def layer_norm(values, gain, shift):
    centre = lax.optimization_barrier(jnp.mean(values, axis=-1, keepdims=True))
    centred = values - centre
    return centred * lax.rsqrt(lax.optimization_barrier(jnp.mean(centred * centred, axis=-1, keepdims=True)) + eps) * gain + shift

def long_conv(filters, signal):
    padded_len = 2 * L
    spec = jnp.fft.rfft(signal, n=padded_len, axis=1) * jnp.fft.rfft(filters, n=padded_len, axis=0)[None]
    return jnp.fft.irfft(spec, n=padded_len, axis=1)[:, :L]

def block(dense, filters, input_tokens):
    gain_one, shift_one, in_matrix, in_projection_bias, w_short, skip_all, out_matrix, out_projection_bias, gain_two, shift_two, up_matrix, up_projection_bias, down_matrix, down_projection_bias = dense
    first_normalized = low(layer_norm(input_tokens, gain_one, shift_one))
    projected_rows = lowered_backward(jnp.einsum('qcr,ro->qco', first_normalized, in_matrix, precision=HIGH_ACCURACY) + in_projection_bias)
    before = jnp.pad(projected_rows, ((0, 0), (2, 0), (0, 0)))
    short_out = w_short[0] * projected_rows + w_short[1] * before[:, 1:-1] + w_short[2] * before[:, :-2]
    out_gate = short_out[..., :D]
    in_gate = short_out[..., D:2 * D]
    signal = short_out[..., 2 * D:]
    gated_val = low(in_gate * signal)
    long_out = lowered_backward(long_conv(filters, gated_val))
    branch_output = low(out_gate * (long_out + skip_all * gated_val))
    residual_stream = input_tokens + lowered_backward(jnp.einsum('qcr,ro->qco', branch_output, out_matrix, precision=HIGH_ACCURACY) + out_projection_bias)
    second_normalized = low(layer_norm(residual_stream, gain_two, shift_two))
    hidden_rows = lowered_backward(jnp.einsum('ikz,zm->ikm', second_normalized, up_matrix, precision=HIGH_ACCURACY) + up_projection_bias)
    activated_rows = low(jax.nn.gelu(hidden_rows, approximate=False))
    return residual_stream + jnp.einsum('xom,mk->xok', activated_rows, down_matrix, precision=HIGH_ACCURACY) + down_projection_bias

def reference(inputs, first_gain, first_shift, in_weight, in_bias, short_weight, skip_gain, pos_weight, pos_bias, mid_weight, mid_bias, filter_weight, decay_rates, out_weight, out_bias, second_gain, second_shift, up_weight, up_bias, down_weight, down_bias, cotangent):
    dense = tuple((item.astype(jnp.float32) for item in (first_gain, first_shift, in_weight, in_bias, short_weight, skip_gain, out_weight, out_bias, second_gain, second_shift, up_weight, up_bias, down_weight, down_bias)))
    network = (pos_weight, pos_bias, mid_weight, mid_bias, filter_weight)

    def make_filter(weights):
        return low(filter_values(0, L, weights, decay_rates))
    filters, filter_back = jax.vjp(make_filter, network)
    seq_total = TOKENS // L
    group_size = 2 if seq_total % 2 == 0 else 1
    tokens_all = inputs.astype(jnp.float32).reshape(seq_total // group_size, group_size, L, D)
    cot_all = cotangent.astype(jnp.float32).reshape(seq_total // group_size, group_size, L, D)

    def step(carry, batch):
        dense_sum, filter_sum = carry
        input_tokens, cot_in = batch
        out_vals, back = jax.vjp(block, dense, filters, input_tokens)
        dense_grad, filter_grad, token_grad = back(cot_in)
        dense_sum = jax.tree.map(lambda left, right: left + right, dense_sum, dense_grad)
        return ((dense_sum, filter_sum + filter_grad), (out_vals.astype(jnp.bfloat16), token_grad.astype(jnp.bfloat16)))
    start_carry = (jax.tree.map(jnp.zeros_like, dense), jnp.zeros_like(filters))
    (dense_sum, filter_sum), (outs_all, grads_all) = lax.scan(step, start_carry, (tokens_all, cot_all))
    net_grads = filter_back(filter_sum)[0]
    return (outs_all.reshape(TOKENS, D), grads_all.reshape(TOKENS, D), dense_sum[0], dense_sum[1], dense_sum[2], dense_sum[3], dense_sum[4], dense_sum[5], net_grads[0], net_grads[1], net_grads[2], net_grads[3], net_grads[4], dense_sum[6], dense_sum[7], dense_sum[8], dense_sum[9], dense_sum[10], dense_sum[11], dense_sum[12], dense_sum[13])
```

```python
import functools
import math

import jax
import jax.numpy as jnp
import numpy as np
from jax import lax
from jax.experimental import pallas as pl
from jax.experimental.pallas import tpu as pltpu
from jax.sharding import PartitionSpec as P

D = 1024
FF = 4096
BANDS = 16
L = 2048
PH = 4
ML = L // PH
TILE = 256
PAD = 8

HIGH_ACCURACY = lax.Precision.HIGHEST
eps = 1e-05
decay_floor = 0.05
F32 = jnp.float32
BF16 = jnp.bfloat16
VMEM_BYTES = 62 << 20


def dot_nn(a, b):
    return lax.dot_general(a, b, (((1,), (0,)), ((), ())), preferred_element_type=F32)


def dot_nt(a, b):
    return lax.dot_general(a, b, (((1,), (1,)), ((), ())), preferred_element_type=F32)


def dot_tn(a, b):
    return lax.dot_general(a, b, (((0,), (0,)), ((), ())), preferred_element_type=F32)


def dft_tables():
    times = PH * np.arange(ML)[None, None, :] + np.arange(PH)[:, None, None]
    odd = 2 * np.arange(ML)[None, :, None] + 1
    angle = 2.0 * np.pi / (4 * L) * ((times * odd) % (4 * L)).astype(np.float64)
    table = np.concatenate([np.cos(angle), -np.sin(angle)], axis=1)
    forward = table.reshape(PH * 2 * ML, ML).astype(jnp.bfloat16)
    backward = np.swapaxes(table, 1, 2).reshape(PH * ML, 2 * ML).astype(jnp.bfloat16)
    return forward, backward


def whole(shape):
    return pl.BlockSpec(shape, lambda *_: (0,) * len(shape), pipeline_mode=pl.Buffered(1))


def params(**kw):
    return pltpu.CompilerParams(vmem_limit_bytes=VMEM_BYTES, **kw)


def cost(flops, moved):
    return pl.CostEstimate(flops=int(flops), bytes_accessed=int(moved), transcendentals=0)


def forward_dft(tab_ref, src, dst_ref):
    for r in range(PH):
        dst_ref[pl.ds(r * 2 * ML, 2 * ML), :] = dot_nn(tab_ref[pl.ds(r * 2 * ML, 2 * ML), :], src(r))


def split_bins(part, rows):
    re = [part(r * 2 * ML + rows) for r in range(PH)]
    im = [part(r * 2 * ML + ML + rows) for r in range(PH)]
    ar, ai, br, bi = re[0] + re[2], im[0] + im[2], re[0] - re[2], im[0] - im[2]
    cr, ci, dr, di = re[1] + re[3], im[1] + im[3], re[1] - re[3], im[1] - im[3]
    return [(ar + cr, ai + ci), (br + di, bi - dr), (ar - cr, ai - ci), (br - di, bi + dr)]


def join_bins(bins, put, rows):
    (r0, i0), (r1, i1), (r2, i2), (r3, i3) = bins
    ar, ai, br, bi = r0 + r2, i0 + i2, r0 - r2, i0 - i2
    cr, ci, dr, di = r1 + r3, i1 + i3, r1 - r3, i1 - i3
    out = [(ar + cr, ai + ci), (br - di, bi + dr), (ar - cr, ai - ci), (br + di, bi - dr)]
    for r in range(PH):
        put(r * 2 * ML + rows, out[r][0])
        put(r * 2 * ML + ML + rows, out[r][1])


def filter_kernel(tab_ref, filt_ref, spec_ref, part_ref):
    forward_dft(tab_ref, lambda r: filt_ref[pl.ds(r * ML, ML), :], part_ref)
    step = 16

    @pl.loop(0, ML // step)
    def _(i):
        rows = pl.multiple_of(i * step, step)
        bins = split_bins(lambda at: part_ref[pl.ds(at, step), :], rows)
        for j in range(PH):
            spec_ref[pl.ds(j * 2 * ML + rows, step), :] = (bins[j][0] * (1.0 / L)).astype(BF16)
            spec_ref[pl.ds(j * 2 * ML + ML + rows, step), :] = (bins[j][1] * (1.0 / L)).astype(BF16)


def filter_spectrum(tab, filters):
    return pl.pallas_call(
        filter_kernel,
        grid=(D // TILE,),
        in_specs=[whole((PH * 2 * ML, ML)), pl.BlockSpec((L, TILE), lambda i: (0, i))],
        out_specs=pl.BlockSpec((2 * L, TILE), lambda i: (0, i)),
        out_shape=jax.ShapeDtypeStruct((2 * L, D), BF16),
        scratch_shapes=[pltpu.VMEM((2 * L, TILE), F32)],
        compiler_params=params(),
        cost_estimate=cost(2 * 2 * L * ML * D, 16 << 20),
        name="filter_spectrum",
    )(tab, filters)


def front_kernel(
    n1_ref, wa_ref, wb_ref, wc_ref, ba_ref, bb_ref, bc_ref, ta_ref, tb_ref, tc_ref, skip_ref,
    tab_ref, itab_ref, spec_ref,
    proj_ref, gate_ref, gated_ref, mixed_ref, branch_ref, sig_ref,
    sa_ref, sb_ref, sc_ref, part_ref, turn_ref,
):
    scr = (sa_ref, sb_ref, sc_ref)
    for ref, w_ref, b_ref in zip(scr, (wa_ref, wb_ref, wc_ref), (ba_ref, bb_ref, bc_ref)):
        for r in range(PH):
            ref[r, pl.ds(0, PAD), :] = jnp.zeros((PAD, TILE), F32)
            ref[r, pl.ds(PAD, ML), :] = dot_nn(n1_ref[pl.ds(r * ML, ML), :], w_ref[...]) + b_ref[...]
    taps = [[t[pl.ds(j, 1), :] for j in range(3)] for t in (ta_ref, tb_ref, tc_ref)]
    step = 32

    @pl.loop(0, ML // step)
    def _(i):
        rows = pl.multiple_of(i * step, step)
        outs = []
        for n in range(3):
            ref = scr[n]
            p = [ref[r, pl.ds(PAD + rows, step), :] for r in range(PH)]
            low = [pltpu.roll(ref[r, pl.ds(rows, step + PAD), :], 1, 0)[PAD:, :] for r in (2, 3)]
            seq = low + p
            w0, w1, w2 = taps[n]
            short = [w0 * seq[r + 2] + w1 * seq[r + 1] + w2 * seq[r] for r in range(PH)]
            for r in range(PH):
                proj_ref[n, pl.ds(r * ML + rows, step), :] = p[r].astype(BF16)
                gate_ref[n, pl.ds(r * ML + rows, step), :] = short[r].astype(BF16)
            outs.append(short)
        for r in range(PH):
            gated_ref[pl.ds(r * ML + rows, step), :] = (outs[1][r] * outs[2][r]).astype(BF16)

    forward_dft(tab_ref, lambda r: gated_ref[pl.ds(r * ML, ML), :], part_ref)
    step2 = 16

    @pl.loop(0, ML // step2)
    def _(i):
        rows = pl.multiple_of(i * step2, step2)
        bins = split_bins(lambda at: part_ref[pl.ds(at, step2), :], rows)
        out = []
        for j in range(PH):
            xr, xi = bins[j]
            at = j * 2 * ML + rows
            sig_ref[pl.ds(at, step2), :] = xr.astype(BF16)
            sig_ref[pl.ds(at + ML, step2), :] = xi.astype(BF16)
            hr = spec_ref[pl.ds(at, step2), :].astype(F32)
            hi = spec_ref[pl.ds(at + ML, step2), :].astype(F32)
            out.append((xr * hr - xi * hi, xr * hi + xi * hr))

        def put(at, value):
            turn_ref[pl.ds(at, step2), :] = value.astype(BF16)

        join_bins(out, put, rows)

    skip = skip_ref[...]
    for r in range(PH):
        part_ref[pl.ds(r * ML, ML), :] = dot_nn(
            itab_ref[pl.ds(r * ML, ML), :], turn_ref[pl.ds(r * 2 * ML, 2 * ML), :]
        )

    @pl.loop(0, ML // step)
    def _(i):
        rows = pl.multiple_of(i * step, step)
        for r in range(PH):
            at = pl.ds(r * ML + rows, step)
            mixed = part_ref[at, :] + skip * gated_ref[at, :].astype(F32)
            mixed_ref[at, :] = mixed.astype(BF16)
            branch_ref[at, :] = (gate_ref[0, at, :].astype(F32) * mixed).astype(BF16)


def front(n1, in_w, in_b, taps, skip, tab, itab, spec):
    nt = D // TILE
    cols = lambda k: pl.BlockSpec((D, TILE), lambda i, k=k: (0, k * nt + i))
    row = lambda k, h: pl.BlockSpec((h, TILE), lambda i, k=k: (0, k * nt + i))
    out = pl.BlockSpec((L, TILE), lambda i: (0, i))
    out3 = pl.BlockSpec((3, L, TILE), lambda i: (0, 0, i))
    return pl.pallas_call(
        front_kernel,
        grid=(nt,),
        in_specs=[whole((L, D))] + [cols(k) for k in range(3)] + [row(k, 1) for k in range(3)]
        + [row(k, 3) for k in range(3)] + [row(0, 1), whole((PH * 2 * ML, ML)), whole((PH * ML, 2 * ML)),
           pl.BlockSpec((2 * L, TILE), lambda i: (0, i))],
        out_specs=[out3, out3, out, out, out, pl.BlockSpec((2 * L, TILE), lambda i: (0, i))],
        out_shape=[
            jax.ShapeDtypeStruct((3, L, D), BF16), jax.ShapeDtypeStruct((3, L, D), BF16),
            jax.ShapeDtypeStruct((L, D), BF16), jax.ShapeDtypeStruct((L, D), BF16),
            jax.ShapeDtypeStruct((L, D), BF16), jax.ShapeDtypeStruct((2 * L, D), BF16),
        ],
        scratch_shapes=[pltpu.VMEM((PH, PAD + ML, TILE), F32)] * 3
        + [pltpu.VMEM((2 * L, TILE), F32), pltpu.VMEM((2 * L, TILE), BF16)],
        compiler_params=params(),
        cost_estimate=cost(2 * L * D * 3 * D + 4 * 2 * L * ML * D, 80 << 20),
        name="front",
    )(n1, in_w, in_w, in_w, in_b, in_b, in_b, taps, taps, taps, skip, tab, itab, spec)


def gelu_parts(h):
    a = jnp.abs(h)
    t = 1.0 / (1.0 + (0.3275911 / math.sqrt(2.0)) * a)
    bell = jnp.exp(-0.5 * h * h)
    poly = ((((0.5 * 1.061405429 * t - 0.5 * 1.453152027) * t + 0.5 * 1.421413741) * t - 0.5 * 0.284496736) * t + 0.5 * 0.254829592) * t
    tail = poly * bell
    phi = jnp.where(h >= 0, 1.0 - tail, tail)
    return h * phi, phi + h * (bell * (1.0 / math.sqrt(2.0 * math.pi)))


def norm_stats(v):
    centre = jnp.mean(v, axis=-1, keepdims=True)
    centred = v - centre
    inv = lax.rsqrt(jnp.mean(centred * centred, axis=-1, keepdims=True) + eps)
    return centred * inv, inv


ROWS = 256
CHUNK = 512


def up_kernel(x_ref, branch_ref, ow_ref, ob_ref, g_ref, s_ref, uw_ref, ub_ref, res_ref, n2_ref, act_ref, slope_ref):
    res = x_ref[...].astype(F32) + dot_nn(branch_ref[...], ow_ref[...]) + ob_ref[...]
    res_ref[...] = res
    hat, _ = norm_stats(res)
    n2_ref[...] = (hat * g_ref[...] + s_ref[...]).astype(BF16)
    n2 = n2_ref[...]
    for c in range(FF // CHUNK):
        at = pl.ds(c * CHUNK, CHUNK)
        h = dot_nn(n2, uw_ref[:, at]) + ub_ref[:, at]
        act, slope = gelu_parts(h)
        act_ref[:, at] = act.astype(BF16)
        slope_ref[:, at] = slope.astype(BF16)


def up_stage(x, branch, ow, ob, g, s, uw, ub):
    rows = lambda n: pl.BlockSpec((ROWS, n), lambda i: (i, 0))
    return pl.pallas_call(
        up_kernel,
        grid=(L // ROWS,),
        in_specs=[rows(D), rows(D), whole((D, D)), whole((1, D)), whole((1, D)), whole((1, D)), whole((D, FF)), whole((1, FF))],
        out_specs=[rows(D), rows(D), rows(FF), rows(FF)],
        out_shape=[
            jax.ShapeDtypeStruct((L, D), F32), jax.ShapeDtypeStruct((L, D), BF16),
            jax.ShapeDtypeStruct((L, FF), BF16), jax.ShapeDtypeStruct((L, FF), BF16),
        ],
        compiler_params=params(),
        cost_estimate=cost(2 * L * D * (D + FF), 60 << 20),
        name="up_stage",
    )(x, branch, ow, ob, g, s, uw, ub)


def interleave(value, mix_ref, out_ref):
    q = ROWS // PH
    for c in range(D // 128):
        lanes = slice(c * 128, (c + 1) * 128)
        for r in range(PH):
            mix_ref[c, pl.ds(r, q, stride=PH), :] = value[r * q:(r + 1) * q, lanes]
        out_ref[:, lanes] = mix_ref[c].astype(BF16)


def down_kernel(act_ref, slope_ref, res_ref, cot_ref, dw_ref, db_ref, uw_ref, g_ref, out_ref, gh_ref, gres_ref, low_ref, sums_ref, ubg_ref, mix_ref):
    i = pl.program_id(0)

    @pl.when(i == 0)
    def _():
        sums_ref[...] = jnp.zeros_like(sums_ref)
        ubg_ref[...] = jnp.zeros_like(ubg_ref)

    res = res_ref[...].reshape(ROWS, D)
    cot = cot_ref[...].reshape(ROWS, D)
    for c in range(FF // CHUNK):
        at = pl.ds(c * CHUNK, CHUNK)
        ga = dot_nt(cot, dw_ref[at, :])
        gh = (ga * slope_ref[:, :, at].reshape(ROWS, CHUNK).astype(F32)).astype(BF16)
        gh_ref[:, :, at] = gh.reshape(PH, ROWS // PH, CHUNK)
        ubg_ref[pl.ds(0, 1), at] += jnp.sum(gh.astype(F32), axis=0, keepdims=True)
    out = res + dot_nn(act_ref[...].reshape(ROWS, FF), dw_ref[...]) + db_ref[...]
    interleave(out, mix_ref, out_ref)
    gn = dot_nt(gh_ref[...].reshape(ROWS, FF), uw_ref[...])
    hat, inv = norm_stats(res)
    e = gn * g_ref[...]
    cot32 = cot.astype(F32)
    gres = cot32 + inv * (e - jnp.mean(e, axis=-1, keepdims=True) - hat * jnp.mean(e * hat, axis=-1, keepdims=True))
    low = gres.astype(BF16)
    gres_ref[...] = gres.reshape(PH, ROWS // PH, D)
    low_ref[...] = low.reshape(PH, ROWS // PH, D)
    sums_ref[pl.ds(0, 1), :] += jnp.sum(gn * hat, axis=0, keepdims=True)
    sums_ref[pl.ds(1, 1), :] += jnp.sum(gn, axis=0, keepdims=True)
    sums_ref[pl.ds(2, 1), :] += jnp.sum(low.astype(F32), axis=0, keepdims=True)
    sums_ref[pl.ds(3, 1), :] += jnp.sum(cot32, axis=0, keepdims=True)


def down_stage(act, slope, res, cot, dw, db, uw, g):
    q = ROWS // PH
    rows = lambda n: pl.BlockSpec((PH, q, n), lambda i: (0, i, 0))
    fold = lambda a: a.reshape(PH, ML, a.shape[-1])
    out, gh, gres, low, sums, ubg = pl.pallas_call(
        down_kernel,
        grid=(L // ROWS,),
        in_specs=[rows(FF), rows(FF), rows(D), rows(D), whole((FF, D)), whole((1, D)), whole((D, FF)), whole((1, D))],
        out_specs=[pl.BlockSpec((ROWS, D), lambda i: (i, 0)), rows(FF), rows(D), rows(D),
                   pl.BlockSpec((8, D), lambda i: (0, 0)), pl.BlockSpec((8, FF), lambda i: (0, 0))],
        out_shape=[
            jax.ShapeDtypeStruct((L, D), BF16), jax.ShapeDtypeStruct((PH, ML, FF), BF16),
            jax.ShapeDtypeStruct((PH, ML, D), F32), jax.ShapeDtypeStruct((PH, ML, D), BF16),
            jax.ShapeDtypeStruct((8, D), F32), jax.ShapeDtypeStruct((8, FF), F32),
        ],
        scratch_shapes=[pltpu.VMEM((D // 128, ROWS, 128), F32)],
        compiler_params=params(),
        cost_estimate=cost(2 * L * D * 3 * FF, 100 << 20),
        name="down_stage",
    )(fold(act), fold(slope), fold(res), fold(cot), dw, db, uw, g)
    return out, gh.reshape(L, FF), gres.reshape(L, D), low.reshape(L, D), sums, ubg


def grad_kernel(a_ref, b_ref, o_ref):
    o_ref[...] = dot_tn(a_ref[...], b_ref[...]).astype(o_ref.dtype)


def weight_grad(a, b, bm, bn, name):
    m, n = a.shape[1], b.shape[1]
    return pl.pallas_call(
        grad_kernel,
        grid=(m // bm, n // bn),
        in_specs=[pl.BlockSpec((L, bm), lambda i, j: (0, i)), pl.BlockSpec((L, bn), lambda i, j: (0, j))],
        out_specs=pl.BlockSpec((bm, bn), lambda i, j: (i, j)),
        out_shape=jax.ShapeDtypeStruct((m, n), BF16),
        compiler_params=params(),
        cost_estimate=cost(2 * L * m * n, 2 * (L * (m + n) + m * n)),
        name=name,
    )(a, b)


def short_back(n, step, scr, taps_ref, proj_ref, gproj_ref, sums_ref):
    ref = scr[n]
    w = [taps_ref[n, pl.ds(j, 1), :] for j in range(3)]

    def second(i, acc, ref=ref, w=w, n=n):
        rows = pl.multiple_of(i * step, step)
        seq = [ref[r, pl.ds(rows, step), :] for r in range(PH)]
        seq += [pltpu.roll(ref[r, pl.ds(rows, step + PAD), :], step + PAD - 1, 0)[:step, :] for r in range(2)]
        acc = list(acc)
        for r in range(PH):
            at = pl.ds(r * ML + rows, step)
            g = (w[0] * seq[r] + w[1] * seq[r + 1] + w[2] * seq[r + 2]).astype(BF16)
            gproj_ref[n, at, :] = g
            p = proj_ref[n, at, :].astype(F32)
            terms = (g.astype(F32), seq[r] * p, seq[r + 1] * p, seq[r + 2] * p)
            for q in range(4):
                for k in range(step // 8):
                    acc[q] = acc[q] + terms[q][k * 8:(k + 1) * 8, :]
        return tuple(acc)

    zero = jnp.zeros((8, TILE), F32)
    acc = lax.fori_loop(0, ML // step, second, (zero,) * 4)
    for q in range(4):
        sums_ref[pl.ds(1 + 4 * n + q, 1), :] = jnp.sum(acc[q], axis=0, keepdims=True)


def back_kernel(
    low_ref, ow_ref, gate_ref, proj_ref, gated_ref, mixed_ref, sig_ref, spec_ref, taps_ref, skip_ref, tab_ref, itab_ref,
    gproj_ref, gfilt_ref, sums_ref,
    gb_ref, gl_ref, part_ref, turn_ref, cross_ref, s1_ref, s2_ref,
):
    scr = (s1_ref, s1_ref, s2_ref)
    gb_ref[...] = dot_nt(low_ref[...], ow_ref[...])
    step = 32
    skip = skip_ref[...]

    def first(i, acc):
        rows = pl.multiple_of(i * step, step)
        for r in range(PH):
            at = pl.ds(r * ML + rows, step)
            gb = gb_ref[at, :]
            gp = gb * gate_ref[0, at, :].astype(F32)
            gl_ref[at, :] = gp.astype(BF16)
            s1_ref[r, pl.ds(rows, step), :] = gb * mixed_ref[at, :].astype(F32)
            gb_ref[at, :] = gp
            prod = gp * gated_ref[at, :].astype(F32)
            for k in range(step // 8):
                acc = acc + prod[k * 8:(k + 1) * 8, :]
        return acc

    acc = lax.fori_loop(0, ML // step, first, jnp.zeros((8, TILE), F32))
    sums_ref[pl.ds(0, 1), :] = jnp.sum(acc, axis=0, keepdims=True)
    for ref in (s1_ref, s2_ref):
        for r in range(2):
            ref[r, pl.ds(ML, PAD), :] = jnp.zeros((PAD, TILE), F32)
    short_back(0, step, scr, taps_ref, proj_ref, gproj_ref, sums_ref)
    forward_dft(tab_ref, lambda r: gl_ref[pl.ds(r * ML, ML), :], part_ref)
    step2 = 16

    @pl.loop(0, ML // step2)
    def _(i):
        rows = pl.multiple_of(i * step2, step2)
        bins = split_bins(lambda at: part_ref[pl.ds(at, step2), :], rows)
        for other_ref, into_ref in ((spec_ref, turn_ref), (sig_ref, cross_ref)):
            out = []
            for j in range(PH):
                gr, gi = bins[j]
                at = j * 2 * ML + rows
                hr = other_ref[pl.ds(at, step2), :].astype(F32)
                hi = other_ref[pl.ds(at + ML, step2), :].astype(F32)
                out.append((hr * gr + hi * gi, hr * gi - hi * gr))

            def put(at, value, into_ref=into_ref):
                into_ref[pl.ds(at, step2), :] = value.astype(BF16)

            join_bins(out, put, rows)

    for r in range(PH):
        rows = pl.ds(r * ML, ML)
        freq = pl.ds(r * 2 * ML, 2 * ML)
        gfilt_ref[rows, :] = (dot_nn(itab_ref[rows, :], cross_ref[freq, :]) * (1.0 / L)).astype(BF16)
        part_ref[rows, :] = dot_nn(itab_ref[rows, :], turn_ref[freq, :])

    @pl.loop(0, ML // step)
    def _(i):
        rows = pl.multiple_of(i * step, step)
        for r in range(PH):
            at = pl.ds(r * ML + rows, step)
            gg = part_ref[at, :] + gb_ref[at, :] * skip
            s1_ref[r, pl.ds(rows, step), :] = gg * gate_ref[2, at, :].astype(F32)
            s2_ref[r, pl.ds(rows, step), :] = gg * gate_ref[1, at, :].astype(F32)

    for n in (1, 2):
        short_back(n, step, scr, taps_ref, proj_ref, gproj_ref, sums_ref)


def back(low, ow, gate, proj, gated, mixed, sig, spec, taps3, skip, tab, itab):
    nt = D // TILE
    tile = lambda h: pl.BlockSpec((h, TILE), lambda i: (0, i))
    tile3 = lambda h: pl.BlockSpec((3, h, TILE), lambda i: (0, 0, i))
    once = lambda h: pl.BlockSpec((h, TILE), lambda i: (0, i), pipeline_mode=pl.Buffered(1))
    return pl.pallas_call(
        back_kernel,
        grid=(nt,),
        in_specs=[whole((L, D)), pl.BlockSpec((TILE, D), lambda i: (i, 0)), tile3(L), tile3(L), once(L), once(L),
                  tile(2 * L), tile(2 * L), tile3(3), tile(1), whole((PH * 2 * ML, ML)), whole((PH * ML, 2 * ML))],
        out_specs=[tile3(L), tile(L), tile(16)],
        out_shape=[jax.ShapeDtypeStruct((3, L, D), BF16), jax.ShapeDtypeStruct((L, D), BF16), jax.ShapeDtypeStruct((16, D), F32)],
        scratch_shapes=[
            pltpu.VMEM((L, TILE), F32), pltpu.VMEM((L, TILE), BF16), pltpu.VMEM((2 * L, TILE), F32),
            pltpu.VMEM((2 * L, TILE), BF16), pltpu.VMEM((2 * L, TILE), BF16),
        ] + [pltpu.VMEM((PH, ML + PAD, TILE), F32)] * 2,
        compiler_params=params(),
        cost_estimate=cost(2 * L * D * D + 6 * 2 * L * ML * D, 80 << 20),
        name="back",
    )(low, ow, gate, proj, gated, mixed, sig, spec, taps3, skip, tab, itab)


def in_grad_kernel(n1_ref, g_ref, o_ref):
    o_ref[...] = dot_tn(n1_ref[...], g_ref[0]).astype(BF16)


def in_weight_grad(n1, gproj):
    bm = 512
    return pl.pallas_call(
        in_grad_kernel,
        grid=(D // bm, 3),
        in_specs=[pl.BlockSpec((L, bm), lambda i, j: (0, i)), pl.BlockSpec((1, L, D), lambda i, j: (j, 0, 0))],
        out_specs=pl.BlockSpec((bm, D), lambda i, j: (i, j)),
        out_shape=jax.ShapeDtypeStruct((D, 3 * D), BF16),
        compiler_params=params(),
        cost_estimate=cost(2 * L * D * 3 * D, 40 << 20),
        name="in_weight_grad",
    )(n1, gproj)


def last_kernel(gp_ref, iw_ref, x_ref, gres_ref, g_ref, out_ref, sums_ref, mix_ref):
    i = pl.program_id(0)

    @pl.when(i == 0)
    def _():
        sums_ref[...] = jnp.zeros_like(sums_ref)

    gn = dot_nt(gp_ref[0].reshape(ROWS, D), iw_ref[:, pl.ds(0, D)])
    gn += dot_nt(gp_ref[1].reshape(ROWS, D), iw_ref[:, pl.ds(D, D)])
    gn += dot_nt(gp_ref[2].reshape(ROWS, D), iw_ref[:, pl.ds(2 * D, D)])
    hat, inv = norm_stats(x_ref[...].reshape(ROWS, D).astype(F32))
    e = gn * g_ref[...]
    out = gres_ref[...].reshape(ROWS, D) + inv * (e - jnp.mean(e, axis=-1, keepdims=True) - hat * jnp.mean(e * hat, axis=-1, keepdims=True))
    interleave(out, mix_ref, out_ref)
    sums_ref[pl.ds(0, 1), :] += jnp.sum(gn * hat, axis=0, keepdims=True)
    sums_ref[pl.ds(1, 1), :] += jnp.sum(gn, axis=0, keepdims=True)


def last_stage(gproj, in_w, x, gres, g):
    q = ROWS // PH
    rows = pl.BlockSpec((PH, q, D), lambda i: (0, i, 0))
    fold = lambda a: a.reshape(PH, ML, D)
    return pl.pallas_call(
        last_kernel,
        grid=(L // ROWS,),
        in_specs=[pl.BlockSpec((3, PH, q, D), lambda i: (0, 0, i, 0)), whole((D, 3 * D)), rows, rows, whole((1, D))],
        out_specs=[pl.BlockSpec((ROWS, D), lambda i: (i, 0)), pl.BlockSpec((8, D), lambda i: (0, 0))],
        out_shape=[jax.ShapeDtypeStruct((L, D), BF16), jax.ShapeDtypeStruct((8, D), F32)],
        scratch_shapes=[pltpu.VMEM((D // 128, ROWS, 128), F32)],
        compiler_params=params(),
        cost_estimate=cost(2 * L * D * 3 * D, 30 << 20),
        name="last_stage",
    )(gproj.reshape(3, PH, ML, D), in_w, fold(x), fold(gres), g)


def positions_table(places):
    places = places.astype(F32)
    harmonics = jnp.arange(1, BANDS + 1).astype(F32)
    angles = 2.0 * math.pi / L * places[:, None] * harmonics[None, :]
    return places, jnp.concatenate([places[:, None] / L, jnp.cos(angles), jnp.sin(angles)], axis=1)


def filter_values(places, network, rates):
    pos_weight, pos_bias, mid_weight, mid_bias, filter_weight = network
    places, features = positions_table(places)
    first_layer = jnp.sin(jnp.dot(features, pos_weight, precision=HIGH_ACCURACY) + pos_bias)
    second_layer = jnp.sin(jnp.dot(first_layer, mid_weight, precision=HIGH_ACCURACY) + mid_bias)
    shaped = jnp.dot(second_layer, filter_weight, precision=HIGH_ACCURACY)
    return shaped * (jnp.exp(-rates[None, :] * places[:, None] / L) + decay_floor)


def by_phase(a):
    return a.reshape(ML, PH, a.shape[-1]).swapaxes(0, 1).reshape(L, a.shape[-1])


VECTORS = (
    ("first_gain", 1), ("first_shift", 1), ("in_bias", 3), ("short", 9), ("skip", 1), ("out_bias", 1),
    ("second_gain", 1), ("second_shift", 1), ("up_bias", 4), ("down_bias", 1),
)


def swap_bit(x, axis, bit):
    size = lax.axis_size(axis)
    return lax.ppermute(x, axis, [(i, i ^ bit) for i in range(size)])


def bits_of(axis, falling):
    size = lax.axis_size(axis)
    out = [1 << b for b in range(size.bit_length() - 1)]
    return out[::-1] if falling else out


def add_low(a, b):
    return (a.astype(F32) + b.astype(F32)).astype(BF16)


def halve(x, axis, falling):
    size = lax.axis_size(axis)
    place = lax.axis_index(axis)
    bits = bits_of(axis, falling)
    left = list(bits)
    for bit in bits:
        n = len(left)
        order = sorted(left, reverse=True)
        at = order.index(bit)
        cube = x.reshape((2,) * n + x.shape[1:])
        mine = (place // bit) % 2
        keep = lax.dynamic_index_in_dim(cube, mine, at, False)
        send = lax.dynamic_index_in_dim(cube, 1 - mine, at, False)
        tail = x.shape[1:]
        x = add_low(keep.reshape((1 << (n - 1),) + tail), swap_bit(send.reshape((1 << (n - 1),) + tail), axis, bit))
        left.remove(bit)
    return x[0]


def double(x, axis, falling):
    place = lax.axis_index(axis)
    x = x[None]
    got = []
    for bit in bits_of(axis, falling)[::-1]:
        other = swap_bit(x, axis, bit)
        mine = (place // bit) % 2
        got.append(bit)
        order = sorted(got, reverse=True)
        at = order.index(bit)
        n = len(got)
        tail = x.shape[1:]
        shape = (2,) * (n - 1) + tail
        low = jnp.where(mine == 0, x, other).reshape(shape)
        high = jnp.where(mine == 0, other, x).reshape(shape)
        x = jnp.stack([low, high], axis=at).reshape((1 << n,) + tail)
    return x


def sum_rows(grad):
    mp = lax.axis_size("mp")
    core = lax.axis_index("core")
    rows, cols = grad.shape
    own = rows // mp
    cube = grad.reshape(mp, 2, own // 2, cols)
    keep = lax.dynamic_index_in_dim(cube, core, 1, False)
    send = lax.dynamic_index_in_dim(cube, 1 - core, 1, False)
    half = add_low(keep, swap_bit(send, "core", 1))
    q = own // 4
    first = halve(half[:, :q], "mp", True)
    second = halve(half[:, q:], "mp", False)
    z = lax.axis_size("z")
    parts = []
    for part in (first, second):
        share = halve(part.reshape(z, q // z, cols), "z", True)
        parts.append(double(share, "z", True).reshape(q, cols))
    mine = jnp.concatenate(parts, axis=0)
    other = swap_bit(mine, "core", 1)
    low = jnp.where(core == 0, mine, other)
    high = jnp.where(core == 0, other, mine)
    return jnp.concatenate([low, high], axis=0).astype(F32)


def sum_all(flat):
    total = flat.shape[0]
    mp, z = lax.axis_size("mp"), lax.axis_size("z")
    x = flat.reshape(2, total // 2)
    core = lax.axis_index("core")
    x = lax.dynamic_index_in_dim(x, core, 0, False) + swap_bit(lax.dynamic_index_in_dim(x, 1 - core, 0, False), "core", 1)
    for axis in ("mp", "z"):
        for bit in bits_of(axis, False):
            x = x + swap_bit(x, axis, bit)
    other = swap_bit(x, "core", 1)
    return jnp.concatenate([jnp.where(core == 0, x, other), jnp.where(core == 0, other, x)], axis=0)


def gather_rows(shard):
    rows = shard.shape[0]
    half = lax.dynamic_slice_in_dim(shard, lax.axis_index("core") * (rows // 2), rows // 2, 0)
    return lax.all_gather(half, ("mp", "core"), axis=0, tiled=True)


def shards(
    inputs, first_gain, first_shift, in_weight, in_bias, short_weight, skip_gain, pos_weight, pos_bias,
    mid_weight, mid_bias, filter_weight, decay_rates, out_weight, out_bias, second_gain, second_shift,
    up_weight, up_bias, down_weight, down_bias, cotangent,
):
    mp = lax.axis_size("mp")
    own = D // mp
    local = (first_gain, first_shift, in_bias, short_weight, skip_gain, out_bias, second_gain, second_shift, up_bias, down_bias)
    packed = jnp.concatenate([v.reshape(-1) for v in local]).reshape(1, -1)
    spread = lax.all_gather(packed, "mp", axis=0, tiled=True).astype(F32)
    full = {}
    at = 0
    for name, count in VECTORS:
        part = spread[:, at:at + count * own]
        at += count * own
        if name == "short":
            part = part.reshape(mp, 3, 3 * own).swapaxes(0, 1)
            full[name] = part.reshape(3, 3 * D)
        else:
            full[name] = part.reshape(1, count * D)
    in_matrix = gather_rows(in_weight)
    out_matrix = gather_rows(out_weight)
    up_matrix = gather_rows(up_weight)
    down_matrix = gather_rows(down_weight)

    tab, itab = (jnp.asarray(t) for t in dft_tables())
    x = by_phase(inputs)
    cot = by_phase(cotangent)
    places = (jnp.arange(PH)[:, None] + PH * jnp.arange(ML)[None, :]).reshape(L)
    network = (pos_weight, pos_bias, mid_weight, mid_bias, filter_weight)
    filters, filter_back = jax.vjp(lambda weights: filter_values(places, weights, decay_rates), network)
    spec = filter_spectrum(tab, filters.astype(BF16))
    hat_one, _ = norm_stats(x.astype(F32))
    n1 = (hat_one * full["first_gain"] + full["first_shift"]).astype(BF16)
    proj, gate, gated, mixed, branch, sig = front(n1, in_matrix, full["in_bias"], full["short"], full["skip"], tab, itab, spec)
    res, n2, act, slope = up_stage(x, branch, out_matrix, full["out_bias"], full["second_gain"], full["second_shift"], up_matrix, full["up_bias"])
    block_out, gh, gres, low, sums_two, up_bias_sum = down_stage(act, slope, res, cot, down_matrix, full["down_bias"], up_matrix, full["second_gain"])
    down_sum = sum_rows(weight_grad(act, cot, 1024, 1024, "down_weight_grad"))
    up_sum = sum_rows(weight_grad(n2, gh, 1024, 1024, "up_weight_grad"))
    taps3 = full["short"].reshape(3, 3, D).swapaxes(0, 1)
    gproj, gfilt, sums_mid = back(low, out_matrix, gate, proj, gated, mixed, sig, spec, taps3, full["skip"], tab, itab)
    out_sum = sum_rows(weight_grad(branch, low, 512, 1024, "out_weight_grad"))
    in_sum = sum_rows(in_weight_grad(n1, gproj))
    net = filter_back(gfilt.astype(F32))[0]
    input_grad, sums_one = last_stage(gproj, in_matrix, x, gres, full["first_gain"])
    mids = sums_mid[1:13].reshape(3, 4, D)
    vectors = {
        "first_gain": sums_one[0], "first_shift": sums_one[1], "in_bias": mids[:, 0].reshape(3 * D),
        "short": mids[:, 1:].swapaxes(0, 1).reshape(3, 3 * D), "skip": sums_mid[0], "out_bias": sums_two[2],
        "second_gain": sums_two[0], "second_shift": sums_two[1], "up_bias": up_bias_sum[0], "down_bias": sums_two[3],
    }
    flats = [vectors[name].reshape(-1) for name, _ in VECTORS] + [n.reshape(-1) for n in net]
    sizes = [f.shape[0] for f in flats]
    total = sum(sizes)
    pad = -total % 4096
    summed = sum_all(jnp.concatenate(flats + [jnp.zeros((pad,), F32)]))
    pieces = []
    at = 0
    for size in sizes:
        pieces.append(summed[at:at + size])
        at += size
    me = lax.axis_index("mp")
    mine = {}
    for (name, count), piece in zip(VECTORS, pieces):
        if name == "short":
            mine[name] = lax.dynamic_slice_in_dim(piece.reshape(3, 3 * D), me * 3 * own, 3 * own, 1)
        else:
            mine[name] = lax.dynamic_slice_in_dim(piece, me * count * own, count * own, 0)
    net_sum = [p.reshape(n.shape) for p, n in zip(pieces[len(VECTORS):], net)]
    return (
        block_out, input_grad, mine["first_gain"], mine["first_shift"], in_sum, mine["in_bias"], mine["short"], mine["skip"],
        *net_sum, out_sum, mine["out_bias"], mine["second_gain"], mine["second_shift"], up_sum, mine["up_bias"],
        down_sum, mine["down_bias"],
    )


def solution(mesh):
    dp, mp = mesh.devices.shape
    split = jax.sharding.Mesh(mesh.devices.reshape(dp // 2, 2, mp), ("z", "core", "mp"))
    tokens = P(("z", "core", "mp"), None)
    row, vec, rep = P("mp", None), P("mp"), P()
    return jax.shard_map(
        shards,
        mesh=split,
        in_specs=(
            tokens, vec, vec, row, vec, P(None, "mp"), vec, rep, rep, rep, rep, rep, rep, row, vec, vec, vec, row, vec, row,
            vec, tokens,
        ),
        out_specs=(
            tokens, tokens, vec, vec, row, vec, P(None, "mp"), vec, rep, rep, rep, rep, rep, row, vec, vec, vec, row, vec,
            row, vec,
        ),
        check_vma=False,
    )
```

```python
import functools
import math

import jax
import jax.numpy as jnp
import numpy as np
from jax import lax
from jax.experimental import pallas as pl
from jax.experimental.pallas import tpu as pltpu
from jax.sharding import PartitionSpec as P

D = 1024
FF = 4096
BANDS = 16
L = 2048
PH = 4
ML = L // PH
TILE = 256
PAD = 8

HIGH_ACCURACY = lax.Precision.HIGHEST
eps = 1e-05
decay_floor = 0.05
F32 = jnp.float32
BF16 = jnp.bfloat16
VMEM_BYTES = 62 << 20


def dot_nn(a, b):
    return lax.dot_general(a, b, (((1,), (0,)), ((), ())), preferred_element_type=F32)


def dot_nt(a, b):
    return lax.dot_general(a, b, (((1,), (1,)), ((), ())), preferred_element_type=F32)


def dot_tn(a, b):
    return lax.dot_general(a, b, (((0,), (0,)), ((), ())), preferred_element_type=F32)


def dft_tables():
    times = PH * np.arange(ML)[None, None, :] + np.arange(PH)[:, None, None]
    odd = 2 * np.arange(ML)[None, :, None] + 1
    angle = 2.0 * np.pi / (4 * L) * ((times * odd) % (4 * L)).astype(np.float64)
    table = np.concatenate([np.cos(angle), -np.sin(angle)], axis=1)
    forward = table.reshape(PH * 2 * ML, ML).astype(jnp.bfloat16)
    backward = np.swapaxes(table, 1, 2).reshape(PH * ML, 2 * ML).astype(jnp.bfloat16)
    return forward, backward


def whole(shape):
    return pl.BlockSpec(shape, lambda *_: (0,) * len(shape), pipeline_mode=pl.Buffered(1))


def params(**kw):
    return pltpu.CompilerParams(vmem_limit_bytes=VMEM_BYTES, **kw)


def cost(flops, moved):
    return pl.CostEstimate(flops=int(flops), bytes_accessed=int(moved), transcendentals=0)


def forward_dft(tab_ref, src, dst_ref):
    for r in range(PH):
        dst_ref[pl.ds(r * 2 * ML, 2 * ML), :] = dot_nn(tab_ref[pl.ds(r * 2 * ML, 2 * ML), :], src(r)).astype(BF16)


def split_bins(part, rows):
    re = [part(r * 2 * ML + rows) for r in range(PH)]
    im = [part(r * 2 * ML + ML + rows) for r in range(PH)]
    ar, ai, br, bi = re[0] + re[2], im[0] + im[2], re[0] - re[2], im[0] - im[2]
    cr, ci, dr, di = re[1] + re[3], im[1] + im[3], re[1] - re[3], im[1] - im[3]
    return [(ar + cr, ai + ci), (br + di, bi - dr), (ar - cr, ai - ci), (br - di, bi + dr)]


def join_bins(bins, put, rows):
    (r0, i0), (r1, i1), (r2, i2), (r3, i3) = bins
    ar, ai, br, bi = r0 + r2, i0 + i2, r0 - r2, i0 - i2
    cr, ci, dr, di = r1 + r3, i1 + i3, r1 - r3, i1 - i3
    out = [(ar + cr, ai + ci), (br - di, bi + dr), (ar - cr, ai - ci), (br + di, bi - dr)]
    for r in range(PH):
        put(r * 2 * ML + rows, out[r][0])
        put(r * 2 * ML + ML + rows, out[r][1])


def filter_kernel(tab_ref, filt_ref, spec_ref, part_ref):
    forward_dft(tab_ref, lambda r: filt_ref[pl.ds(r * ML, ML), :], part_ref)
    step = 16

    @pl.loop(0, ML // step)
    def _(i):
        rows = pl.multiple_of(i * step, step)
        bins = split_bins(lambda at: part_ref[pl.ds(at, step), :], rows)
        for j in range(PH):
            spec_ref[pl.ds(j * 2 * ML + rows, step), :] = bins[j][0] * jnp.bfloat16(1.0 / L)
            spec_ref[pl.ds(j * 2 * ML + ML + rows, step), :] = bins[j][1] * jnp.bfloat16(1.0 / L)


def filter_spectrum(tab, filters):
    return pl.pallas_call(
        filter_kernel,
        grid=(D // TILE,),
        in_specs=[whole((PH * 2 * ML, ML)), pl.BlockSpec((L, TILE), lambda i: (0, i))],
        out_specs=pl.BlockSpec((2 * L, TILE), lambda i: (0, i)),
        out_shape=jax.ShapeDtypeStruct((2 * L, D), BF16),
        scratch_shapes=[pltpu.VMEM((2 * L, TILE), BF16)],
        compiler_params=params(),
        cost_estimate=cost(2 * 2 * L * ML * D, 16 << 20),
        name="filter_spectrum",
    )(tab, filters)


def front_kernel(
    n1_ref, wa_ref, wb_ref, wc_ref, ba_ref, bb_ref, bc_ref, ta_ref, tb_ref, tc_ref, skip_ref,
    tab_ref, itab_ref, spec_ref,
    proj_ref, gate_ref, gated_ref, mixed_ref, branch_ref, sig_ref,
    sa_ref, sb_ref, sc_ref, part_ref, turn_ref, long_ref,
):
    scr = (sa_ref, sb_ref, sc_ref)
    for ref, w_ref, b_ref in zip(scr, (wa_ref, wb_ref, wc_ref), (ba_ref, bb_ref, bc_ref)):
        for r in range(PH):
            ref[r, pl.ds(0, PAD), :] = jnp.zeros((PAD, TILE), F32)
            ref[r, pl.ds(PAD, ML), :] = dot_nn(n1_ref[pl.ds(r * ML, ML), :], w_ref[...]) + b_ref[...]
    taps = [[t[pl.ds(j, 1), :] for j in range(3)] for t in (ta_ref, tb_ref, tc_ref)]
    step = 32

    @pl.loop(0, ML // step)
    def _(i):
        rows = pl.multiple_of(i * step, step)
        outs = []
        for n in range(3):
            ref = scr[n]
            p = [ref[r, pl.ds(PAD + rows, step), :] for r in range(PH)]
            low = [pltpu.roll(ref[r, pl.ds(rows, step + PAD), :], 1, 0)[PAD:, :] for r in (2, 3)]
            seq = low + p
            w0, w1, w2 = taps[n]
            short = [w0 * seq[r + 2] + w1 * seq[r + 1] + w2 * seq[r] for r in range(PH)]
            for r in range(PH):
                proj_ref[n, pl.ds(r * ML + rows, step), :] = p[r].astype(BF16)
                gate_ref[n, pl.ds(r * ML + rows, step), :] = short[r].astype(BF16)
            outs.append(short)
        for r in range(PH):
            gated_ref[pl.ds(r * ML + rows, step), :] = (outs[1][r] * outs[2][r]).astype(BF16)

    forward_dft(tab_ref, lambda r: gated_ref[pl.ds(r * ML, ML), :], part_ref)
    step2 = 32

    @pl.loop(0, ML // step2)
    def _(i):
        rows = pl.multiple_of(i * step2, step2)
        bins = split_bins(lambda at: part_ref[pl.ds(at, step2), :], rows)
        out = []
        for j in range(PH):
            xr, xi = bins[j]
            at = j * 2 * ML + rows
            sig_ref[pl.ds(at, step2), :] = xr
            sig_ref[pl.ds(at + ML, step2), :] = xi
            hr = spec_ref[pl.ds(at, step2), :]
            hi = spec_ref[pl.ds(at + ML, step2), :]
            out.append((xr * hr - xi * hi, xr * hi + xi * hr))

        def put(at, value):
            turn_ref[pl.ds(at, step2), :] = value

        join_bins(out, put, rows)

    skip = skip_ref[...]
    for r in range(PH):
        long_ref[pl.ds(r * ML, ML), :] = dot_nn(
            itab_ref[pl.ds(r * ML, ML), :], turn_ref[pl.ds(r * 2 * ML, 2 * ML), :]
        )

    @pl.loop(0, ML // step)
    def _(i):
        rows = pl.multiple_of(i * step, step)
        for r in range(PH):
            at = pl.ds(r * ML + rows, step)
            mixed = long_ref[at, :] + skip * gated_ref[at, :].astype(F32)
            mixed_ref[at, :] = mixed.astype(BF16)
            branch_ref[at, :] = (gate_ref[0, at, :].astype(F32) * mixed).astype(BF16)


def front(n1, in_w, in_b, taps, skip, tab, itab, spec):
    nt = D // TILE
    cols = lambda k: pl.BlockSpec((D, TILE), lambda i, k=k: (0, k * nt + i))
    row = lambda k, h: pl.BlockSpec((h, TILE), lambda i, k=k: (0, k * nt + i))
    out = pl.BlockSpec((L, TILE), lambda i: (0, i))
    out3 = pl.BlockSpec((3, L, TILE), lambda i: (0, 0, i))
    return pl.pallas_call(
        front_kernel,
        grid=(nt,),
        in_specs=[whole((L, D))] + [cols(k) for k in range(3)] + [row(k, 1) for k in range(3)]
        + [row(k, 3) for k in range(3)] + [row(0, 1), whole((PH * 2 * ML, ML)), whole((PH * ML, 2 * ML)),
           pl.BlockSpec((2 * L, TILE), lambda i: (0, i))],
        out_specs=[out3, out3, out, out, out, pl.BlockSpec((2 * L, TILE), lambda i: (0, i))],
        out_shape=[
            jax.ShapeDtypeStruct((3, L, D), BF16), jax.ShapeDtypeStruct((3, L, D), BF16),
            jax.ShapeDtypeStruct((L, D), BF16), jax.ShapeDtypeStruct((L, D), BF16),
            jax.ShapeDtypeStruct((L, D), BF16), jax.ShapeDtypeStruct((2 * L, D), BF16),
        ],
        scratch_shapes=[pltpu.VMEM((PH, PAD + ML, TILE), F32)] * 3
        + [pltpu.VMEM((2 * L, TILE), BF16), pltpu.VMEM((2 * L, TILE), BF16), pltpu.VMEM((L, TILE), F32)],
        compiler_params=params(),
        cost_estimate=cost(2 * L * D * 3 * D + 4 * 2 * L * ML * D, 80 << 20),
        name="front",
    )(n1, in_w, in_w, in_w, in_b, in_b, in_b, taps, taps, taps, skip, tab, itab, spec)


def gelu_parts(h):
    c = lambda v: jnp.bfloat16(v)
    h = h.astype(BF16)
    t = c(1.0) / (c(1.0) + c(0.3275911 / math.sqrt(2.0)) * jnp.abs(h))
    bell = jnp.exp(c(-0.5) * h * h)
    poly = c(0.5 * 1.061405429) * t - c(0.5 * 1.453152027)
    for k in (0.5 * 1.421413741, -0.5 * 0.284496736, 0.5 * 0.254829592):
        poly = poly * t + c(k)
    tail = poly * t * bell
    phi = jnp.where(h >= 0, c(1.0) - tail, tail)
    return h * phi, phi + h * (bell * c(1.0 / math.sqrt(2.0 * math.pi)))


def norm_stats(v):
    centre = jnp.mean(v, axis=-1, keepdims=True)
    centred = v - centre
    inv = lax.rsqrt(jnp.mean(centred * centred, axis=-1, keepdims=True) + eps)
    return centred * inv, inv


ROWS = 256
CHUNK = 512


def up_kernel(x_ref, branch_ref, ow_ref, ob_ref, g_ref, s_ref, uw_ref, ub_ref, res_ref, n2_ref, act_ref, slope_ref):
    res = x_ref[...].astype(F32) + dot_nn(branch_ref[...], ow_ref[...]) + ob_ref[...]
    res_ref[...] = res
    hat, _ = norm_stats(res)
    n2_ref[...] = (hat * g_ref[...] + s_ref[...]).astype(BF16)
    n2 = n2_ref[...]
    for c in range(FF // CHUNK):
        at = pl.ds(c * CHUNK, CHUNK)
        h = dot_nn(n2, uw_ref[:, at]) + ub_ref[:, at]
        act, slope = gelu_parts(h)
        act_ref[:, at] = act
        slope_ref[:, at] = slope


def up_part():
    return pl.BlockSpec((D, FF), lambda *_: (0, 0), pipeline_mode=pl.Buffered(1))


def out_part():
    return pl.BlockSpec((D, D), lambda *_: (0, FF // D), pipeline_mode=pl.Buffered(1))


def up_stage(x, branch, upout, ob, g, s, ub):
    rows = lambda n: pl.BlockSpec((ROWS, n), lambda i: (i, 0))
    return pl.pallas_call(
        up_kernel,
        grid=(L // ROWS,),
        in_specs=[rows(D), rows(D), out_part(), whole((1, D)), whole((1, D)), whole((1, D)), up_part(), whole((1, FF))],
        out_specs=[rows(D), rows(D), rows(FF), rows(FF)],
        out_shape=[
            jax.ShapeDtypeStruct((L, D), F32), jax.ShapeDtypeStruct((L, D), BF16),
            jax.ShapeDtypeStruct((L, FF), BF16), jax.ShapeDtypeStruct((L, FF), BF16),
        ],
        compiler_params=params(),
        cost_estimate=cost(2 * L * D * (D + FF), 60 << 20),
        name="up_stage",
    )(x, branch, upout, ob, g, s, upout, ub)


def interleave(value, mix_ref, out_ref):
    q = ROWS // PH
    for c in range(D // 128):
        lanes = slice(c * 128, (c + 1) * 128)
        for r in range(PH):
            mix_ref[c, pl.ds(r, q, stride=PH), :] = value[r * q:(r + 1) * q, lanes]
        out_ref[:, lanes] = mix_ref[c].astype(BF16)


def down_kernel(act_ref, slope_ref, res_ref, cot_ref, dw_ref, db_ref, uw_ref, g_ref, out_ref, gh_ref, gres_ref, low_ref, sums_ref, ubg_ref, mix_ref):
    i = pl.program_id(0)

    @pl.when(i == 0)
    def _():
        sums_ref[...] = jnp.zeros_like(sums_ref)
        ubg_ref[...] = jnp.zeros_like(ubg_ref)

    res = res_ref[...].reshape(ROWS, D)
    cot = cot_ref[...].reshape(ROWS, D)
    for c in range(FF // CHUNK):
        at = pl.ds(c * CHUNK, CHUNK)
        ga = dot_nt(cot, dw_ref[at, :])
        gh = (ga * slope_ref[:, :, at].reshape(ROWS, CHUNK).astype(F32)).astype(BF16)
        gh_ref[:, :, at] = gh.reshape(PH, ROWS // PH, CHUNK)
        ubg_ref[pl.ds(0, 1), at] += jnp.sum(gh.astype(F32), axis=0, keepdims=True)
    out = res + dot_nn(act_ref[...].reshape(ROWS, FF), dw_ref[...]) + db_ref[...]
    interleave(out, mix_ref, out_ref)
    gn = dot_nt(gh_ref[...].reshape(ROWS, FF), uw_ref[...])
    hat, inv = norm_stats(res)
    e = gn * g_ref[...]
    cot32 = cot.astype(F32)
    gres = cot32 + inv * (e - jnp.mean(e, axis=-1, keepdims=True) - hat * jnp.mean(e * hat, axis=-1, keepdims=True))
    low = gres.astype(BF16)
    gres_ref[...] = gres.reshape(PH, ROWS // PH, D)
    low_ref[...] = low.reshape(PH, ROWS // PH, D)
    sums_ref[pl.ds(0, 1), :] += jnp.sum(gn * hat, axis=0, keepdims=True)
    sums_ref[pl.ds(1, 1), :] += jnp.sum(gn, axis=0, keepdims=True)
    sums_ref[pl.ds(2, 1), :] += jnp.sum(low.astype(F32), axis=0, keepdims=True)
    sums_ref[pl.ds(3, 1), :] += jnp.sum(cot32, axis=0, keepdims=True)


def down_stage(act, slope, res, cot, dw, db, uw, g):
    q = ROWS // PH
    rows = lambda n: pl.BlockSpec((PH, q, n), lambda i: (0, i, 0))
    fold = lambda a: a.reshape(PH, ML, a.shape[-1])
    out, gh, gres, low, sums, ubg = pl.pallas_call(
        down_kernel,
        grid=(L // ROWS,),
        in_specs=[rows(FF), rows(FF), rows(D), rows(D), whole((FF, D)), whole((1, D)), up_part(), whole((1, D))],
        out_specs=[pl.BlockSpec((ROWS, D), lambda i: (i, 0)), rows(FF), rows(D), rows(D),
                   pl.BlockSpec((8, D), lambda i: (0, 0)), pl.BlockSpec((8, FF), lambda i: (0, 0))],
        out_shape=[
            jax.ShapeDtypeStruct((L, D), BF16), jax.ShapeDtypeStruct((PH, ML, FF), BF16),
            jax.ShapeDtypeStruct((PH, ML, D), F32), jax.ShapeDtypeStruct((PH, ML, D), BF16),
            jax.ShapeDtypeStruct((8, D), F32), jax.ShapeDtypeStruct((8, FF), F32),
        ],
        scratch_shapes=[pltpu.VMEM((D // 128, ROWS, 128), F32)],
        compiler_params=params(),
        cost_estimate=cost(2 * L * D * 3 * FF, 100 << 20),
        name="down_stage",
    )(fold(act), fold(slope), fold(res), fold(cot), dw, db, uw, g)
    return out, gh.reshape(L, FF), gres.reshape(L, D), low.reshape(L, D), sums, ubg


def grad_kernel(a_ref, b_ref, o_ref):
    o_ref[...] = dot_tn(a_ref[...], b_ref[...]).astype(o_ref.dtype)


def weight_grad(a, b, bm, bn, name):
    m, n = a.shape[1], b.shape[1]
    return pl.pallas_call(
        grad_kernel,
        grid=(m // bm, n // bn),
        in_specs=[pl.BlockSpec((L, bm), lambda i, j: (0, i)), pl.BlockSpec((L, bn), lambda i, j: (0, j))],
        out_specs=pl.BlockSpec((bm, bn), lambda i, j: (i, j)),
        out_shape=jax.ShapeDtypeStruct((m, n), BF16),
        compiler_params=params(),
        cost_estimate=cost(2 * L * m * n, 2 * (L * (m + n) + m * n)),
        name=name,
    )(a, b)


def short_back(n, step, scr, taps_ref, proj_ref, gproj_ref, sums_ref):
    ref = scr[n]
    w = [taps_ref[n, pl.ds(j, 1), :] for j in range(3)]

    def second(i, acc, ref=ref, w=w, n=n):
        rows = pl.multiple_of(i * step, step)
        seq = [ref[r, pl.ds(rows, step), :] for r in range(PH)]
        seq += [pltpu.roll(ref[r, pl.ds(rows, step + PAD), :], step + PAD - 1, 0)[:step, :] for r in range(2)]
        acc = list(acc)
        for r in range(PH):
            at = pl.ds(r * ML + rows, step)
            g = (w[0] * seq[r] + w[1] * seq[r + 1] + w[2] * seq[r + 2]).astype(BF16)
            gproj_ref[n, at, :] = g
            p = proj_ref[n, at, :].astype(F32)
            terms = (g.astype(F32), seq[r] * p, seq[r + 1] * p, seq[r + 2] * p)
            for q in range(4):
                for k in range(step // 8):
                    acc[q] = acc[q] + terms[q][k * 8:(k + 1) * 8, :]
        return tuple(acc)

    zero = jnp.zeros((8, TILE), F32)
    acc = lax.fori_loop(0, ML // step, second, (zero,) * 4)
    for q in range(4):
        sums_ref[pl.ds(1 + 4 * n + q, 1), :] = jnp.sum(acc[q], axis=0, keepdims=True)


def back_kernel(
    low_ref, ow_ref, gate_ref, proj_ref, gated_ref, mixed_ref, sig_ref, spec_ref, taps_ref, skip_ref, tab_ref, itab_ref,
    gproj_ref, gfilt_ref, sums_ref,
    gb_ref, gl_ref, part_ref, turn_ref, cross_ref, long_ref, s1_ref, s2_ref,
):
    scr = (s1_ref, s1_ref, s2_ref)
    gb_ref[...] = dot_nt(low_ref[...], ow_ref[...])
    step = 32
    skip = skip_ref[...]

    def first(i, acc):
        rows = pl.multiple_of(i * step, step)
        for r in range(PH):
            at = pl.ds(r * ML + rows, step)
            gb = gb_ref[at, :]
            gp = gb * gate_ref[0, at, :].astype(F32)
            gl_ref[at, :] = gp.astype(BF16)
            s1_ref[r, pl.ds(rows, step), :] = gb * mixed_ref[at, :].astype(F32)
            gb_ref[at, :] = gp
            prod = gp * gated_ref[at, :].astype(F32)
            for k in range(step // 8):
                acc = acc + prod[k * 8:(k + 1) * 8, :]
        return acc

    acc = lax.fori_loop(0, ML // step, first, jnp.zeros((8, TILE), F32))
    sums_ref[pl.ds(0, 1), :] = jnp.sum(acc, axis=0, keepdims=True)
    for ref in (s1_ref, s2_ref):
        for r in range(2):
            ref[r, pl.ds(ML, PAD), :] = jnp.zeros((PAD, TILE), F32)
    short_back(0, step, scr, taps_ref, proj_ref, gproj_ref, sums_ref)
    forward_dft(tab_ref, lambda r: gl_ref[pl.ds(r * ML, ML), :], part_ref)
    step2 = 32

    @pl.loop(0, ML // step2)
    def _(i):
        rows = pl.multiple_of(i * step2, step2)
        bins = split_bins(lambda at: part_ref[pl.ds(at, step2), :], rows)
        for other_ref, into_ref in ((spec_ref, turn_ref), (sig_ref, cross_ref)):
            out = []
            for j in range(PH):
                gr, gi = bins[j]
                at = j * 2 * ML + rows
                hr = other_ref[pl.ds(at, step2), :]
                hi = other_ref[pl.ds(at + ML, step2), :]
                out.append((hr * gr + hi * gi, hr * gi - hi * gr))

            def put(at, value, into_ref=into_ref):
                into_ref[pl.ds(at, step2), :] = value

            join_bins(out, put, rows)

    for r in range(PH):
        rows = pl.ds(r * ML, ML)
        freq = pl.ds(r * 2 * ML, 2 * ML)
        gfilt_ref[rows, :] = (dot_nn(itab_ref[rows, :], cross_ref[freq, :]) * (1.0 / L)).astype(BF16)
        long_ref[rows, :] = dot_nn(itab_ref[rows, :], turn_ref[freq, :])

    @pl.loop(0, ML // step)
    def _(i):
        rows = pl.multiple_of(i * step, step)
        for r in range(PH):
            at = pl.ds(r * ML + rows, step)
            gg = long_ref[at, :] + gb_ref[at, :] * skip
            s1_ref[r, pl.ds(rows, step), :] = gg * gate_ref[2, at, :].astype(F32)
            s2_ref[r, pl.ds(rows, step), :] = gg * gate_ref[1, at, :].astype(F32)

    for n in (1, 2):
        short_back(n, step, scr, taps_ref, proj_ref, gproj_ref, sums_ref)


def back(first, nt, low, upout, gate, proj, gated, mixed, sig, spec, taps3, skip, tab, itab):
    width = nt * TILE
    tile = lambda h: pl.BlockSpec((h, TILE), lambda i: (0, first + i))
    tile3 = lambda h: pl.BlockSpec((3, h, TILE), lambda i: (0, 0, first + i))
    once = lambda h: pl.BlockSpec((h, TILE), lambda i: (0, first + i), pipeline_mode=pl.Buffered(1))
    out = lambda h: pl.BlockSpec((h, TILE), lambda i: (0, i))
    return pl.pallas_call(
        back_kernel,
        grid=(nt,),
        in_specs=[whole((L, D)), pl.BlockSpec((TILE, D), lambda i: (first + i, FF // D)), tile3(L), tile3(L), once(L), once(L),
                  tile(2 * L), tile(2 * L), tile3(3), tile(1), whole((PH * 2 * ML, ML)), whole((PH * ML, 2 * ML))],
        out_specs=[pl.BlockSpec((3, L, TILE), lambda i: (0, 0, i)), out(L), out(16)],
        out_shape=[
            jax.ShapeDtypeStruct((3, L, width), BF16), jax.ShapeDtypeStruct((L, width), BF16), jax.ShapeDtypeStruct((16, width), F32),
        ],
        scratch_shapes=[
            pltpu.VMEM((L, TILE), F32), pltpu.VMEM((L, TILE), BF16), pltpu.VMEM((2 * L, TILE), BF16),
            pltpu.VMEM((2 * L, TILE), BF16), pltpu.VMEM((2 * L, TILE), BF16), pltpu.VMEM((L, TILE), F32),
        ] + [pltpu.VMEM((PH, ML + PAD, TILE), F32)] * 2,
        compiler_params=params(),
        cost_estimate=cost(2 * L * D * width + 12 * L * ML * width, (80 << 20) * nt // 4),
        name=f"back_{first}",
    )(low, upout, gate, proj, gated, mixed, sig, spec, taps3, skip, tab, itab)


def in_grad_kernel(core_ref, n1_ref, g_ref, keep_ref, send_ref):
    core = core_ref[0]
    blocks, half, width = keep_ref.shape
    value = dot_tn(n1_ref[...], g_ref[0]).astype(BF16).reshape(blocks, 2, half, width)
    keep_ref[...] = jnp.where(core == 0, value[:, 0], value[:, 1])
    send_ref[...] = jnp.where(core == 0, value[:, 1], value[:, 0])


def in_weight_grad(n1, gproj, core, owners):
    bm = 512
    half = D // (2 * owners)
    out = pl.BlockSpec((bm // (2 * half), half, D), lambda i, j, c: (i, 0, j))
    shape = jax.ShapeDtypeStruct((owners, half, 3 * D), BF16)
    return pl.pallas_call(
        in_grad_kernel,
        grid_spec=pltpu.PrefetchScalarGridSpec(
            num_scalar_prefetch=1,
            grid=(D // bm, 3),
            in_specs=[pl.BlockSpec((L, bm), lambda i, j, c: (0, i)), pl.BlockSpec((1, L, D), lambda i, j, c: (j, 0, 0))],
            out_specs=[out, out],
        ),
        out_shape=[shape, shape],
        compiler_params=params(),
        cost_estimate=cost(2 * L * D * 3 * D, 40 << 20),
        name="in_weight_grad",
    )(core, n1, gproj)


def up_out_kernel(n2_ref, br_ref, gh_ref, low_ref, o_ref):
    j = pl.program_id(0)

    @pl.when(j < FF // D)
    def _():
        o_ref[...] = dot_tn(n2_ref[...], gh_ref[...]).astype(BF16)

    @pl.when(j == FF // D)
    def _():
        o_ref[...] = dot_tn(br_ref[...], low_ref[...]).astype(BF16)


def up_out_grad(n2, branch, gh, low):
    nj = FF // D
    return pl.pallas_call(
        up_out_kernel,
        grid=(nj + 1,),
        in_specs=[whole((L, D)), whole((L, D)), pl.BlockSpec((L, D), lambda j: (0, jnp.minimum(j, nj - 1))), whole((L, D))],
        out_specs=pl.BlockSpec((D, D), lambda j: (0, j)),
        out_shape=jax.ShapeDtypeStruct((D, FF + D), BF16),
        compiler_params=params(),
        cost_estimate=cost(2 * L * D * (FF + D), 40 << 20),
        name="up_out_grad",
    )(n2, branch, gh, low)


def last_kernel(gp_ref, iw_ref, x_ref, gres_ref, g_ref, out_ref, sums_ref, mix_ref):
    i = pl.program_id(0)

    @pl.when(i == 0)
    def _():
        sums_ref[...] = jnp.zeros_like(sums_ref)

    both = jnp.concatenate([gp_ref[n].reshape(ROWS, D) for n in range(3)], axis=1)
    gn = dot_nt(both, iw_ref[...])
    hat, inv = norm_stats(x_ref[...].reshape(ROWS, D).astype(F32))
    e = gn * g_ref[...]
    out = gres_ref[...].reshape(ROWS, D) + inv * (e - jnp.mean(e, axis=-1, keepdims=True) - hat * jnp.mean(e * hat, axis=-1, keepdims=True))
    interleave(out, mix_ref, out_ref)
    sums_ref[pl.ds(0, 1), :] += jnp.sum(gn * hat, axis=0, keepdims=True)
    sums_ref[pl.ds(1, 1), :] += jnp.sum(gn, axis=0, keepdims=True)


def last_stage(first, count, gproj, in_w, x, gres, g):
    q = ROWS // PH
    rows = pl.BlockSpec((PH, q, D), lambda i: (0, first + i, 0))
    grads = pl.BlockSpec((3, PH, q, D), lambda i: (0, 0, first + i, 0))
    fold = lambda a: a.reshape(PH, ML, D)
    return pl.pallas_call(
        last_kernel,
        grid=(count,),
        in_specs=[grads, whole((D, 3 * D)), rows, rows, whole((1, D))],
        out_specs=[pl.BlockSpec((ROWS, D), lambda i: (i, 0)), pl.BlockSpec((8, D), lambda i: (0, 0))],
        out_shape=[jax.ShapeDtypeStruct((count * ROWS, D), BF16), jax.ShapeDtypeStruct((8, D), F32)],
        scratch_shapes=[pltpu.VMEM((D // 128, ROWS, 128), F32)],
        compiler_params=params(),
        cost_estimate=cost(2 * count * ROWS * D * 3 * D, 20 << 20),
        name=f"last_stage_{first}",
    )(gproj.reshape(3, PH, ML, D), in_w, fold(x), fold(gres), g)


def deinterleave(src_ref, mix_ref, put):
    q = ROWS // PH
    for c in range(D // 128):
        lanes = slice(c * 128, (c + 1) * 128)
        mix_ref[c] = src_ref[:, lanes].astype(F32)
        for r in range(PH):
            put(r, lanes, mix_ref[c, pl.ds(r, q, stride=PH), :])


def prep_kernel(x_ref, cot_ref, g_ref, s_ref, xp_ref, cp_ref, n1_ref, mix_ref, flat_ref):
    q = ROWS // PH

    def put_cot(r, lanes, value):
        cp_ref[r, :, lanes] = value.astype(BF16)

    def put_x(r, lanes, value):
        xp_ref[r, :, lanes] = value.astype(BF16)
        flat_ref[pl.ds(r * q, q), lanes] = value

    deinterleave(cot_ref, mix_ref, put_cot)
    deinterleave(x_ref, mix_ref, put_x)
    hat, _ = norm_stats(flat_ref[...])
    n1_ref[...] = (hat * g_ref[...] + s_ref[...]).astype(BF16).reshape(PH, q, D)


def prep(inputs, cotangent, g, s):
    flat = pl.BlockSpec((ROWS, D), lambda i: (i, 0))
    rows = pl.BlockSpec((PH, ROWS // PH, D), lambda i: (0, i, 0))
    out = jax.ShapeDtypeStruct((PH, ML, D), BF16)
    x, cot, n1 = pl.pallas_call(
        prep_kernel,
        grid=(L // ROWS,),
        in_specs=[flat, flat, whole((1, D)), whole((1, D))],
        out_specs=[rows] * 3,
        out_shape=[out] * 3,
        scratch_shapes=[pltpu.VMEM((D // 128, ROWS, 128), F32), pltpu.VMEM((ROWS, D), F32)],
        compiler_params=params(),
        cost_estimate=cost(20 * L * D, 20 << 20),
        name="prep",
    )(inputs, cotangent, g, s)
    return x.reshape(L, D), cot.reshape(L, D), n1.reshape(L, D)


def positions_table(places):
    places = places.astype(F32)
    harmonics = jnp.arange(1, BANDS + 1).astype(F32)
    angles = 2.0 * math.pi / L * places[:, None] * harmonics[None, :]
    return places, jnp.concatenate([places[:, None] / L, jnp.cos(angles), jnp.sin(angles)], axis=1)


def filter_values(places, network, rates):
    pos_weight, pos_bias, mid_weight, mid_bias, filter_weight = network
    places, features = positions_table(places)
    first_layer = jnp.sin(jnp.dot(features, pos_weight, precision=HIGH_ACCURACY) + pos_bias)
    second_layer = jnp.sin(jnp.dot(first_layer, mid_weight, precision=HIGH_ACCURACY) + mid_bias)
    shaped = jnp.dot(second_layer, filter_weight, precision=HIGH_ACCURACY)
    return shaped * (jnp.exp(-rates[None, :] * places[:, None] / L) + decay_floor)


VECTORS = (
    ("first_gain", 1), ("first_shift", 1), ("in_bias", 3), ("short", 9), ("skip", 1), ("out_bias", 1),
    ("second_gain", 1), ("second_shift", 1), ("up_bias", 4), ("down_bias", 1),
)


def swap_bit(x, axis, bit):
    size = lax.axis_size(axis)
    return lax.ppermute(x, axis, [(i, i ^ bit) for i in range(size)])


def add_low(*parts):
    total = parts[0].astype(F32)
    for part in parts[1:]:
        total = total + part.astype(F32)
    return total.astype(BF16)


def hold(*values):
    return lax.optimization_barrier(values)


def entry(x, i):
    return lax.dynamic_index_in_dim(x, i, 0, False)


def in_order(pieces, axis):
    place = lax.axis_index(axis)
    stacked = jnp.stack(pieces)
    return jnp.concatenate([entry(stacked, place ^ i) for i in range(len(pieces))], axis=0)


def spread_steps(x, axis, add):
    place = lax.axis_index(axis)
    got = yield [(entry(x, place ^ b), axis, b) for b in range(1, x.shape[0])]
    return add(entry(x, place), *got)


def collect_steps(x, axis):
    got = yield [(x, axis, b) for b in range(1, lax.axis_size(axis))]
    return in_order([x] + list(got), axis)


def halve_steps(x, axis):
    place = lax.axis_index(axis)
    bits = [1 << b for b in range(lax.axis_size(axis).bit_length() - 1)]
    rows = x.shape[1] // 2
    sides = [[x[:, :rows], bits[::-1], list(bits)], [x[:, rows:], bits, list(bits)]]
    for step in range(len(bits)):
        kept, sends = [], []
        for side in sides:
            value, order, left = side
            bit = order[step]
            at = sorted(left, reverse=True).index(bit)
            left.remove(bit)
            cube = value.reshape((2,) * (len(left) + 1) + value.shape[1:])
            mine = (place // bit) % 2
            part = lambda i: lax.dynamic_index_in_dim(cube, i, at, False).reshape((1 << len(left),) + value.shape[1:])
            kept.append(part(mine))
            sends.append((part(1 - mine), axis, bit))
        got = yield sends
        for side, keep, new in zip(sides, kept, got):
            side[0] = add_low(keep, new)
    return jnp.concatenate([side[0][0] for side in sides], axis=0)


def share_steps(share):
    z = lax.axis_size("z")
    rows, cols = share.shape
    mine = yield from spread_steps(share.reshape(z, rows // z, cols), "z", add_low)
    mine = yield from collect_steps(mine, "z")
    return (yield from collect_steps(mine, "core")).astype(F32)


def rows_steps(keep, send):
    (got,) = yield [(send, "core", 1)]
    mine = yield from halve_steps(add_low(keep, got), "mp")
    return (yield from share_steps(mine))


def flat_steps(x):
    for axis in ("core", "mp", "z"):
        for b in range(lax.axis_size(axis).bit_length() - 1):
            (got,) = yield [(x.astype(BF16), axis, 1 << b)]
            x = x.astype(BF16).astype(F32) + got.astype(F32)
    return x


class Chains:
    def __init__(self):
        self.live, self.done = {}, {}

    def start(self, name, steps):
        self.live[name] = (steps, next(steps))

    def move(self, names, first, kernel):
        names = [n for n in names if n in self.live]
        sends = [send for n in names for send in self.live[n][1]]
        held = hold(first, *(s[0] for s in sends))
        got = [swap_bit(v, s[1], s[2]) for v, s in zip(held[1:], sends)]
        out = kernel(held[0])
        flat, tree = jax.tree.flatten(out)
        held = hold(*flat, *got)
        out = jax.tree.unflatten(tree, held[:len(flat)])
        got = list(held[len(flat):])
        for n in names:
            steps, wanted = self.live.pop(n)
            arrived, got = got[:len(wanted)], got[len(wanted):]
            try:
                self.live[n] = (steps, steps.send(arrived))
            except StopIteration as stop:
                self.done[n] = stop.value
        return out

    def finish(self):
        while self.live:
            self.move(list(self.live), jnp.zeros((8, 128), F32), lambda v: v)


def scatter_rows(grad):
    return lax.psum_scatter(grad, ("mp", "core"), scatter_dimension=0, tiled=True)


def gather_rows(shard):
    rows = shard.shape[0]
    half = lax.dynamic_slice_in_dim(shard, lax.axis_index("core") * (rows // 2), rows // 2, 0)
    return lax.all_gather(half, ("mp", "core"), axis=0, tiled=True)


def shards(
    inputs, first_gain, first_shift, in_weight, in_bias, short_weight, skip_gain, pos_weight, pos_bias,
    mid_weight, mid_bias, filter_weight, decay_rates, out_weight, out_bias, second_gain, second_shift,
    up_weight, up_bias, down_weight, down_bias, cotangent,
):
    mp = lax.axis_size("mp")
    own = D // mp
    local = (first_gain, first_shift, in_bias, short_weight, skip_gain, out_bias, second_gain, second_shift, up_bias, down_bias)
    packed = jnp.concatenate([v.reshape(-1) for v in local]).reshape(1, -1)
    spread = lax.all_gather(packed, "mp", axis=0, tiled=True).astype(F32)
    full = {}
    at = 0
    for name, count in VECTORS:
        part = spread[:, at:at + count * own]
        at += count * own
        if name == "short":
            part = part.reshape(mp, 3, 3 * own).swapaxes(0, 1)
            full[name] = part.reshape(3, 3 * D)
        else:
            full[name] = part.reshape(1, count * D)
    in_matrix = gather_rows(in_weight)
    upout = gather_rows(jnp.concatenate([up_weight, out_weight], axis=1))
    down_matrix = gather_rows(down_weight)

    tab, itab = (jnp.asarray(t) for t in dft_tables())
    x, cot, n1 = prep(inputs, cotangent, full["first_gain"], full["first_shift"])
    places = (jnp.arange(PH)[:, None] + PH * jnp.arange(ML)[None, :]).reshape(L)
    network = (pos_weight, pos_bias, mid_weight, mid_bias, filter_weight)
    filters, filter_back = jax.vjp(lambda weights: filter_values(places, weights, decay_rates), network)
    spec = filter_spectrum(tab, filters.astype(BF16))
    proj, gate, gated, mixed, branch, sig = front(n1, in_matrix, full["in_bias"], full["short"], full["skip"], tab, itab, spec)
    res, n2, act, slope = up_stage(x, branch, upout, full["out_bias"], full["second_gain"], full["second_shift"], full["up_bias"])
    down_grad = weight_grad(act, cot, 1024, 1024, "down_weight_grad")
    act, down_grad = hold(act, down_grad)
    block_out, gh, gres, low, sums_two, up_bias_sum = down_stage(act, slope, res, cot, down_matrix, full["down_bias"], upout, full["second_gain"])
    down_share = scatter_rows(down_grad)
    chains = Chains()
    low, down_share = hold(low, down_share)
    down_half = lax.psum(down_share, "z")
    up_out = up_out_grad(n2, branch, gh, low)
    low, up_out = hold(low, up_out)
    up_share = scatter_rows(up_out)
    taps3 = full["short"].reshape(3, 3, D).swapaxes(0, 1)
    core = lax.axis_index("core").astype(jnp.int32).reshape(1)
    gproj, gfilt, sums_mid = back(0, D // TILE, low, upout, gate, proj, gated, mixed, sig, spec, taps3, full["skip"], tab, itab)
    gproj, down_half = hold(gproj, down_half)
    chains.start("down", collect_steps(down_half, "core"))
    keep, send = chains.move(["down"], gproj, lambda v: in_weight_grad(n1, v, core, mp))
    chains.start("in", rows_steps(keep, send))
    gfilt, up_share = hold(gfilt, up_share)
    chains.start("up", share_steps(up_share))
    net = chains.move(["in", "up"], gfilt, lambda v: filter_back(v.astype(F32))[0])
    mids = sums_mid[1:13].reshape(3, 4, D)
    vectors = {
        "in_bias": mids[:, 0].reshape(3 * D), "short": mids[:, 1:].swapaxes(0, 1).reshape(3, 3 * D), "skip": sums_mid[0],
        "out_bias": sums_two[2], "second_gain": sums_two[0], "second_shift": sums_two[1], "up_bias": up_bias_sum[0],
        "down_bias": sums_two[3],
    }
    flats = [vectors[name].reshape(-1) for name, _ in VECTORS if name in vectors] + [n.reshape(-1) for n in net]
    sizes = [f.shape[0] for f in flats]
    chains.start("flat", flat_steps(jnp.concatenate(flats + [jnp.zeros((-sum(sizes) % 1024,), F32)])))
    blocks = L // ROWS
    last = lambda first, v: last_stage(first, blocks // 2, v, in_matrix, x, gres, full["first_gain"])
    grad_lo, sums_lo = chains.move(["in", "up", "flat"], gproj, lambda v: last(0, v))
    grad_hi, sums_hi = chains.move(["in", "up", "flat"], gproj, lambda v: last(blocks // 2, v))
    input_grad = jnp.concatenate([grad_lo, grad_hi], axis=0)
    chains.start("first", flat_steps((sums_lo[:2] + sums_hi[:2]).reshape(-1)))
    chains.finish()
    done = chains.done
    down_sum = done["down"].astype(F32)
    up_sum, out_sum = done["up"][:, :FF].astype(F32), done["up"][:, FF:].astype(F32)
    in_sum = done["in"]
    pieces = {"first_gain": done["first"][:D], "first_shift": done["first"][D:]}
    at = 0
    names = [name for name, _ in VECTORS if name in vectors] + list(range(len(net)))
    for name, size in zip(names, sizes):
        pieces[name] = done["flat"][at:at + size]
        at += size
    me = lax.axis_index("mp")
    mine = {}
    for name, count in VECTORS:
        if name == "short":
            mine[name] = lax.dynamic_slice_in_dim(pieces[name].reshape(3, 3 * D), me * 3 * own, 3 * own, 1)
        else:
            mine[name] = lax.dynamic_slice_in_dim(pieces[name], me * count * own, count * own, 0)
    net_sum = [pieces[i].reshape(n.shape) for i, n in enumerate(net)]
    return (
        block_out, input_grad, mine["first_gain"], mine["first_shift"], in_sum, mine["in_bias"], mine["short"], mine["skip"],
        *net_sum, out_sum, mine["out_bias"], mine["second_gain"], mine["second_shift"], up_sum, mine["up_bias"],
        down_sum, mine["down_bias"],
    )


def solution(mesh):
    dp, mp = mesh.devices.shape
    split = jax.sharding.Mesh(mesh.devices.reshape(dp // 2, 2, mp), ("z", "core", "mp"))
    tokens = P(("z", "core", "mp"), None)
    row, vec, rep = P("mp", None), P("mp"), P()
    return jax.shard_map(
        shards,
        mesh=split,
        in_specs=(
            tokens, vec, vec, row, vec, P(None, "mp"), vec, rep, rep, rep, rep, rep, rep, row, vec, vec, vec, row, vec, row,
            vec, tokens,
        ),
        out_specs=(
            tokens, tokens, vec, vec, row, vec, P(None, "mp"), vec, rep, rep, rep, rep, rep, row, vec, vec, vec, row, vec,
            row, vec,
        ),
        check_vma=False,
    )
```

```python
import functools
import math

import jax
import jax.numpy as jnp
import numpy as np
from jax import lax
from jax.experimental import pallas as pl
from jax.experimental.pallas import tpu as pltpu
from jax.sharding import PartitionSpec as P

D = 1024
FF = 4096
BANDS = 16
L = 2048
PH = 4
ML = L // PH
TILE = 256
PAD = 8

HIGH_ACCURACY = lax.Precision.HIGHEST
eps = 1e-05
decay_floor = 0.05
F32 = jnp.float32
BF16 = jnp.bfloat16
VMEM_BYTES = 62 << 20


def dot_nn(a, b):
    return lax.dot_general(a, b, (((1,), (0,)), ((), ())), preferred_element_type=F32)


def dot_nt(a, b):
    return lax.dot_general(a, b, (((1,), (1,)), ((), ())), preferred_element_type=F32)


def dot_tn(a, b):
    return lax.dot_general(a, b, (((0,), (0,)), ((), ())), preferred_element_type=F32)


def dft_tables():
    times = PH * np.arange(ML)[None, None, :] + np.arange(PH)[:, None, None]
    odd = 2 * np.arange(ML)[None, :, None] + 1
    angle = 2.0 * np.pi / (4 * L) * ((times * odd) % (4 * L)).astype(np.float64)
    table = np.concatenate([np.cos(angle), -np.sin(angle)], axis=1)
    forward = table.reshape(PH * 2 * ML, ML).astype(jnp.bfloat16)
    backward = np.swapaxes(table, 1, 2).reshape(PH * ML, 2 * ML).astype(jnp.bfloat16)
    return forward, backward


def whole(shape):
    return pl.BlockSpec(shape, lambda *_: (0,) * len(shape), pipeline_mode=pl.Buffered(1))


def params(**kw):
    return pltpu.CompilerParams(vmem_limit_bytes=VMEM_BYTES, **kw)


def cost(flops, moved):
    return pl.CostEstimate(flops=int(flops), bytes_accessed=int(moved), transcendentals=0)


def forward_dft(tab_ref, src, dst_ref):
    for r in range(PH):
        dst_ref[pl.ds(r * 2 * ML, 2 * ML), :] = dot_nn(tab_ref[pl.ds(r * 2 * ML, 2 * ML), :], src(r)).astype(BF16)


def split_bins(part, rows):
    re = [part(r * 2 * ML + rows) for r in range(PH)]
    im = [part(r * 2 * ML + ML + rows) for r in range(PH)]
    ar, ai, br, bi = re[0] + re[2], im[0] + im[2], re[0] - re[2], im[0] - im[2]
    cr, ci, dr, di = re[1] + re[3], im[1] + im[3], re[1] - re[3], im[1] - im[3]
    return [(ar + cr, ai + ci), (br + di, bi - dr), (ar - cr, ai - ci), (br - di, bi + dr)]


def join_bins(bins, put, rows):
    (r0, i0), (r1, i1), (r2, i2), (r3, i3) = bins
    ar, ai, br, bi = r0 + r2, i0 + i2, r0 - r2, i0 - i2
    cr, ci, dr, di = r1 + r3, i1 + i3, r1 - r3, i1 - i3
    out = [(ar + cr, ai + ci), (br - di, bi + dr), (ar - cr, ai - ci), (br + di, bi - dr)]
    for r in range(PH):
        put(r * 2 * ML + rows, out[r][0])
        put(r * 2 * ML + ML + rows, out[r][1])


def filter_kernel(tab_ref, filt_ref, spec_ref, part_ref):
    forward_dft(tab_ref, lambda r: filt_ref[pl.ds(r * ML, ML), :], part_ref)
    step = 16

    @pl.loop(0, ML // step)
    def _(i):
        rows = pl.multiple_of(i * step, step)
        bins = split_bins(lambda at: part_ref[pl.ds(at, step), :], rows)
        for j in range(PH):
            spec_ref[pl.ds(j * 2 * ML + rows, step), :] = bins[j][0] * jnp.bfloat16(1.0 / L)
            spec_ref[pl.ds(j * 2 * ML + ML + rows, step), :] = bins[j][1] * jnp.bfloat16(1.0 / L)


def filter_spectrum(tab, filters):
    return pl.pallas_call(
        filter_kernel,
        grid=(D // TILE,),
        in_specs=[whole((PH * 2 * ML, ML)), pl.BlockSpec((L, TILE), lambda i: (0, i))],
        out_specs=pl.BlockSpec((2 * L, TILE), lambda i: (0, i)),
        out_shape=jax.ShapeDtypeStruct((2 * L, D), BF16),
        scratch_shapes=[pltpu.VMEM((2 * L, TILE), BF16)],
        compiler_params=params(),
        cost_estimate=cost(2 * 2 * L * ML * D, 16 << 20),
        name="filter_spectrum",
    )(tab, filters)


def front_kernel(
    n1_ref, wa_ref, wb_ref, wc_ref, ba_ref, bb_ref, bc_ref, ta_ref, tb_ref, tc_ref, skip_ref,
    tab_ref, itab_ref, spec_ref,
    proj_ref, gate_ref, gated_ref, mixed_ref, branch_ref, sig_ref,
    sa_ref, sb_ref, sc_ref, part_ref, turn_ref, long_ref,
):
    scr = (sa_ref, sb_ref, sc_ref)
    for ref, w_ref, b_ref in zip(scr, (wa_ref, wb_ref, wc_ref), (ba_ref, bb_ref, bc_ref)):
        for r in range(PH):
            ref[r, pl.ds(0, PAD), :] = jnp.zeros((PAD, TILE), F32)
            ref[r, pl.ds(PAD, ML), :] = dot_nn(n1_ref[pl.ds(r * ML, ML), :], w_ref[...]) + b_ref[...]
    taps = [[t[pl.ds(j, 1), :] for j in range(3)] for t in (ta_ref, tb_ref, tc_ref)]
    step = 32

    @pl.loop(0, ML // step)
    def _(i):
        rows = pl.multiple_of(i * step, step)
        outs = []
        for n in range(3):
            ref = scr[n]
            p = [ref[r, pl.ds(PAD + rows, step), :] for r in range(PH)]
            low = [pltpu.roll(ref[r, pl.ds(rows, step + PAD), :], 1, 0)[PAD:, :] for r in (2, 3)]
            seq = low + p
            w0, w1, w2 = taps[n]
            short = [w0 * seq[r + 2] + w1 * seq[r + 1] + w2 * seq[r] for r in range(PH)]
            for r in range(PH):
                proj_ref[n, pl.ds(r * ML + rows, step), :] = p[r].astype(BF16)
                gate_ref[n, pl.ds(r * ML + rows, step), :] = short[r].astype(BF16)
            outs.append(short)
        for r in range(PH):
            gated_ref[pl.ds(r * ML + rows, step), :] = (outs[1][r] * outs[2][r]).astype(BF16)

    forward_dft(tab_ref, lambda r: gated_ref[pl.ds(r * ML, ML), :], part_ref)
    step2 = 32

    @pl.loop(0, ML // step2)
    def _(i):
        rows = pl.multiple_of(i * step2, step2)
        bins = split_bins(lambda at: part_ref[pl.ds(at, step2), :], rows)
        out = []
        for j in range(PH):
            xr, xi = bins[j]
            at = j * 2 * ML + rows
            sig_ref[pl.ds(at, step2), :] = xr
            sig_ref[pl.ds(at + ML, step2), :] = xi
            hr = spec_ref[pl.ds(at, step2), :]
            hi = spec_ref[pl.ds(at + ML, step2), :]
            out.append((xr * hr - xi * hi, xr * hi + xi * hr))

        def put(at, value):
            turn_ref[pl.ds(at, step2), :] = value

        join_bins(out, put, rows)

    skip = skip_ref[...]
    for r in range(PH):
        long_ref[pl.ds(r * ML, ML), :] = dot_nn(
            itab_ref[pl.ds(r * ML, ML), :], turn_ref[pl.ds(r * 2 * ML, 2 * ML), :]
        )

    @pl.loop(0, ML // step)
    def _(i):
        rows = pl.multiple_of(i * step, step)
        for r in range(PH):
            at = pl.ds(r * ML + rows, step)
            mixed = long_ref[at, :] + skip * gated_ref[at, :].astype(F32)
            mixed_ref[at, :] = mixed.astype(BF16)
            branch_ref[at, :] = (gate_ref[0, at, :].astype(F32) * mixed).astype(BF16)


def front(n1, in_w, in_b, taps, skip, tab, itab, spec):
    nt = D // TILE
    cols = lambda k: pl.BlockSpec((D, TILE), lambda i, k=k: (0, k * nt + i))
    row = lambda k, h: pl.BlockSpec((h, TILE), lambda i, k=k: (0, k * nt + i))
    out = pl.BlockSpec((L, TILE), lambda i: (0, i))
    out3 = pl.BlockSpec((3, L, TILE), lambda i: (0, 0, i))
    return pl.pallas_call(
        front_kernel,
        grid=(nt,),
        in_specs=[whole((L, D))] + [cols(k) for k in range(3)] + [row(k, 1) for k in range(3)]
        + [row(k, 3) for k in range(3)] + [row(0, 1), whole((PH * 2 * ML, ML)), whole((PH * ML, 2 * ML)),
           pl.BlockSpec((2 * L, TILE), lambda i: (0, i))],
        out_specs=[out3, out3, out, out, out, pl.BlockSpec((2 * L, TILE), lambda i: (0, i))],
        out_shape=[
            jax.ShapeDtypeStruct((3, L, D), BF16), jax.ShapeDtypeStruct((3, L, D), BF16),
            jax.ShapeDtypeStruct((L, D), BF16), jax.ShapeDtypeStruct((L, D), BF16),
            jax.ShapeDtypeStruct((L, D), BF16), jax.ShapeDtypeStruct((2 * L, D), BF16),
        ],
        scratch_shapes=[pltpu.VMEM((PH, PAD + ML, TILE), F32)] * 3
        + [pltpu.VMEM((2 * L, TILE), BF16), pltpu.VMEM((2 * L, TILE), BF16), pltpu.VMEM((L, TILE), F32)],
        compiler_params=params(),
        cost_estimate=cost(2 * L * D * 3 * D + 4 * 2 * L * ML * D, 80 << 20),
        name="front",
    )(n1, in_w, in_w, in_w, in_b, in_b, in_b, taps, taps, taps, skip, tab, itab, spec)


def gelu_parts(h):
    c = lambda v: jnp.bfloat16(v)
    h = h.astype(BF16)
    t = c(1.0) / (c(1.0) + c(0.3275911 / math.sqrt(2.0)) * jnp.abs(h))
    bell = jnp.exp(c(-0.5) * h * h)
    poly = c(0.5 * 1.061405429) * t - c(0.5 * 1.453152027)
    for k in (0.5 * 1.421413741, -0.5 * 0.284496736, 0.5 * 0.254829592):
        poly = poly * t + c(k)
    tail = poly * t * bell
    phi = jnp.where(h >= 0, c(1.0) - tail, tail)
    return h * phi, phi + h * (bell * c(1.0 / math.sqrt(2.0 * math.pi)))


def norm_stats(v):
    centre = jnp.mean(v, axis=-1, keepdims=True)
    centred = v - centre
    inv = lax.rsqrt(jnp.mean(centred * centred, axis=-1, keepdims=True) + eps)
    return centred * inv, inv


ROWS = 256
CHUNK = 512


def up_kernel(x_ref, branch_ref, ow_ref, ob_ref, g_ref, s_ref, uw_ref, ub_ref, res_ref, n2_ref, act_ref, slope_ref):
    res = x_ref[...].astype(F32) + dot_nn(branch_ref[...], ow_ref[...]) + ob_ref[...]
    res_ref[...] = res
    hat, _ = norm_stats(res)
    n2_ref[...] = (hat * g_ref[...] + s_ref[...]).astype(BF16)
    n2 = n2_ref[...]
    for c in range(FF // CHUNK):
        at = pl.ds(c * CHUNK, CHUNK)
        h = dot_nn(n2, uw_ref[:, at]) + ub_ref[:, at]
        act, slope = gelu_parts(h)
        act_ref[:, at] = act
        slope_ref[:, at] = slope


def up_part():
    return pl.BlockSpec((D, FF), lambda *_: (0, 0), pipeline_mode=pl.Buffered(1))


def out_part():
    return pl.BlockSpec((D, D), lambda *_: (0, FF // D), pipeline_mode=pl.Buffered(1))


def up_stage(x, branch, upout, ob, g, s, ub):
    rows = lambda n: pl.BlockSpec((ROWS, n), lambda i: (i, 0))
    return pl.pallas_call(
        up_kernel,
        grid=(L // ROWS,),
        in_specs=[rows(D), rows(D), out_part(), whole((1, D)), whole((1, D)), whole((1, D)), up_part(), whole((1, FF))],
        out_specs=[rows(D), rows(D), rows(FF), rows(FF)],
        out_shape=[
            jax.ShapeDtypeStruct((L, D), F32), jax.ShapeDtypeStruct((L, D), BF16),
            jax.ShapeDtypeStruct((L, FF), BF16), jax.ShapeDtypeStruct((L, FF), BF16),
        ],
        compiler_params=params(),
        cost_estimate=cost(2 * L * D * (D + FF), 60 << 20),
        name="up_stage",
    )(x, branch, upout, ob, g, s, upout, ub)


def interleave(value, mix_ref, out_ref):
    q = ROWS // PH
    for c in range(D // 128):
        lanes = slice(c * 128, (c + 1) * 128)
        for r in range(PH):
            mix_ref[c, pl.ds(r, q, stride=PH), :] = value[r * q:(r + 1) * q, lanes]
        out_ref[:, lanes] = mix_ref[c].astype(BF16)


def down_kernel(act_ref, slope_ref, res_ref, cot_ref, dw_ref, db_ref, uw_ref, g_ref, out_ref, gh_ref, gres_ref, low_ref, sums_ref, ubg_ref, mix_ref):
    i = pl.program_id(0)

    @pl.when(i == 0)
    def _():
        sums_ref[...] = jnp.zeros_like(sums_ref)
        ubg_ref[...] = jnp.zeros_like(ubg_ref)

    res = res_ref[...].reshape(ROWS, D)
    cot = cot_ref[...].reshape(ROWS, D)
    for c in range(FF // CHUNK):
        at = pl.ds(c * CHUNK, CHUNK)
        ga = dot_nt(cot, dw_ref[at, :])
        gh = (ga * slope_ref[:, :, at].reshape(ROWS, CHUNK).astype(F32)).astype(BF16)
        gh_ref[:, :, at] = gh.reshape(PH, ROWS // PH, CHUNK)
        ubg_ref[pl.ds(0, 1), at] += jnp.sum(gh.astype(F32), axis=0, keepdims=True)
    out = res + dot_nn(act_ref[...].reshape(ROWS, FF), dw_ref[...]) + db_ref[...]
    interleave(out, mix_ref, out_ref)
    gn = dot_nt(gh_ref[...].reshape(ROWS, FF), uw_ref[...])
    hat, inv = norm_stats(res)
    e = gn * g_ref[...]
    cot32 = cot.astype(F32)
    gres = cot32 + inv * (e - jnp.mean(e, axis=-1, keepdims=True) - hat * jnp.mean(e * hat, axis=-1, keepdims=True))
    low = gres.astype(BF16)
    gres_ref[...] = gres.reshape(PH, ROWS // PH, D)
    low_ref[...] = low.reshape(PH, ROWS // PH, D)
    sums_ref[pl.ds(0, 1), :] += jnp.sum(gn * hat, axis=0, keepdims=True)
    sums_ref[pl.ds(1, 1), :] += jnp.sum(gn, axis=0, keepdims=True)
    sums_ref[pl.ds(2, 1), :] += jnp.sum(low.astype(F32), axis=0, keepdims=True)
    sums_ref[pl.ds(3, 1), :] += jnp.sum(cot32, axis=0, keepdims=True)


def down_stage(act, slope, res, cot, dw, db, uw, g):
    q = ROWS // PH
    rows = lambda n: pl.BlockSpec((PH, q, n), lambda i: (0, i, 0))
    fold = lambda a: a.reshape(PH, ML, a.shape[-1])
    out, gh, gres, low, sums, ubg = pl.pallas_call(
        down_kernel,
        grid=(L // ROWS,),
        in_specs=[rows(FF), rows(FF), rows(D), rows(D), whole((FF, D)), whole((1, D)), up_part(), whole((1, D))],
        out_specs=[pl.BlockSpec((ROWS, D), lambda i: (i, 0)), rows(FF), rows(D), rows(D),
                   pl.BlockSpec((8, D), lambda i: (0, 0)), pl.BlockSpec((8, FF), lambda i: (0, 0))],
        out_shape=[
            jax.ShapeDtypeStruct((L, D), BF16), jax.ShapeDtypeStruct((PH, ML, FF), BF16),
            jax.ShapeDtypeStruct((PH, ML, D), F32), jax.ShapeDtypeStruct((PH, ML, D), BF16),
            jax.ShapeDtypeStruct((8, D), F32), jax.ShapeDtypeStruct((8, FF), F32),
        ],
        scratch_shapes=[pltpu.VMEM((D // 128, ROWS, 128), F32)],
        compiler_params=params(),
        cost_estimate=cost(2 * L * D * 3 * FF, 100 << 20),
        name="down_stage",
    )(fold(act), fold(slope), fold(res), fold(cot), dw, db, uw, g)
    return out, gh.reshape(L, FF), gres.reshape(L, D), low.reshape(L, D), sums, ubg


def grad_kernel(a_ref, b_ref, o_ref):
    o_ref[...] = dot_tn(a_ref[...], b_ref[...]).astype(o_ref.dtype)


def weight_grad(a, b, bm, bn, name):
    m, n = a.shape[1], b.shape[1]
    return pl.pallas_call(
        grad_kernel,
        grid=(m // bm, n // bn),
        in_specs=[pl.BlockSpec((L, bm), lambda i, j: (0, i)), pl.BlockSpec((L, bn), lambda i, j: (0, j))],
        out_specs=pl.BlockSpec((bm, bn), lambda i, j: (i, j)),
        out_shape=jax.ShapeDtypeStruct((m, n), BF16),
        compiler_params=params(),
        cost_estimate=cost(2 * L * m * n, 2 * (L * (m + n) + m * n)),
        name=name,
    )(a, b)


def short_back(n, step, scr, taps_ref, proj_ref, gproj_ref, sums_ref):
    ref = scr[n]
    w = [taps_ref[n, pl.ds(j, 1), :] for j in range(3)]

    def second(i, acc, ref=ref, w=w, n=n):
        rows = pl.multiple_of(i * step, step)
        seq = [ref[r, pl.ds(rows, step), :] for r in range(PH)]
        seq += [pltpu.roll(ref[r, pl.ds(rows, step + PAD), :], step + PAD - 1, 0)[:step, :] for r in range(2)]
        acc = list(acc)
        for r in range(PH):
            at = pl.ds(r * ML + rows, step)
            g = (w[0] * seq[r] + w[1] * seq[r + 1] + w[2] * seq[r + 2]).astype(BF16)
            gproj_ref[n, at, :] = g
            p = proj_ref[n, at, :].astype(F32)
            terms = (g.astype(F32), seq[r] * p, seq[r + 1] * p, seq[r + 2] * p)
            for q in range(4):
                for k in range(step // 8):
                    acc[q] = acc[q] + terms[q][k * 8:(k + 1) * 8, :]
        return tuple(acc)

    zero = jnp.zeros((8, TILE), F32)
    acc = lax.fori_loop(0, ML // step, second, (zero,) * 4)
    for q in range(4):
        sums_ref[pl.ds(1 + 4 * n + q, 1), :] = jnp.sum(acc[q], axis=0, keepdims=True)


def back_kernel(
    low_ref, ow_ref, gate_ref, proj_ref, gated_ref, mixed_ref, sig_ref, spec_ref, taps_ref, skip_ref, tab_ref, itab_ref,
    gproj_ref, gfilt_ref, sums_ref,
    gb_ref, gl_ref, part_ref, turn_ref, cross_ref, long_ref, s1_ref, s2_ref,
):
    scr = (s1_ref, s1_ref, s2_ref)
    gb_ref[...] = dot_nt(low_ref[...], ow_ref[...])
    step = 32
    skip = skip_ref[...]

    def first(i, acc):
        rows = pl.multiple_of(i * step, step)
        for r in range(PH):
            at = pl.ds(r * ML + rows, step)
            gb = gb_ref[at, :]
            gp = gb * gate_ref[0, at, :].astype(F32)
            gl_ref[at, :] = gp.astype(BF16)
            s1_ref[r, pl.ds(rows, step), :] = gb * mixed_ref[at, :].astype(F32)
            gb_ref[at, :] = gp
            prod = gp * gated_ref[at, :].astype(F32)
            for k in range(step // 8):
                acc = acc + prod[k * 8:(k + 1) * 8, :]
        return acc

    acc = lax.fori_loop(0, ML // step, first, jnp.zeros((8, TILE), F32))
    sums_ref[pl.ds(0, 1), :] = jnp.sum(acc, axis=0, keepdims=True)
    for ref in (s1_ref, s2_ref):
        for r in range(2):
            ref[r, pl.ds(ML, PAD), :] = jnp.zeros((PAD, TILE), F32)
    short_back(0, step, scr, taps_ref, proj_ref, gproj_ref, sums_ref)
    forward_dft(tab_ref, lambda r: gl_ref[pl.ds(r * ML, ML), :], part_ref)
    step2 = 32

    @pl.loop(0, ML // step2)
    def _(i):
        rows = pl.multiple_of(i * step2, step2)
        bins = split_bins(lambda at: part_ref[pl.ds(at, step2), :], rows)
        for other_ref, into_ref in ((spec_ref, turn_ref), (sig_ref, cross_ref)):
            out = []
            for j in range(PH):
                gr, gi = bins[j]
                at = j * 2 * ML + rows
                hr = other_ref[pl.ds(at, step2), :]
                hi = other_ref[pl.ds(at + ML, step2), :]
                out.append((hr * gr + hi * gi, hr * gi - hi * gr))

            def put(at, value, into_ref=into_ref):
                into_ref[pl.ds(at, step2), :] = value

            join_bins(out, put, rows)

    for r in range(PH):
        rows = pl.ds(r * ML, ML)
        freq = pl.ds(r * 2 * ML, 2 * ML)
        gfilt_ref[rows, :] = (dot_nn(itab_ref[rows, :], cross_ref[freq, :]) * (1.0 / L)).astype(BF16)
        long_ref[rows, :] = dot_nn(itab_ref[rows, :], turn_ref[freq, :])

    @pl.loop(0, ML // step)
    def _(i):
        rows = pl.multiple_of(i * step, step)
        for r in range(PH):
            at = pl.ds(r * ML + rows, step)
            gg = long_ref[at, :] + gb_ref[at, :] * skip
            s1_ref[r, pl.ds(rows, step), :] = gg * gate_ref[2, at, :].astype(F32)
            s2_ref[r, pl.ds(rows, step), :] = gg * gate_ref[1, at, :].astype(F32)

    for n in (1, 2):
        short_back(n, step, scr, taps_ref, proj_ref, gproj_ref, sums_ref)


def back(first, nt, low, upout, gate, proj, gated, mixed, sig, spec, taps3, skip, tab, itab):
    width = nt * TILE
    tile = lambda h: pl.BlockSpec((h, TILE), lambda i: (0, first + i))
    tile3 = lambda h: pl.BlockSpec((3, h, TILE), lambda i: (0, 0, first + i))
    once = lambda h: pl.BlockSpec((h, TILE), lambda i: (0, first + i), pipeline_mode=pl.Buffered(1))
    out = lambda h: pl.BlockSpec((h, TILE), lambda i: (0, i))
    return pl.pallas_call(
        back_kernel,
        grid=(nt,),
        in_specs=[whole((L, D)), pl.BlockSpec((TILE, D), lambda i: (first + i, FF // D)), tile3(L), tile3(L), once(L), once(L),
                  tile(2 * L), tile(2 * L), tile3(3), tile(1), whole((PH * 2 * ML, ML)), whole((PH * ML, 2 * ML))],
        out_specs=[pl.BlockSpec((3, L, TILE), lambda i: (0, 0, i)), out(L), out(16)],
        out_shape=[
            jax.ShapeDtypeStruct((3, L, width), BF16), jax.ShapeDtypeStruct((L, width), BF16), jax.ShapeDtypeStruct((16, width), F32),
        ],
        scratch_shapes=[
            pltpu.VMEM((L, TILE), F32), pltpu.VMEM((L, TILE), BF16), pltpu.VMEM((2 * L, TILE), BF16),
            pltpu.VMEM((2 * L, TILE), BF16), pltpu.VMEM((2 * L, TILE), BF16), pltpu.VMEM((L, TILE), F32),
        ] + [pltpu.VMEM((PH, ML + PAD, TILE), F32)] * 2,
        compiler_params=params(),
        cost_estimate=cost(2 * L * D * width + 12 * L * ML * width, (80 << 20) * nt // 4),
        name=f"back_{first}",
    )(low, upout, gate, proj, gated, mixed, sig, spec, taps3, skip, tab, itab)


def in_grad_kernel(core_ref, n1_ref, g_ref, keep_ref, send_ref):
    core = core_ref[0]
    count, blocks, half, width = keep_ref.shape
    value = dot_tn(n1_ref[...], g_ref[0]).astype(BF16).reshape(blocks, 2, half, D)
    keep = jnp.where(core == 0, value[:, 0], value[:, 1])
    send = jnp.where(core == 0, value[:, 1], value[:, 0])
    for i in range(count):
        at = slice(i * width, (i + 1) * width)
        keep_ref[i] = keep[:, :, at]
        send_ref[i] = send[:, :, at]


def in_weight_grad(n1, gproj, core, owners, width):
    bm = 512
    half = D // (2 * owners)
    out = pl.BlockSpec((D // width, bm // (2 * half), half, width), lambda i, j, c: (j, i, 0, 0))
    shape = jax.ShapeDtypeStruct((3 * D // width, owners, half, width), BF16)
    return pl.pallas_call(
        in_grad_kernel,
        grid_spec=pltpu.PrefetchScalarGridSpec(
            num_scalar_prefetch=1,
            grid=(D // bm, 3),
            in_specs=[pl.BlockSpec((L, bm), lambda i, j, c: (0, i)), pl.BlockSpec((1, L, D), lambda i, j, c: (j, 0, 0))],
            out_specs=[out, out],
        ),
        out_shape=[shape, shape],
        compiler_params=params(),
        cost_estimate=cost(2 * L * D * 3 * D, 40 << 20),
        name="in_weight_grad",
    )(core, n1, gproj)


def up_out_kernel(n2_ref, br_ref, gh_ref, low_ref, o_ref):
    j = pl.program_id(0)

    @pl.when(j < FF // D)
    def _():
        o_ref[...] = dot_tn(n2_ref[...], gh_ref[...]).astype(BF16)

    @pl.when(j == FF // D)
    def _():
        o_ref[...] = dot_tn(br_ref[...], low_ref[...]).astype(BF16)


def up_out_grad(n2, branch, gh, low):
    nj = FF // D
    return pl.pallas_call(
        up_out_kernel,
        grid=(nj + 1,),
        in_specs=[whole((L, D)), whole((L, D)), pl.BlockSpec((L, D), lambda j: (0, jnp.minimum(j, nj - 1))), whole((L, D))],
        out_specs=pl.BlockSpec((D, D), lambda j: (0, j)),
        out_shape=jax.ShapeDtypeStruct((D, FF + D), BF16),
        compiler_params=params(),
        cost_estimate=cost(2 * L * D * (FF + D), 40 << 20),
        name="up_out_grad",
    )(n2, branch, gh, low)


def last_kernel(gp_ref, iw_ref, x_ref, gres_ref, g_ref, out_ref, sums_ref, mix_ref):
    i = pl.program_id(0)

    @pl.when(i == 0)
    def _():
        sums_ref[...] = jnp.zeros_like(sums_ref)

    both = jnp.concatenate([gp_ref[n].reshape(ROWS, D) for n in range(3)], axis=1)
    gn = dot_nt(both, iw_ref[...])
    hat, inv = norm_stats(x_ref[...].reshape(ROWS, D).astype(F32))
    e = gn * g_ref[...]
    out = gres_ref[...].reshape(ROWS, D) + inv * (e - jnp.mean(e, axis=-1, keepdims=True) - hat * jnp.mean(e * hat, axis=-1, keepdims=True))
    interleave(out, mix_ref, out_ref)
    sums_ref[pl.ds(0, 1), :] += jnp.sum(gn * hat, axis=0, keepdims=True)
    sums_ref[pl.ds(1, 1), :] += jnp.sum(gn, axis=0, keepdims=True)


def last_stage(first, count, gproj, in_w, x, gres, g):
    q = ROWS // PH
    rows = pl.BlockSpec((PH, q, D), lambda i: (0, first + i, 0))
    grads = pl.BlockSpec((3, PH, q, D), lambda i: (0, 0, first + i, 0))
    fold = lambda a: a.reshape(PH, ML, D)
    return pl.pallas_call(
        last_kernel,
        grid=(count,),
        in_specs=[grads, whole((D, 3 * D)), rows, rows, whole((1, D))],
        out_specs=[pl.BlockSpec((ROWS, D), lambda i: (i, 0)), pl.BlockSpec((8, D), lambda i: (0, 0))],
        out_shape=[jax.ShapeDtypeStruct((count * ROWS, D), BF16), jax.ShapeDtypeStruct((8, D), F32)],
        scratch_shapes=[pltpu.VMEM((D // 128, ROWS, 128), F32)],
        compiler_params=params(),
        cost_estimate=cost(2 * count * ROWS * D * 3 * D, 20 << 20),
        name=f"last_stage_{first}",
    )(gproj.reshape(3, PH, ML, D), in_w, fold(x), fold(gres), g)


def deinterleave(src_ref, mix_ref, put):
    q = ROWS // PH
    for c in range(D // 128):
        lanes = slice(c * 128, (c + 1) * 128)
        mix_ref[c] = src_ref[:, lanes].astype(F32)
        for r in range(PH):
            put(r, lanes, mix_ref[c, pl.ds(r, q, stride=PH), :])


def prep_kernel(x_ref, cot_ref, g_ref, s_ref, xp_ref, cp_ref, n1_ref, mix_ref, flat_ref):
    q = ROWS // PH

    def put_cot(r, lanes, value):
        cp_ref[r, :, lanes] = value.astype(BF16)

    def put_x(r, lanes, value):
        xp_ref[r, :, lanes] = value.astype(BF16)
        flat_ref[pl.ds(r * q, q), lanes] = value

    deinterleave(cot_ref, mix_ref, put_cot)
    deinterleave(x_ref, mix_ref, put_x)
    hat, _ = norm_stats(flat_ref[...])
    n1_ref[...] = (hat * g_ref[...] + s_ref[...]).astype(BF16).reshape(PH, q, D)


def prep(inputs, cotangent, g, s):
    flat = pl.BlockSpec((ROWS, D), lambda i: (i, 0))
    rows = pl.BlockSpec((PH, ROWS // PH, D), lambda i: (0, i, 0))
    out = jax.ShapeDtypeStruct((PH, ML, D), BF16)
    x, cot, n1 = pl.pallas_call(
        prep_kernel,
        grid=(L // ROWS,),
        in_specs=[flat, flat, whole((1, D)), whole((1, D))],
        out_specs=[rows] * 3,
        out_shape=[out] * 3,
        scratch_shapes=[pltpu.VMEM((D // 128, ROWS, 128), F32), pltpu.VMEM((ROWS, D), F32)],
        compiler_params=params(),
        cost_estimate=cost(20 * L * D, 20 << 20),
        name="prep",
    )(inputs, cotangent, g, s)
    return x.reshape(L, D), cot.reshape(L, D), n1.reshape(L, D)


def positions_table(places):
    places = places.astype(F32)
    harmonics = jnp.arange(1, BANDS + 1).astype(F32)
    angles = 2.0 * math.pi / L * places[:, None] * harmonics[None, :]
    return places, jnp.concatenate([places[:, None] / L, jnp.cos(angles), jnp.sin(angles)], axis=1)


def filter_values(places, network, rates):
    pos_weight, pos_bias, mid_weight, mid_bias, filter_weight = network
    places, features = positions_table(places)
    first_layer = jnp.sin(jnp.dot(features, pos_weight, precision=HIGH_ACCURACY) + pos_bias)
    second_layer = jnp.sin(jnp.dot(first_layer, mid_weight, precision=HIGH_ACCURACY) + mid_bias)
    shaped = jnp.dot(second_layer, filter_weight, precision=HIGH_ACCURACY)
    return shaped * (jnp.exp(-rates[None, :] * places[:, None] / L) + decay_floor)


def finish_kernel(
    sizes, keep_ref, send_ref, flat_ref, gain_ref, gp_any, iw_any, x_any, gres_any, out_any, rows_ref, total_ref, firsts_ref,
    gp, iw, xs, gres, mix, done_ref, f0, r1, half, r2, part, r3, sum_ref, f1, g1, f2, g2, g3, u1, u2, u3, sem_s, sem_r, sem_l,
):
    mp, z = sizes
    me = {name: lax.axis_index(name) for name in ("z", "core", "mp")}
    other = {"core": 1 - me["core"]}
    to_mp = [(b, {"mp": lax.rem(me["mp"] + b, mp)}) for b in range(1, mp)]
    to_z = [(b, {"z": lax.rem(me["z"] + b, z)}) for b in range(1, z)]
    q = ROWS // PH
    tiles = L // ROWS

    def load(i, src, dst):
        out = pltpu.make_async_copy(src, dst, sem_l.at[i])
        out.start()
        return out

    loads, stores = {}, []

    def fetch(i):
        if i < tiles:
            at = pl.ds(i * q, q)
            loads[i] = [
                load(1 + 3 * i, gp_any.at[:, :, at], gp.at[:, :, at]),
                load(2 + 3 * i, x_any.at[:, at], xs.at[:, at]),
                load(3 + 3 * i, gres_any.at[:, at], gres.at[:, at]),
            ]

    def last_tile(i):
        at = pl.ds(i * q, q)
        for c in loads[i]:
            c.wait()
        fetch(i + 2)
        both = jnp.concatenate([gp[n, :, at].reshape(ROWS, D) for n in range(3)], axis=1)
        gn = dot_nt(both, iw[...])
        hat, inv = norm_stats(xs[:, at].reshape(ROWS, D).astype(F32))
        e = gn * gain_ref[...]
        fix = jnp.mean(e, axis=-1, keepdims=True) + hat * jnp.mean(e * hat, axis=-1, keepdims=True)
        natural = pl.ds(i * ROWS, ROWS)
        interleave(gres[:, at].reshape(ROWS, D) + inv * (e - fix), mix, done_ref.at[natural])
        stores.append(load(1 + 3 * tiles + i, done_ref.at[natural], out_any.at[natural]))
        return jnp.sum(gn * hat, axis=0, keepdims=True), jnp.sum(gn, axis=0, keepdims=True)

    barrier = pltpu.get_barrier_semaphore()
    peers = [other] + [p for _, p in to_mp] + [p for _, p in to_z]
    for peer in peers:
        pl.semaphore_signal(barrier, inc=1, device_id=peer, device_id_type=pl.DeviceIdType.MESH)
    pl.semaphore_wait(barrier, len(peers))

    count = [0]

    def copy(src, dst, peer):
        i = count[0]
        count[0] += 1
        out = pltpu.make_async_remote_copy(
            src_ref=src, dst_ref=dst, send_sem=sem_s.at[i], recv_sem=sem_r.at[i], device_id=peer,
            device_id_type=pl.DeviceIdType.MESH,
        )
        out.start()
        return out

    chunks = keep_ref.shape[0]
    rows, width = keep_ref.shape[2:]
    piece = width // z
    sent = []

    def wait(copies):
        for c in copies:
            c.wait_recv()
        sent.extend(copies)

    cols = lambda i: pl.ds(pl.multiple_of(i * piece, piece), piece)
    mine = cols(me["z"])
    first = [copy(send_ref.at[c], r1.at[c], other) for c in range(chunks)]
    flat_now = [[copy(flat_ref.at[1 - me["core"]], g1, other)]]
    second, third, fourth, fifth = {}, {}, {}, {}

    def step_one(c):
        wait([first[c]])
        half[c] = (keep_ref[c].astype(F32) + r1[c].astype(F32)).astype(BF16)
        second[c] = [copy(half.at[c, p["mp"]], r2.at[c, b - 1], p) for b, p in to_mp]

    def step_two(c):
        total = half[c, me["mp"]].astype(F32)
        for b in range(mp - 1):
            total = total + r2[c, b].astype(F32)
        part[c] = total.astype(BF16)
        third[c] = [copy(part.at[c, :, cols(p["z"])], r3.at[c, b - 1], p) for b, p in to_z]

    def step_three(c):
        wait(third[c])
        total = part[c, :, mine].astype(F32)
        for b in range(z - 1):
            total = total + r3[c, b].astype(F32)
        sum_ref[me["core"], c, :, mine] = total.astype(BF16)
        here = sum_ref.at[me["core"], c, :, mine]
        fourth[c] = [copy(here, here, p) for b, p in to_z]

    def step_four(c):
        wait(fourth[c])
        here = sum_ref.at[me["core"], c]
        fifth[c] = copy(here, here, other)

    def flat_sum(value, got):
        for b in range(got.shape[0]):
            value = value + got[b]
        return value

    def flat_step(i):
        core, at = me["core"], total_ref.at
        if i == 0:
            wait(flat_now[0])
            f1[...] = flat_ref[core] + g1[...]
            flat_now[0] = [copy(f1.at[p["mp"]], g2.at[b - 1], p) for b, p in to_mp]
        elif i == 1:
            wait(flat_now[0])
            f2[...] = flat_sum(f1[me["mp"]], g2)
            flat_now[0] = [copy(f2.at[p["z"]], g3.at[b - 1], p) for b, p in to_z]
        elif i == 2:
            wait(flat_now[0])
            total_ref[core, me["mp"], me["z"]] = flat_sum(f2[me["z"]], g3)
            own = at[core, me["mp"], me["z"]]
            flat_now[0] = [copy(own, own, p) for b, p in to_z]
        elif i == 3:
            wait(flat_now[0])
            own = at[core, me["mp"]]
            flat_now[0] = [copy(own, own, p) for b, p in to_mp]
        elif i == 4:
            wait(flat_now[0])
            own = at[core]
            flat_now[0] = [copy(own, own, other)]

    weights = load(0, iw_any, iw)
    fetch(0)
    fetch(1)
    weights.wait()
    gain_sum, shift_sum = last_tile(0)
    for c in range(min(2, chunks)):
        step_one(c)
    done, early = 1, 4
    first_now = [None]

    def first_step(i):
        if i == 0:
            for n, value in enumerate((gain_sum, shift_sum)):
                for j in range(D // 128):
                    f0[0, n * 8 + j:n * 8 + j + 1, :] = value[:, j * 128:(j + 1) * 128]
            first_now[0] = [copy(f0.at[0], u1, other)]
        elif i == 1:
            wait(first_now[0])
            f0[1] = f0[0] + u1[...]
            first_now[0] = [copy(f0.at[1], u2.at[b - 1], p) for b, p in to_mp]
        elif i == 2:
            wait(first_now[0])
            f0[2] = flat_sum(f0[1], u2)
            first_now[0] = [copy(f0.at[2], u3.at[b - 1], p) for b, p in to_z]

    for c in range(max(chunks + 2, early + 3, 5)):
        if c < early:
            for i in range(done, min(tiles, done + -(-(tiles - 1) // early))):
                gain, shift = last_tile(i)
                gain_sum, shift_sum = gain_sum + gain, shift_sum + shift
                done = i + 1
        if c < chunks:
            wait(second[c])
            if c + 2 < chunks:
                step_one(c + 2)
            step_two(c)
        if 1 <= c <= chunks:
            step_three(c - 1)
        if 2 <= c < chunks + 2:
            step_four(c - 2)
        flat_step(c)
        if c >= early:
            first_step(c - early)
    wait(first_now[0])
    firsts_ref[...] = flat_sum(f0[2], u3)
    wait(flat_now[0] + [fifth[c] for c in range(chunks)])
    for c in range(chunks):
        for core in range(2):
            rows_ref[core, :, c * width:(c + 1) * width] = sum_ref[core, c].astype(F32)
    for c in stores:
        c.wait()
    for c in sent:
        c.wait_send()


def finish(keep, send, flat, gain, gproj, in_w, x, gres):
    mp, z = lax.axis_size("mp"), lax.axis_size("z")
    chunks, _, rows, width = keep.shape
    piece = width // z
    word = flat.shape[-1]
    copies = chunks * (2 + (mp - 1) + 2 * (z - 1)) + 3 + 3 * (mp - 1) + 3 * (z - 1)
    vm = lambda *shape: pltpu.VMEM(shape, BF16)
    vf = lambda *shape: pltpu.VMEM(shape, F32)
    spec = pl.BlockSpec(memory_space=pltpu.VMEM)
    far = pl.BlockSpec(memory_space=pl.ANY)
    fold = lambda a: a.reshape(PH, ML, D)
    out, row_sum, total, firsts = pl.pallas_call(
        functools.partial(finish_kernel, (mp, z)),
        in_specs=[spec, far, spec, spec] + [far] * 4,
        out_specs=[far] + [spec] * 3,
        out_shape=[
            jax.ShapeDtypeStruct((L, D), BF16), jax.ShapeDtypeStruct((2, rows, chunks * width), F32),
            jax.ShapeDtypeStruct(flat.shape, F32), jax.ShapeDtypeStruct((16, 128), F32),
        ],
        scratch_shapes=[
            vm(3, PH, ML, D), vm(D, 3 * D), vm(PH, ML, D), vf(PH, ML, D), vf(D // 128, ROWS, 128), vm(L, D), vf(3, 16, 128),
            vm(chunks, mp, rows, width), vm(chunks, mp, rows, width), vm(chunks, mp - 1, rows, width),
            vm(chunks, rows, width), vm(chunks, z - 1, rows, piece), vm(2, chunks, rows, width),
            vf(mp, z, 8, word), vf(mp, z, 8, word), vf(z, 8, word), vf(mp - 1, z, 8, word), vf(z - 1, 8, word),
            vf(16, 128), vf(mp - 1, 16, 128), vf(z - 1, 16, 128),
            pltpu.SemaphoreType.DMA((copies,)), pltpu.SemaphoreType.DMA((copies,)),
            pltpu.SemaphoreType.DMA((1 + 4 * (L // ROWS),)),
        ],
        compiler_params=params(collective_id=0, has_side_effects=True),
        cost_estimate=cost(2 * L * D * 3 * D, 60 << 20),
        name="finish",
    )(keep, send, flat, gain, gproj.reshape(3, PH, ML, D), in_w, fold(x), fold(gres))
    return out, row_sum.reshape(2 * rows, chunks * width), total, firsts


VECTORS = (
    ("first_gain", 1), ("first_shift", 1), ("in_bias", 3), ("short", 9), ("skip", 1), ("out_bias", 1),
    ("second_gain", 1), ("second_shift", 1), ("up_bias", 4), ("down_bias", 1),
)


def swap_bit(x, axis, bit):
    size = lax.axis_size(axis)
    return lax.ppermute(x, axis, [(i, i ^ bit) for i in range(size)])


def add_low(*parts):
    total = parts[0].astype(F32)
    for part in parts[1:]:
        total = total + part.astype(F32)
    return total.astype(BF16)


def hold(*values):
    return lax.optimization_barrier(values)


def entry(x, i):
    return lax.dynamic_index_in_dim(x, i, 0, False)


def in_order(pieces, axis):
    place = lax.axis_index(axis)
    stacked = jnp.stack(pieces)
    return jnp.concatenate([entry(stacked, place ^ i) for i in range(len(pieces))], axis=0)


def spread_steps(x, axis, add):
    place = lax.axis_index(axis)
    got = yield [(entry(x, place ^ b), axis, b) for b in range(1, x.shape[0])]
    return add(entry(x, place), *got)


def collect_steps(x, axis):
    got = yield [(x, axis, b) for b in range(1, lax.axis_size(axis))]
    return in_order([x] + list(got), axis)


def share_steps(share):
    z = lax.axis_size("z")
    rows, cols = share.shape
    mine = yield from spread_steps(share.reshape(z, rows // z, cols), "z", add_low)
    mine = yield from collect_steps(mine, "z")
    return (yield from collect_steps(mine, "core")).astype(F32)


class Chains:
    def __init__(self):
        self.live, self.done = {}, {}

    def start(self, name, steps):
        self.live[name] = (steps, next(steps))

    def move(self, names, first, kernel):
        names = [n for n in names if n in self.live]
        sends = [send for n in names for send in self.live[n][1]]
        held = hold(first, *(s[0] for s in sends))
        got = [swap_bit(v, s[1], s[2]) for v, s in zip(held[1:], sends)]
        out = kernel(held[0])
        flat, tree = jax.tree.flatten(out)
        held = hold(*flat, *got)
        out = jax.tree.unflatten(tree, held[:len(flat)])
        got = list(held[len(flat):])
        for n in names:
            steps, wanted = self.live.pop(n)
            arrived, got = got[:len(wanted)], got[len(wanted):]
            try:
                self.live[n] = (steps, steps.send(arrived))
            except StopIteration as stop:
                self.done[n] = stop.value
        return out

    def finish(self):
        while self.live:
            self.move(list(self.live), jnp.zeros((8, 128), F32), lambda v: v)


def scatter_rows(grad):
    return lax.psum_scatter(grad, ("mp", "core"), scatter_dimension=0, tiled=True)


def gather_rows(shard):
    rows = shard.shape[0]
    half = lax.dynamic_slice_in_dim(shard, lax.axis_index("core") * (rows // 2), rows // 2, 0)
    return lax.all_gather(half, ("mp", "core"), axis=0, tiled=True)


def shards(
    inputs, first_gain, first_shift, in_weight, in_bias, short_weight, skip_gain, pos_weight, pos_bias,
    mid_weight, mid_bias, filter_weight, decay_rates, out_weight, out_bias, second_gain, second_shift,
    up_weight, up_bias, down_weight, down_bias, cotangent,
):
    mp = lax.axis_size("mp")
    own = D // mp
    local = (first_gain, first_shift, in_bias, short_weight, skip_gain, out_bias, second_gain, second_shift, up_bias, down_bias)
    packed = jnp.concatenate([v.reshape(-1) for v in local]).reshape(1, -1)
    spread = lax.all_gather(packed, "mp", axis=0, tiled=True).astype(F32)
    full = {}
    at = 0
    for name, count in VECTORS:
        part = spread[:, at:at + count * own]
        at += count * own
        if name == "short":
            part = part.reshape(mp, 3, 3 * own).swapaxes(0, 1)
            full[name] = part.reshape(3, 3 * D)
        else:
            full[name] = part.reshape(1, count * D)
    in_matrix = gather_rows(in_weight)
    upout = gather_rows(jnp.concatenate([up_weight, out_weight], axis=1))
    down_matrix = gather_rows(down_weight)

    tab, itab = (jnp.asarray(t) for t in dft_tables())
    x, cot, n1 = prep(inputs, cotangent, full["first_gain"], full["first_shift"])
    places = (jnp.arange(PH)[:, None] + PH * jnp.arange(ML)[None, :]).reshape(L)
    network = (pos_weight, pos_bias, mid_weight, mid_bias, filter_weight)
    filters, filter_back = jax.vjp(lambda weights: filter_values(places, weights, decay_rates), network)
    spec = filter_spectrum(tab, filters.astype(BF16))
    proj, gate, gated, mixed, branch, sig = front(n1, in_matrix, full["in_bias"], full["short"], full["skip"], tab, itab, spec)
    res, n2, act, slope = up_stage(x, branch, upout, full["out_bias"], full["second_gain"], full["second_shift"], full["up_bias"])
    down_grad = weight_grad(act, cot, 1024, 1024, "down_weight_grad")
    act, down_grad = hold(act, down_grad)
    block_out, gh, gres, low, sums_two, up_bias_sum = down_stage(act, slope, res, cot, down_matrix, full["down_bias"], upout, full["second_gain"])
    down_share = scatter_rows(down_grad)
    chains = Chains()
    low, down_share = hold(low, down_share)
    chains.start("down", share_steps(down_share))
    up_out = chains.move(["down"], low, lambda v: up_out_grad(n2, branch, gh, v))
    low, up_out = hold(low, up_out)
    up_share = scatter_rows(up_out)
    taps3 = full["short"].reshape(3, 3, D).swapaxes(0, 1)
    core = lax.axis_index("core").astype(jnp.int32).reshape(1)
    kept = (upout, gate, proj, gated, mixed, sig, spec, taps3, full["skip"], tab, itab)
    gproj, gfilt, sums_mid = chains.move(["down"], low, lambda v: back(0, D // TILE, v, *kept))
    gproj, gfilt, up_share = hold(gproj, gfilt, up_share)
    chains.start("up", share_steps(up_share))
    keep, send = chains.move(["down", "up"], gproj, lambda v: in_weight_grad(n1, v, core, mp, 128 * lax.axis_size("z")))
    gfilt, keep = hold(gfilt, keep)
    net = filter_back(gfilt.astype(F32))[0]
    mids = sums_mid[1:13].reshape(3, 4, D)
    vectors = {
        "in_bias": mids[:, 0].reshape(3 * D), "short": mids[:, 1:].swapaxes(0, 1).reshape(3, 3 * D), "skip": sums_mid[0],
        "out_bias": sums_two[2], "second_gain": sums_two[0], "second_shift": sums_two[1], "up_bias": up_bias_sum[0],
        "down_bias": sums_two[3],
    }
    by_owner = lambda name, count: vectors[name].reshape(-1, mp, count * own).swapaxes(0, 1).reshape(mp, -1)
    middle = [(name, 3 if name == "short" else count) for name, count in VECTORS[2:]]
    flats = [jnp.concatenate([by_owner(*item) for item in middle], axis=1).reshape(-1)]
    flats += [n.reshape(-1) for n in net]
    length = sum(f.shape[0] for f in flats)
    group = (2, mp, lax.axis_size("z"), 8)
    count = math.prod(group)
    word = -(-length // (128 * count)) * 128
    flat = jnp.concatenate(flats + [jnp.zeros((count * word - length,), F32)]).reshape(group + (word,))
    kernel = lambda v: finish(v, send, flat, full["first_gain"], gproj, in_matrix, x, gres)
    input_grad, in_sum, flat_sum, firsts = chains.move(["up"], keep, kernel)
    chains.finish()
    done = chains.done
    down_sum = done["down"]
    up_sum, out_sum = done["up"][:, :FF], done["up"][:, FF:]
    me = lax.axis_index("mp")
    firsts = firsts.reshape(2, D)
    mine = {
        "first_gain": lax.dynamic_slice_in_dim(firsts[0], me * own, own, 0),
        "first_shift": lax.dynamic_slice_in_dim(firsts[1], me * own, own, 0),
    }
    flat_sum = flat_sum.reshape(-1)
    span = sum(count for _, count in VECTORS[2:]) * own
    local = lax.dynamic_slice_in_dim(flat_sum, me * span, span, 0)
    at = 0
    for name, count in VECTORS[2:]:
        mine[name] = local[at:at + count * own]
        at += count * own
    mine["short"] = mine["short"].reshape(3, 3 * own)
    at = mp * span
    pieces = []
    for n in net:
        pieces.append(flat_sum[at:at + n.size])
        at += n.size
    net_sum = [pieces[i].reshape(n.shape) for i, n in enumerate(net)]
    return (
        block_out, input_grad, mine["first_gain"], mine["first_shift"], in_sum, mine["in_bias"], mine["short"], mine["skip"],
        *net_sum, out_sum, mine["out_bias"], mine["second_gain"], mine["second_shift"], up_sum, mine["up_bias"],
        down_sum, mine["down_bias"],
    )


def solution(mesh):
    dp, mp = mesh.devices.shape
    split = jax.sharding.Mesh(mesh.devices.reshape(dp // 2, 2, mp), ("z", "core", "mp"))
    tokens = P(("z", "core", "mp"), None)
    row, vec, rep = P("mp", None), P("mp"), P()
    return jax.shard_map(
        shards,
        mesh=split,
        in_specs=(
            tokens, vec, vec, row, vec, P(None, "mp"), vec, rep, rep, rep, rep, rep, rep, row, vec, vec, vec, row, vec, row,
            vec, tokens,
        ),
        out_specs=(
            tokens, tokens, vec, vec, row, vec, P(None, "mp"), vec, rep, rep, rep, rep, rep, row, vec, vec, vec, row, vec,
            row, vec,
        ),
        check_vma=False,
    )
```

```python
import functools
import math

import jax
import jax.numpy as jnp
import numpy as np
from jax import lax
from jax.experimental import pallas as pl
from jax.experimental.pallas import tpu as pltpu
from jax.sharding import PartitionSpec as P

D = 1024
FF = 4096
BANDS = 16
L = 2048
PH = 4
ML = L // PH
TILE = 256
PAD = 8

HIGH_ACCURACY = lax.Precision.HIGHEST
eps = 1e-05
decay_floor = 0.05
F32 = jnp.float32
BF16 = jnp.bfloat16
VMEM_BYTES = 62 << 20


def dot_nn(a, b):
    return lax.dot_general(a, b, (((1,), (0,)), ((), ())), preferred_element_type=F32)


def dot_nt(a, b):
    return lax.dot_general(a, b, (((1,), (1,)), ((), ())), preferred_element_type=F32)


def dot_tn(a, b):
    return lax.dot_general(a, b, (((0,), (0,)), ((), ())), preferred_element_type=F32)


def dft_tables():
    times = PH * np.arange(ML)[None, None, :] + np.arange(PH)[:, None, None]
    odd = 2 * np.arange(ML)[None, :, None] + 1
    angle = 2.0 * np.pi / (4 * L) * ((times * odd) % (4 * L)).astype(np.float64)
    table = np.concatenate([np.cos(angle), -np.sin(angle)], axis=1)
    forward = table.reshape(PH * 2 * ML, ML).astype(jnp.bfloat16)
    backward = np.swapaxes(table, 1, 2).reshape(PH * ML, 2 * ML).astype(jnp.bfloat16)
    return forward, backward


def whole(shape):
    return pl.BlockSpec(shape, lambda *_: (0,) * len(shape), pipeline_mode=pl.Buffered(1))


def params(**kw):
    return pltpu.CompilerParams(vmem_limit_bytes=VMEM_BYTES, **kw)


def cost(flops, moved):
    return pl.CostEstimate(flops=int(flops), bytes_accessed=int(moved), transcendentals=0)


def forward_dft(tab_ref, src, dst_ref):
    for r in range(PH):
        dst_ref[pl.ds(r * 2 * ML, 2 * ML), :] = dot_nn(tab_ref[pl.ds(r * 2 * ML, 2 * ML), :], src(r)).astype(BF16)


def split_bins(part, rows):
    re = [part(r * 2 * ML + rows) for r in range(PH)]
    im = [part(r * 2 * ML + ML + rows) for r in range(PH)]
    ar, ai, br, bi = re[0] + re[2], im[0] + im[2], re[0] - re[2], im[0] - im[2]
    cr, ci, dr, di = re[1] + re[3], im[1] + im[3], re[1] - re[3], im[1] - im[3]
    return [(ar + cr, ai + ci), (br + di, bi - dr), (ar - cr, ai - ci), (br - di, bi + dr)]


def join_bins(bins, put, rows):
    (r0, i0), (r1, i1), (r2, i2), (r3, i3) = bins
    ar, ai, br, bi = r0 + r2, i0 + i2, r0 - r2, i0 - i2
    cr, ci, dr, di = r1 + r3, i1 + i3, r1 - r3, i1 - i3
    out = [(ar + cr, ai + ci), (br - di, bi + dr), (ar - cr, ai - ci), (br + di, bi - dr)]
    for r in range(PH):
        put(r * 2 * ML + rows, out[r][0])
        put(r * 2 * ML + ML + rows, out[r][1])


def phase_decay(r, rates):
    places = (PH * lax.broadcasted_iota(jnp.int32, (ML, TILE), 0) + r).astype(F32)
    return jnp.exp(-rates * places * (1.0 / L)) + decay_floor


def filter_kernel(tab_ref, second_ref, fw_ref, rates_ref, spec_ref, part_ref, filt_ref, wide_ref):
    width = second_ref.shape[1]

    @pl.when(pl.program_id(0) == 0)
    def _():
        value = second_ref[...]
        high = value.astype(BF16)
        wide_ref[:, 0:width] = high
        wide_ref[:, width:2 * width] = (value - high.astype(F32)).astype(BF16)
        wide_ref[:, 2 * width:3 * width] = high

    weight = fw_ref[...]
    high = weight.astype(BF16)
    rest = (weight - high.astype(F32)).astype(BF16)
    three = jnp.concatenate([high, high, rest], axis=0)
    rates = rates_ref[...]
    for r in range(PH):
        rows = pl.ds(r * ML, ML)
        filt_ref[rows, :] = (dot_nn(wide_ref[rows, :], three) * phase_decay(r, rates)).astype(BF16)
    forward_dft(tab_ref, lambda r: filt_ref[pl.ds(r * ML, ML), :], part_ref)
    step = 32

    @pl.loop(0, ML // step)
    def _(i):
        rows = pl.multiple_of(i * step, step)
        bins = split_bins(lambda at: part_ref[pl.ds(at, step), :], rows)
        for j in range(PH):
            spec_ref[pl.ds(j * 2 * ML + rows, step), :] = bins[j][0] * jnp.bfloat16(1.0 / L)
            spec_ref[pl.ds(j * 2 * ML + ML + rows, step), :] = bins[j][1] * jnp.bfloat16(1.0 / L)


def filter_spectrum(tab, second, filter_weight, rates):
    width = second.shape[1]
    return pl.pallas_call(
        filter_kernel,
        grid=(D // TILE,),
        in_specs=[whole((PH * 2 * ML, ML)), whole((L, width)), pl.BlockSpec((width, TILE), lambda i: (0, i)),
                  pl.BlockSpec((1, TILE), lambda i: (0, i))],
        out_specs=pl.BlockSpec((2 * L, TILE), lambda i: (0, i)),
        out_shape=jax.ShapeDtypeStruct((2 * L, D), BF16),
        scratch_shapes=[pltpu.VMEM((2 * L, TILE), BF16), pltpu.VMEM((L, TILE), BF16), pltpu.VMEM((L, 3 * width), BF16)],
        compiler_params=params(),
        cost_estimate=cost(2 * 2 * L * ML * D, 16 << 20),
        name="filter_spectrum",
    )(tab, second, filter_weight, rates)


def fetch_tables(tab_any, itab_any, tab_ref, itab_ref, sem):
    copies = [pltpu.make_async_copy(tab_any, tab_ref, sem.at[0]), pltpu.make_async_copy(itab_any, itab_ref, sem.at[1])]
    is_first = pl.program_id(0) == 0

    @pl.when(is_first)
    def _():
        for c in copies:
            c.start()

    def ready(n):
        @pl.when(is_first)
        def _():
            copies[n].wait()

    return ready


TABLES = [pltpu.VMEM((PH * 2 * ML, ML), BF16), pltpu.VMEM((PH * ML, 2 * ML), BF16), pltpu.SemaphoreType.DMA((2,))]
FAR = pl.BlockSpec(memory_space=pl.ANY)


def front_kernel(
    n1_ref, wa_ref, wb_ref, wc_ref, ba_ref, bb_ref, bc_ref, ta_ref, tb_ref, tc_ref, skip_ref,
    tab_any, itab_any, spec_ref,
    proj_ref, gate_ref, gated_ref, mixed_ref, branch_ref, sig_ref,
    sa_ref, sb_ref, sc_ref, part_ref, turn_ref, long_ref, tab_ref, itab_ref, tab_sem,
):
    ready = fetch_tables(tab_any, itab_any, tab_ref, itab_ref, tab_sem)
    scr = (sa_ref, sb_ref, sc_ref)
    for ref, w_ref, b_ref in zip(scr, (wa_ref, wb_ref, wc_ref), (ba_ref, bb_ref, bc_ref)):
        for r in range(PH):
            ref[r, pl.ds(0, PAD), :] = jnp.zeros((PAD, TILE), F32)
            ref[r, pl.ds(PAD, ML), :] = dot_nn(n1_ref[pl.ds(r * ML, ML), :], w_ref[...]) + b_ref[...]
    taps = [[t[pl.ds(j, 1), :] for j in range(3)] for t in (ta_ref, tb_ref, tc_ref)]
    step = 32

    @pl.loop(0, ML // step)
    def _(i):
        rows = pl.multiple_of(i * step, step)
        outs = []
        for n in range(3):
            ref = scr[n]
            p = [ref[r, pl.ds(PAD + rows, step), :] for r in range(PH)]
            low = [pltpu.roll(ref[r, pl.ds(rows, step + PAD), :], 1, 0)[PAD:, :] for r in (2, 3)]
            seq = low + p
            w0, w1, w2 = taps[n]
            short = [w0 * seq[r + 2] + w1 * seq[r + 1] + w2 * seq[r] for r in range(PH)]
            for r in range(PH):
                proj_ref[n, pl.ds(r * ML + rows, step), :] = p[r].astype(BF16)
                gate_ref[n, pl.ds(r * ML + rows, step), :] = short[r].astype(BF16)
            outs.append(short)
        for r in range(PH):
            gated_ref[pl.ds(r * ML + rows, step), :] = (outs[1][r] * outs[2][r]).astype(BF16)

    ready(0)
    forward_dft(tab_ref, lambda r: gated_ref[pl.ds(r * ML, ML), :], part_ref)
    step2 = 32

    @pl.loop(0, ML // step2)
    def _(i):
        rows = pl.multiple_of(i * step2, step2)
        bins = split_bins(lambda at: part_ref[pl.ds(at, step2), :], rows)
        out = []
        for j in range(PH):
            xr, xi = bins[j]
            at = j * 2 * ML + rows
            sig_ref[pl.ds(at, step2), :] = xr
            sig_ref[pl.ds(at + ML, step2), :] = xi
            hr = spec_ref[pl.ds(at, step2), :]
            hi = spec_ref[pl.ds(at + ML, step2), :]
            out.append((xr * hr - xi * hi, xr * hi + xi * hr))

        def put(at, value):
            turn_ref[pl.ds(at, step2), :] = value

        join_bins(out, put, rows)

    skip = skip_ref[...]
    ready(1)
    for r in range(PH):
        long_ref[pl.ds(r * ML, ML), :] = dot_nn(
            itab_ref[pl.ds(r * ML, ML), :], turn_ref[pl.ds(r * 2 * ML, 2 * ML), :]
        )

    @pl.loop(0, ML // step)
    def _(i):
        rows = pl.multiple_of(i * step, step)
        for r in range(PH):
            at = pl.ds(r * ML + rows, step)
            mixed = long_ref[at, :] + skip * gated_ref[at, :].astype(F32)
            mixed_ref[at, :] = mixed.astype(BF16)
            branch_ref[at, :] = (gate_ref[0, at, :].astype(F32) * mixed).astype(BF16)


def front(n1, in_w, in_b, taps, skip, tab, itab, spec):
    nt = D // TILE
    cols = lambda k: pl.BlockSpec((D, TILE), lambda i, k=k: (0, k * nt + i))
    row = lambda k, h: pl.BlockSpec((h, TILE), lambda i, k=k: (0, k * nt + i))
    out = pl.BlockSpec((L, TILE), lambda i: (0, i))
    out3 = pl.BlockSpec((3, L, TILE), lambda i: (0, 0, i))
    return pl.pallas_call(
        front_kernel,
        grid=(nt,),
        in_specs=[whole((L, D))] + [cols(k) for k in range(3)] + [row(k, 1) for k in range(3)]
        + [row(k, 3) for k in range(3)] + [row(0, 1), FAR, FAR,
           pl.BlockSpec((2 * L, TILE), lambda i: (0, i))],
        out_specs=[out3, out3, out, out, out, pl.BlockSpec((2 * L, TILE), lambda i: (0, i))],
        out_shape=[
            jax.ShapeDtypeStruct((3, L, D), BF16), jax.ShapeDtypeStruct((3, L, D), BF16),
            jax.ShapeDtypeStruct((L, D), BF16), jax.ShapeDtypeStruct((L, D), BF16),
            jax.ShapeDtypeStruct((L, D), BF16), jax.ShapeDtypeStruct((2 * L, D), BF16),
        ],
        scratch_shapes=[pltpu.VMEM((PH, PAD + ML, TILE), F32)] * 3
        + [pltpu.VMEM((2 * L, TILE), BF16), pltpu.VMEM((2 * L, TILE), BF16), pltpu.VMEM((L, TILE), F32)] + TABLES,
        compiler_params=params(),
        cost_estimate=cost(2 * L * D * 3 * D + 4 * 2 * L * ML * D, 80 << 20),
        name="front",
    )(n1, in_w, in_w, in_w, in_b, in_b, in_b, taps, taps, taps, skip, tab, itab, spec)


def gelu_parts(h):
    c = lambda v: jnp.bfloat16(v)
    h = h.astype(BF16)
    t = c(1.0) / (c(1.0) + c(0.3275911 / math.sqrt(2.0)) * jnp.abs(h))
    bell = jnp.exp(c(-0.5) * h * h)
    poly = c(0.5 * 1.061405429) * t - c(0.5 * 1.453152027)
    for k in (0.5 * 1.421413741, -0.5 * 0.284496736, 0.5 * 0.254829592):
        poly = poly * t + c(k)
    tail = poly * t * bell
    phi = jnp.where(h >= 0, c(1.0) - tail, tail)
    return h * phi, phi + h * (bell * c(1.0 / math.sqrt(2.0 * math.pi)))


def norm_stats(v):
    centre = jnp.mean(v, axis=-1, keepdims=True)
    centred = v - centre
    inv = lax.rsqrt(jnp.mean(centred * centred, axis=-1, keepdims=True) + eps)
    return centred * inv, inv


ROWS = 256
CHUNK = 512


def up_kernel(x_ref, branch_ref, ow_ref, ob_ref, g_ref, s_ref, uw_ref, ub_ref, res_ref, n2_ref, act_ref, slope_ref):
    res = x_ref[...].astype(F32) + dot_nn(branch_ref[...], ow_ref[...]) + ob_ref[...]
    res_ref[...] = res
    hat, _ = norm_stats(res)
    n2_ref[...] = (hat * g_ref[...] + s_ref[...]).astype(BF16)
    n2 = n2_ref[...]
    for c in range(FF // CHUNK):
        at = pl.ds(c * CHUNK, CHUNK)
        h = dot_nn(n2, uw_ref[:, at]) + ub_ref[:, at]
        act, slope = gelu_parts(h)
        act_ref[:, at] = act
        slope_ref[:, at] = slope


def up_part():
    return pl.BlockSpec((D, FF), lambda *_: (0, 0), pipeline_mode=pl.Buffered(1))


def out_part():
    return pl.BlockSpec((D, D), lambda *_: (0, FF // D), pipeline_mode=pl.Buffered(1))


def up_stage(x, branch, upout, ob, g, s, ub):
    rows = lambda n: pl.BlockSpec((ROWS, n), lambda i: (i, 0))
    return pl.pallas_call(
        up_kernel,
        grid=(L // ROWS,),
        in_specs=[rows(D), rows(D), out_part(), whole((1, D)), whole((1, D)), whole((1, D)), up_part(), whole((1, FF))],
        out_specs=[rows(D), rows(D), rows(FF), rows(FF)],
        out_shape=[
            jax.ShapeDtypeStruct((L, D), F32), jax.ShapeDtypeStruct((L, D), BF16),
            jax.ShapeDtypeStruct((L, FF), BF16), jax.ShapeDtypeStruct((L, FF), BF16),
        ],
        compiler_params=params(),
        cost_estimate=cost(2 * L * D * (D + FF), 60 << 20),
        name="up_stage",
    )(x, branch, upout, ob, g, s, upout, ub)


def interleave(value, mix_ref, out_ref):
    q = ROWS // PH
    for c in range(D // 128):
        lanes = slice(c * 128, (c + 1) * 128)
        for r in range(PH):
            mix_ref[c, pl.ds(r, q, stride=PH), :] = value[r * q:(r + 1) * q, lanes]
        out_ref[:, lanes] = mix_ref[c].astype(BF16)


def down_kernel(act_ref, slope_ref, res_ref, cot_ref, dw_ref, db_ref, uw_ref, g_ref, out_ref, gh_ref, gres_ref, low_ref, sums_ref, ubg_ref, mix_ref):
    i = pl.program_id(0)

    @pl.when(i == 0)
    def _():
        sums_ref[...] = jnp.zeros_like(sums_ref)
        ubg_ref[...] = jnp.zeros_like(ubg_ref)

    res = res_ref[...].reshape(ROWS, D)
    cot = cot_ref[...].reshape(ROWS, D)
    for c in range(FF // CHUNK):
        at = pl.ds(c * CHUNK, CHUNK)
        ga = dot_nt(cot, dw_ref[at, :])
        gh = (ga * slope_ref[:, :, at].reshape(ROWS, CHUNK).astype(F32)).astype(BF16)
        gh_ref[:, :, at] = gh.reshape(PH, ROWS // PH, CHUNK)
        ubg_ref[pl.ds(0, 1), at] += jnp.sum(gh.astype(F32), axis=0, keepdims=True)
    out = res + dot_nn(act_ref[...].reshape(ROWS, FF), dw_ref[...]) + db_ref[...]
    interleave(out, mix_ref, out_ref)
    gn = dot_nt(gh_ref[...].reshape(ROWS, FF), uw_ref[...])
    hat, inv = norm_stats(res)
    e = gn * g_ref[...]
    cot32 = cot.astype(F32)
    gres = cot32 + inv * (e - jnp.mean(e, axis=-1, keepdims=True) - hat * jnp.mean(e * hat, axis=-1, keepdims=True))
    low = gres.astype(BF16)
    gres_ref[...] = gres.reshape(PH, ROWS // PH, D)
    low_ref[...] = low.reshape(PH, ROWS // PH, D)
    sums_ref[pl.ds(0, 1), :] += jnp.sum(gn * hat, axis=0, keepdims=True)
    sums_ref[pl.ds(1, 1), :] += jnp.sum(gn, axis=0, keepdims=True)
    sums_ref[pl.ds(2, 1), :] += jnp.sum(low.astype(F32), axis=0, keepdims=True)
    sums_ref[pl.ds(3, 1), :] += jnp.sum(cot32, axis=0, keepdims=True)


def down_stage(act, slope, res, cot, dw, db, uw, g):
    q = ROWS // PH
    rows = lambda n: pl.BlockSpec((PH, q, n), lambda i: (0, i, 0))
    fold = lambda a: a.reshape(PH, ML, a.shape[-1])
    out, gh, gres, low, sums, ubg = pl.pallas_call(
        down_kernel,
        grid=(L // ROWS,),
        in_specs=[rows(FF), rows(FF), rows(D), rows(D), whole((FF, D)), whole((1, D)), up_part(), whole((1, D))],
        out_specs=[pl.BlockSpec((ROWS, D), lambda i: (i, 0)), rows(FF), rows(D), rows(D),
                   pl.BlockSpec((8, D), lambda i: (0, 0)), pl.BlockSpec((8, FF), lambda i: (0, 0))],
        out_shape=[
            jax.ShapeDtypeStruct((L, D), BF16), jax.ShapeDtypeStruct((PH, ML, FF), BF16),
            jax.ShapeDtypeStruct((PH, ML, D), F32), jax.ShapeDtypeStruct((PH, ML, D), BF16),
            jax.ShapeDtypeStruct((8, D), F32), jax.ShapeDtypeStruct((8, FF), F32),
        ],
        scratch_shapes=[pltpu.VMEM((D // 128, ROWS, 128), F32)],
        compiler_params=params(),
        cost_estimate=cost(2 * L * D * 3 * FF, 100 << 20),
        name="down_stage",
    )(fold(act), fold(slope), fold(res), fold(cot), dw, db, uw, g)
    return out, gh.reshape(L, FF), gres.reshape(L, D), low.reshape(L, D), sums, ubg


def grad_kernel(a_ref, b_ref, o_ref):
    o_ref[...] = dot_tn(a_ref[...], b_ref[...]).astype(o_ref.dtype)


def weight_grad(a, b, bm, bn, name):
    m, n = a.shape[1], b.shape[1]
    return pl.pallas_call(
        grad_kernel,
        grid=(m // bm, n // bn),
        in_specs=[pl.BlockSpec((L, bm), lambda i, j: (0, i)), pl.BlockSpec((L, bn), lambda i, j: (0, j))],
        out_specs=pl.BlockSpec((bm, bn), lambda i, j: (i, j)),
        out_shape=jax.ShapeDtypeStruct((m, n), BF16),
        compiler_params=params(),
        cost_estimate=cost(2 * L * m * n, 2 * (L * (m + n) + m * n)),
        name=name,
    )(a, b)


def short_back(n, step, scr, taps_ref, proj_ref, gproj_ref, sums_ref):
    ref = scr[n]
    w = [taps_ref[n, pl.ds(j, 1), :] for j in range(3)]

    def second(i, acc, ref=ref, w=w, n=n):
        rows = pl.multiple_of(i * step, step)
        seq = [ref[r, pl.ds(rows, step), :] for r in range(PH)]
        seq += [pltpu.roll(ref[r, pl.ds(rows, step + PAD), :], step + PAD - 1, 0)[:step, :] for r in range(2)]
        acc = list(acc)
        for r in range(PH):
            at = pl.ds(r * ML + rows, step)
            g = (w[0] * seq[r] + w[1] * seq[r + 1] + w[2] * seq[r + 2]).astype(BF16)
            gproj_ref[n, at, :] = g
            p = proj_ref[n, at, :].astype(F32)
            terms = (g.astype(F32), seq[r] * p, seq[r + 1] * p, seq[r + 2] * p)
            for q in range(4):
                for k in range(step // 8):
                    acc[q] = acc[q] + terms[q][k * 8:(k + 1) * 8, :]
        return tuple(acc)

    zero = jnp.zeros((8, TILE), F32)
    acc = lax.fori_loop(0, ML // step, second, (zero,) * 4)
    for q in range(4):
        sums_ref[pl.ds(1 + 4 * n + q, 1), :] = jnp.sum(acc[q], axis=0, keepdims=True)


def back_kernel(
    low_ref, ow_ref, gate_ref, proj_ref, gated_ref, mixed_ref, sig_ref, spec_ref, taps_ref, skip_ref, tab_any, itab_any,
    second_ref, fw_ref, rates_ref,
    gproj_ref, gfw_ref, gsec_ref, sums_ref,
    gb_ref, gl_ref, part_ref, turn_ref, cross_ref, long_ref, s1_ref, s2_ref, tab_ref, itab_ref, tab_sem,
):
    ready = fetch_tables(tab_any, itab_any, tab_ref, itab_ref, tab_sem)
    scr = (s1_ref, s1_ref, s2_ref)
    gb_ref[...] = dot_nt(low_ref[...], ow_ref[...])
    step = 32
    skip = skip_ref[...]

    def first(i, acc):
        rows = pl.multiple_of(i * step, step)
        for r in range(PH):
            at = pl.ds(r * ML + rows, step)
            gb = gb_ref[at, :]
            gp = gb * gate_ref[0, at, :].astype(F32)
            gl_ref[at, :] = gp.astype(BF16)
            s1_ref[r, pl.ds(rows, step), :] = gb * mixed_ref[at, :].astype(F32)
            gb_ref[at, :] = gp
            prod = gp * gated_ref[at, :].astype(F32)
            for k in range(step // 8):
                acc = acc + prod[k * 8:(k + 1) * 8, :]
        return acc

    acc = lax.fori_loop(0, ML // step, first, jnp.zeros((8, TILE), F32))
    sums_ref[pl.ds(0, 1), :] = jnp.sum(acc, axis=0, keepdims=True)
    for ref in (s1_ref, s2_ref):
        for r in range(2):
            ref[r, pl.ds(ML, PAD), :] = jnp.zeros((PAD, TILE), F32)
    short_back(0, step, scr, taps_ref, proj_ref, gproj_ref, sums_ref)
    ready(0)
    forward_dft(tab_ref, lambda r: gl_ref[pl.ds(r * ML, ML), :], part_ref)
    step2 = 32

    @pl.loop(0, ML // step2)
    def _(i):
        rows = pl.multiple_of(i * step2, step2)
        bins = split_bins(lambda at: part_ref[pl.ds(at, step2), :], rows)
        for other_ref, into_ref in ((spec_ref, turn_ref), (sig_ref, cross_ref)):
            out = []
            for j in range(PH):
                gr, gi = bins[j]
                at = j * 2 * ML + rows
                hr = other_ref[pl.ds(at, step2), :]
                hi = other_ref[pl.ds(at + ML, step2), :]
                out.append((hr * gr + hi * gi, hr * gi - hi * gr))

            def put(at, value, into_ref=into_ref):
                into_ref[pl.ds(at, step2), :] = value

            join_bins(out, put, rows)

    ready(1)
    rates = rates_ref[...]

    @pl.when(pl.program_id(0) == 0)
    def _():
        gsec_ref[...] = jnp.zeros_like(gsec_ref)

    for r in range(PH):
        rows = pl.ds(r * ML, ML)
        freq = pl.ds(r * 2 * ML, 2 * ML)
        gl_ref[rows, :] = (dot_nn(itab_ref[rows, :], cross_ref[freq, :]) * (phase_decay(r, rates) * (1.0 / L))).astype(BF16)
        long_ref[rows, :] = dot_nn(itab_ref[rows, :], turn_ref[freq, :])

    gfw_ref[...] = dot_tn(second_ref[...], gl_ref[...])
    gsec_ref[...] += dot_nt(gl_ref[...], fw_ref[...])

    @pl.loop(0, ML // step)
    def _(i):
        rows = pl.multiple_of(i * step, step)
        for r in range(PH):
            at = pl.ds(r * ML + rows, step)
            gg = long_ref[at, :] + gb_ref[at, :] * skip
            s1_ref[r, pl.ds(rows, step), :] = gg * gate_ref[2, at, :].astype(F32)
            s2_ref[r, pl.ds(rows, step), :] = gg * gate_ref[1, at, :].astype(F32)

    for n in (1, 2):
        short_back(n, step, scr, taps_ref, proj_ref, gproj_ref, sums_ref)


def back(low, upout, gate, proj, gated, mixed, sig, spec, taps3, skip, tab, itab, second, fw, rates):
    tile = lambda h: pl.BlockSpec((h, TILE), lambda i: (0, i))
    tile3 = lambda h: pl.BlockSpec((3, h, TILE), lambda i: (0, 0, i))
    once = lambda h: pl.BlockSpec((h, TILE), lambda i: (0, i), pipeline_mode=pl.Buffered(1))
    width = second.shape[1]
    return pl.pallas_call(
        back_kernel,
        grid=(D // TILE,),
        in_specs=[whole((L, D)), pl.BlockSpec((TILE, D), lambda i: (i, FF // D)), tile3(L), tile3(L), once(L), once(L),
                  tile(2 * L), tile(2 * L), tile3(3), tile(1), FAR, FAR, whole((L, width)), tile(width), tile(1)],
        out_specs=[tile3(L), tile(width), pl.BlockSpec((L, width), lambda i: (0, 0)), tile(16)],
        out_shape=[
            jax.ShapeDtypeStruct((3, L, D), BF16), jax.ShapeDtypeStruct((width, D), F32),
            jax.ShapeDtypeStruct((L, width), F32), jax.ShapeDtypeStruct((16, D), F32),
        ],
        scratch_shapes=[
            pltpu.VMEM((L, TILE), F32), pltpu.VMEM((L, TILE), BF16), pltpu.VMEM((2 * L, TILE), BF16),
            pltpu.VMEM((2 * L, TILE), BF16), pltpu.VMEM((2 * L, TILE), BF16), pltpu.VMEM((L, TILE), F32),
        ] + [pltpu.VMEM((PH, ML + PAD, TILE), F32)] * 2 + TABLES,
        compiler_params=params(),
        cost_estimate=cost(2 * L * D * D + 12 * L * ML * D, 80 << 20),
        name="back",
    )(low, upout, gate, proj, gated, mixed, sig, spec, taps3, skip, tab, itab, second, fw, rates)


def up_out_kernel(n2_ref, br_ref, gh_ref, low_ref, o_ref):
    j = pl.program_id(0)

    @pl.when(j < FF // D)
    def _():
        o_ref[...] = dot_tn(n2_ref[...], gh_ref[...]).astype(BF16)

    @pl.when(j == FF // D)
    def _():
        o_ref[...] = dot_tn(br_ref[...], low_ref[...]).astype(BF16)


def up_out_grad(n2, branch, gh, low):
    nj = FF // D
    return pl.pallas_call(
        up_out_kernel,
        grid=(nj + 1,),
        in_specs=[whole((L, D)), whole((L, D)), pl.BlockSpec((L, D), lambda j: (0, jnp.minimum(j, nj - 1))), whole((L, D))],
        out_specs=pl.BlockSpec((D, D), lambda j: (0, j)),
        out_shape=jax.ShapeDtypeStruct((D, FF + D), BF16),
        compiler_params=params(),
        cost_estimate=cost(2 * L * D * (FF + D), 40 << 20),
        name="up_out_grad",
    )(n2, branch, gh, low)


def deinterleave(src_ref, mix_ref, put):
    q = ROWS // PH
    for c in range(D // 128):
        lanes = slice(c * 128, (c + 1) * 128)
        mix_ref[c] = src_ref[:, lanes].astype(F32)
        for r in range(PH):
            put(r, lanes, mix_ref[c, pl.ds(r, q, stride=PH), :])


def prep_kernel(x_ref, cot_ref, g_ref, s_ref, xp_ref, cp_ref, n1_ref, mix_ref, flat_ref):
    q = ROWS // PH

    def put_cot(r, lanes, value):
        cp_ref[r, :, lanes] = value.astype(BF16)

    def put_x(r, lanes, value):
        xp_ref[r, :, lanes] = value.astype(BF16)
        flat_ref[pl.ds(r * q, q), lanes] = value

    deinterleave(cot_ref, mix_ref, put_cot)
    deinterleave(x_ref, mix_ref, put_x)
    hat, _ = norm_stats(flat_ref[...])
    n1_ref[...] = (hat * g_ref[...] + s_ref[...]).astype(BF16).reshape(PH, q, D)


def prep(inputs, cotangent, g, s):
    flat = pl.BlockSpec((ROWS, D), lambda i: (i, 0))
    rows = pl.BlockSpec((PH, ROWS // PH, D), lambda i: (0, i, 0))
    out = jax.ShapeDtypeStruct((PH, ML, D), BF16)
    x, cot, n1 = pl.pallas_call(
        prep_kernel,
        grid=(L // ROWS,),
        in_specs=[flat, flat, whole((1, D)), whole((1, D))],
        out_specs=[rows] * 3,
        out_shape=[out] * 3,
        scratch_shapes=[pltpu.VMEM((D // 128, ROWS, 128), F32), pltpu.VMEM((ROWS, D), F32)],
        compiler_params=params(),
        cost_estimate=cost(20 * L * D, 20 << 20),
        name="prep",
    )(inputs, cotangent, g, s)
    return x.reshape(L, D), cot.reshape(L, D), n1.reshape(L, D)


def positions_table(places):
    places = places.astype(F32)
    harmonics = jnp.arange(1, BANDS + 1).astype(F32)
    angles = 2.0 * math.pi / L * places[:, None] * harmonics[None, :]
    return places, jnp.concatenate([places[:, None] / L, jnp.cos(angles), jnp.sin(angles)], axis=1)


def network_layers(places, pos_weight, pos_bias, mid_weight, mid_bias):
    _, features = positions_table(places)
    first = jnp.dot(features, pos_weight, precision=HIGH_ACCURACY) + pos_bias
    layer = jnp.sin(first)
    second = jnp.dot(layer, mid_weight, precision=HIGH_ACCURACY) + mid_bias
    return features, layer, jnp.sin(second), jnp.cos(first), jnp.cos(second)


def network_kernel(grad_ref, feat_ref, layer_ref, slope1_ref, slope2_ref, mid_ref, gpw_ref, gpb_ref, gmw_ref, gmb_ref):
    exact = functools.partial(lax.dot_general, precision=HIGH_ACCURACY, preferred_element_type=F32)
    two = grad_ref[...] * slope2_ref[...]
    gmw_ref[...] = exact(layer_ref[...], two, (((0,), (0,)), ((), ())))
    gmb_ref[...] = jnp.sum(two, axis=0, keepdims=True)
    one = exact(two, mid_ref[...], (((1,), (1,)), ((), ()))) * slope1_ref[...]
    gpw_ref[...] = exact(feat_ref[...], one, (((0,), (0,)), ((), ())))
    gpb_ref[...] = jnp.sum(one, axis=0, keepdims=True)


def network_back(grad, layers, mid_weight):
    features, layer, _, slope1, slope2 = layers
    wide, width = features.shape[1], mid_weight.shape[0]
    shape = lambda n: jax.ShapeDtypeStruct((n, width), F32)
    return pl.pallas_call(
        network_kernel,
        out_shape=[shape(wide), shape(1), shape(width), shape(1)],
        compiler_params=params(),
        cost_estimate=cost(6 * 2 * 3 * L * width * width, 5 << 20),
        name="network_back",
    )(grad, features, layer, slope1, slope2, mid_weight)


def finish_kernel(
    sizes, flat_ref, gain_ref, n1_any, gp_any, iw_any, x_any, gres_any, out_any, rows_ref, total_ref, firsts_ref,
    n1, gp, iw, xs, gres, mix, done_ref, f0, leaving, r1, half, r2, part, r3, sum_ref, f1, g1, f2, g2, g3, u1, u2, u3, sem_s, sem_r, sem_l,
):
    mp, z = sizes
    me = {name: lax.axis_index(name) for name in ("z", "core", "mp")}
    other = {"core": 1 - me["core"]}
    to_mp = [(b, {"mp": lax.rem(me["mp"] + b, mp)}) for b in range(1, mp)]
    to_z = [(b, {"z": lax.rem(me["z"] + b, z)}) for b in range(1, z)]
    q = ROWS // PH
    tiles = L // ROWS

    def load(i, src, dst):
        out = pltpu.make_async_copy(src, dst, sem_l.at[i])
        out.start()
        return out

    chunks, _, rows, width = half.shape
    piece = width // z
    loads, stores = {}, {}

    def fetch_chunk(c):
        if c < chunks:
            at = pl.ds(c * width % D, width)
            loads["g", c] = [load(1 + c, gp_any.at[c * width // D, :, :, at], gp.at[c * width // D, :, :, at])]

    def fetch_tile(i):
        if i < tiles:
            at = pl.ds(i * q, q)
            base = 2 + chunks + 2 * i
            loads["t", i] = [load(base, x_any.at[:, at], xs.at[i % 2]), load(base + 1, gres_any.at[:, at], gres.at[i % 2])]

    def grad_chunk(c):
        for item in ([loads["n1"]] if c == 0 else []) + loads["g", c]:
            item.wait()
        fetch_chunk(c + 2)
        if c + 2 == chunks:
            loads["iw"] = load(1 + chunks, iw_any, iw)
        if c + 1 == chunks:
            fetch_tile(0)
            fetch_tile(1)
        at = c * width % D
        g = gp[c * width // D, :, :, at:at + width].reshape(L, width)
        value = dot_tn(n1[...], g).astype(BF16).reshape(mp, 2, rows, width)
        half[c] = jnp.where(me["core"] == 0, value[:, 0], value[:, 1])
        leaving[c] = jnp.where(me["core"] == 0, value[:, 1], value[:, 0])
        first[c] = copy(leaving.at[c], r1.at[c], other)

    def last_tile(i):
        at = pl.ds(i * q, q)
        for item in ([loads["iw"]] if i == 0 else []) + loads["t", i]:
            item.wait()
        both = jnp.concatenate([gp[n, :, at].reshape(ROWS, D) for n in range(3)], axis=1)
        gn = dot_nt(both, iw[...])
        hat, inv = norm_stats(xs[i % 2].reshape(ROWS, D).astype(F32))
        e = gn * gain_ref[...]
        fix = jnp.mean(e, axis=-1, keepdims=True) + hat * jnp.mean(e * hat, axis=-1, keepdims=True)
        if i >= 2:
            stores[i - 2].wait()
        interleave(gres[i % 2].reshape(ROWS, D) + inv * (e - fix), mix, done_ref.at[i % 2])
        stores[i] = load(2 + chunks + 2 * tiles + i, done_ref.at[i % 2], out_any.at[pl.ds(i * ROWS, ROWS)])
        fetch_tile(i + 2)
        return jnp.sum(gn * hat, axis=0, keepdims=True), jnp.sum(gn, axis=0, keepdims=True)

    loads["n1"] = load(0, n1_any, n1)
    fetch_chunk(0)
    fetch_chunk(1)
    barrier = pltpu.get_barrier_semaphore()
    peers = [other] + [p for _, p in to_mp] + [p for _, p in to_z]
    for peer in peers:
        pl.semaphore_signal(barrier, inc=1, device_id=peer, device_id_type=pl.DeviceIdType.MESH)
    pl.semaphore_wait(barrier, len(peers))

    count = [0]

    def copy(src, dst, peer):
        i = count[0]
        count[0] += 1
        out = pltpu.make_async_remote_copy(
            src_ref=src, dst_ref=dst, send_sem=sem_s.at[i], recv_sem=sem_r.at[i], device_id=peer,
            device_id_type=pl.DeviceIdType.MESH,
        )
        out.start()
        return out

    sent = []

    def wait(copies):
        for c in copies:
            c.wait_recv()
        sent.extend(copies)

    cols = lambda i: pl.ds(pl.multiple_of(i * piece, piece), piece)
    mine = cols(me["z"])
    first = {}
    flat_now = [[copy(flat_ref.at[1 - me["core"]], g1, other)]]
    second, third, fourth, fifth = {}, {}, {}, {}

    def step_one(c):
        wait([first[c]])
        half[c] = (half[c].astype(F32) + r1[c].astype(F32)).astype(BF16)
        second[c] = [copy(half.at[c, p["mp"]], r2.at[c, b - 1], p) for b, p in to_mp]

    def step_two(c):
        total = half[c, me["mp"]].astype(F32)
        for b in range(mp - 1):
            total = total + r2[c, b].astype(F32)
        part[c] = total.astype(BF16)
        third[c] = [copy(part.at[c, :, cols(p["z"])], r3.at[c, b - 1], p) for b, p in to_z]

    def step_three(c):
        wait(third[c])
        total = part[c, :, mine].astype(F32)
        for b in range(z - 1):
            total = total + r3[c, b].astype(F32)
        sum_ref[me["core"], c, :, mine] = total.astype(BF16)
        here = sum_ref.at[me["core"], c, :, mine]
        fourth[c] = [copy(here, here, p) for b, p in to_z]

    def step_four(c):
        wait(fourth[c])
        here = sum_ref.at[me["core"], c]
        fifth[c] = copy(here, here, other)

    def flat_sum(value, got):
        for b in range(got.shape[0]):
            value = value + got[b]
        return value

    def flat_step(i):
        core, at = me["core"], total_ref.at
        if i == 0:
            wait(flat_now[0])
            f1[...] = flat_ref[core] + g1[...]
            flat_now[0] = [copy(f1.at[p["mp"]], g2.at[b - 1], p) for b, p in to_mp]
        elif i == 1:
            wait(flat_now[0])
            f2[...] = flat_sum(f1[me["mp"]], g2)
            flat_now[0] = [copy(f2.at[p["z"]], g3.at[b - 1], p) for b, p in to_z]
        elif i == 2:
            wait(flat_now[0])
            total_ref[core, me["mp"], me["z"]] = flat_sum(f2[me["z"]], g3)
            own = at[core, me["mp"], me["z"]]
            flat_now[0] = [copy(own, own, p) for b, p in to_z]
        elif i == 3:
            wait(flat_now[0])
            own = at[core, me["mp"]]
            flat_now[0] = [copy(own, own, p) for b, p in to_mp]
        elif i == 4:
            wait(flat_now[0])
            own = at[core]
            flat_now[0] = [copy(own, own, other)]

    first_now = [None]

    def first_step(i):
        if i == 0:
            for n, value in enumerate((gain_sum, shift_sum)):
                for j in range(D // 128):
                    f0[0, n * 8 + j:n * 8 + j + 1, :] = value[:, j * 128:(j + 1) * 128]
            first_now[0] = [copy(f0.at[0], u1, other)]
        elif i == 1:
            wait(first_now[0])
            f0[1] = f0[0] + u1[...]
            first_now[0] = [copy(f0.at[1], u2.at[b - 1], p) for b, p in to_mp]
        elif i == 2:
            wait(first_now[0])
            f0[2] = flat_sum(f0[1], u2)
            first_now[0] = [copy(f0.at[2], u3.at[b - 1], p) for b, p in to_z]

    one = two = three = four = flats = 0

    def middle():
        nonlocal one, two, three, flats
        if two < one:
            wait(second[two])
            if one < min(chunks, len(first)):
                step_one(one)
                one += 1
            step_two(two)
            two += 1
        if three < two and (three < two - 1 or two == chunks):
            step_three(three)
            three += 1
        flat_step(flats)
        flats += 1

    def back_to_core():
        nonlocal four
        if four < three and (four < three - 1 or three == chunks):
            step_four(four)
            four += 1

    gain_sum = shift_sum = None
    for k in range(chunks + tiles):
        if k < chunks:
            grad_chunk(k)
        else:
            gain, shift = last_tile(k - chunks)
            gain_sum = gain if gain_sum is None else gain_sum + gain
            shift_sum = shift if shift_sum is None else shift_sum + shift
        if k >= 1 and one < min(2, chunks):
            step_one(one)
            one += 1
        elif k >= 3 and k % 2 == 1:
            middle()
        elif k >= 3:
            back_to_core()
    ends = 0
    while four < chunks or flats < 5 or ends < 3:
        first_step(ends)
        ends += 1
        middle()
        back_to_core()
    for i in (tiles - 2, tiles - 1):
        stores[i].wait()
    wait(first_now[0])
    firsts_ref[...] = flat_sum(f0[2], u3)
    wait(flat_now[0] + [fifth[c] for c in range(chunks)])
    for c in range(chunks):
        for core in range(2):
            rows_ref[core, :, c * width:(c + 1) * width] = sum_ref[core, c].astype(F32)
    for c in sent:
        c.wait_send()


def finish(flat, gain, n1, gproj, in_w, x, gres):
    mp, z = lax.axis_size("mp"), lax.axis_size("z")
    width = 128 * z
    chunks = 3 * D // width
    rows = D // (2 * mp)
    word = flat.shape[-1]
    tiles, q = L // ROWS, ROWS // PH
    copies = chunks * (2 + (mp - 1) + 2 * (z - 1)) + 3 + 3 * (mp - 1) + 3 * (z - 1)
    vm = lambda *shape: pltpu.VMEM(shape, BF16)
    vf = lambda *shape: pltpu.VMEM(shape, F32)
    spec = pl.BlockSpec(memory_space=pltpu.VMEM)
    fold = lambda a: a.reshape(PH, ML, D)
    out, row_sum, total, firsts = pl.pallas_call(
        functools.partial(finish_kernel, (mp, z)),
        in_specs=[spec] * 2 + [FAR] * 5,
        out_specs=[FAR] + [spec] * 3,
        out_shape=[
            jax.ShapeDtypeStruct((L, D), BF16), jax.ShapeDtypeStruct((2, rows, 3 * D), F32),
            jax.ShapeDtypeStruct(flat.shape, F32), jax.ShapeDtypeStruct((16, 128), F32),
        ],
        scratch_shapes=[
            vm(L, D), vm(3, PH, ML, D), vm(D, 3 * D), vm(2, PH, q, D), vf(2, PH, q, D), vf(D // 128, ROWS, 128),
            vm(2, ROWS, D), vf(3, 16, 128), vm(chunks, mp, rows, width), vm(chunks, mp, rows, width),
            vm(chunks, mp, rows, width), vm(chunks, mp - 1, rows, width), vm(chunks, rows, width),
            vm(chunks, z - 1, rows, width // z), vm(2, chunks, rows, width),
            vf(mp, z, 8, word), vf(mp, z, 8, word), vf(z, 8, word), vf(mp - 1, z, 8, word), vf(z - 1, 8, word),
            vf(16, 128), vf(mp - 1, 16, 128), vf(z - 1, 16, 128),
            pltpu.SemaphoreType.DMA((copies,)), pltpu.SemaphoreType.DMA((copies,)),
            pltpu.SemaphoreType.DMA((2 + chunks + 3 * tiles,)),
        ],
        compiler_params=params(collective_id=0, has_side_effects=True),
        cost_estimate=cost(2 * 2 * L * D * 3 * D, 60 << 20),
        name="finish",
    )(flat, gain, n1, gproj.reshape(3, PH, ML, D), in_w, fold(x), fold(gres))
    return out, row_sum.reshape(2 * rows, 3 * D), total, firsts


VECTORS = (
    ("first_gain", 1), ("first_shift", 1), ("in_bias", 3), ("short", 9), ("skip", 1), ("out_bias", 1),
    ("second_gain", 1), ("second_shift", 1), ("up_bias", 4), ("down_bias", 1),
)


def swap_bit(x, axis, bit):
    size = lax.axis_size(axis)
    return lax.ppermute(x, axis, [(i, i ^ bit) for i in range(size)])


def add_low(*parts):
    total = parts[0].astype(F32)
    for part in parts[1:]:
        total = total + part.astype(F32)
    return total.astype(BF16)


def hold(*values):
    return lax.optimization_barrier(values)


def entry(x, i):
    return lax.dynamic_index_in_dim(x, i, 0, False)


def in_order(pieces, axis):
    place = lax.axis_index(axis)
    stacked = jnp.stack(pieces)
    return jnp.concatenate([entry(stacked, place ^ i) for i in range(len(pieces))], axis=0)


def spread_steps(x, axis, add):
    place = lax.axis_index(axis)
    got = yield [(entry(x, place ^ b), axis, b) for b in range(1, x.shape[0])]
    return add(entry(x, place), *got)


def collect_steps(x, axis):
    got = yield [(x, axis, b) for b in range(1, lax.axis_size(axis))]
    return in_order([x] + list(got), axis)


def share_steps(share):
    z = lax.axis_size("z")
    rows, cols = share.shape
    mine = yield from spread_steps(share.reshape(z, rows // z, cols), "z", add_low)
    mine = yield from collect_steps(mine, "z")
    return (yield from collect_steps(mine, "core")).astype(F32)


class Chains:
    def __init__(self):
        self.live, self.done = {}, {}

    def start(self, name, steps):
        self.live[name] = (steps, next(steps))

    def move(self, names, first, kernel):
        names = [n for n in names if n in self.live]
        sends = [send for n in names for send in self.live[n][1]]
        held = hold(first, *(s[0] for s in sends))
        got = [swap_bit(v, s[1], s[2]) for v, s in zip(held[1:], sends)]
        out = kernel(held[0])
        flat, tree = jax.tree.flatten(out)
        held = hold(*flat, *got)
        out = jax.tree.unflatten(tree, held[:len(flat)])
        got = list(held[len(flat):])
        for n in names:
            steps, wanted = self.live.pop(n)
            arrived, got = got[:len(wanted)], got[len(wanted):]
            try:
                self.live[n] = (steps, steps.send(arrived))
            except StopIteration as stop:
                self.done[n] = stop.value
        return out

    def finish(self):
        while self.live:
            self.move(list(self.live), jnp.zeros((8, 128), F32), lambda v: v)


def scatter_rows(grad):
    return lax.psum_scatter(grad, ("mp", "core"), scatter_dimension=0, tiled=True)


def gather_rows(shard):
    rows = shard.shape[0]
    half = lax.dynamic_slice_in_dim(shard, lax.axis_index("core") * (rows // 2), rows // 2, 0)
    return lax.all_gather(half, ("mp", "core"), axis=0, tiled=True)


def shards(
    inputs, first_gain, first_shift, in_weight, in_bias, short_weight, skip_gain, pos_weight, pos_bias,
    mid_weight, mid_bias, filter_weight, decay_rates, out_weight, out_bias, second_gain, second_shift,
    up_weight, up_bias, down_weight, down_bias, cotangent,
):
    mp = lax.axis_size("mp")
    own = D // mp
    local = (first_gain, first_shift, in_bias, short_weight, skip_gain, out_bias, second_gain, second_shift, up_bias, down_bias)
    packed = jnp.concatenate([v.reshape(-1) for v in local]).reshape(1, -1)
    spread = in_order([packed] + [swap_bit(packed, "mp", b) for b in range(1, mp)], "mp").astype(F32)
    full = {}
    at = 0
    for name, count in VECTORS:
        part = spread[:, at:at + count * own]
        at += count * own
        if name == "short":
            part = part.reshape(mp, 3, 3 * own).swapaxes(0, 1)
            full[name] = part.reshape(3, 3 * D)
        else:
            full[name] = part.reshape(1, count * D)
    in_matrix = gather_rows(in_weight)
    upout = gather_rows(jnp.concatenate([up_weight, out_weight], axis=1))
    down_matrix = gather_rows(down_weight)

    tab, itab = (jnp.asarray(t) for t in dft_tables())
    x, cot, n1 = prep(inputs, cotangent, full["first_gain"], full["first_shift"])
    places = (jnp.arange(PH)[:, None] + PH * jnp.arange(ML)[None, :]).reshape(L)
    layers = network_layers(places, pos_weight, pos_bias, mid_weight, mid_bias)
    second = layers[2]
    rates = decay_rates.reshape(1, D)
    spec = filter_spectrum(tab, second, filter_weight, rates)
    proj, gate, gated, mixed, branch, sig = front(n1, in_matrix, full["in_bias"], full["short"], full["skip"], tab, itab, spec)
    res, n2, act, slope = up_stage(x, branch, upout, full["out_bias"], full["second_gain"], full["second_shift"], full["up_bias"])
    down_grad = weight_grad(act, cot, 1024, 1024, "down_weight_grad")
    act, down_grad = hold(act, down_grad)
    block_out, gh, gres, low, sums_two, up_bias_sum = down_stage(act, slope, res, cot, down_matrix, full["down_bias"], upout, full["second_gain"])
    down_share = scatter_rows(down_grad)
    chains = Chains()
    low, down_share = hold(low, down_share)
    chains.start("down", share_steps(down_share))
    up_out = chains.move(["down"], low, lambda v: up_out_grad(n2, branch, gh, v))
    low, up_out = hold(low, up_out)
    up_share = scatter_rows(up_out)
    taps3 = full["short"].reshape(3, 3, D).swapaxes(0, 1)
    kept = (upout, gate, proj, gated, mixed, sig, spec, taps3, full["skip"], tab, itab, second.astype(BF16), filter_weight.astype(BF16), rates)
    gproj, gfw, gsec, sums_mid = chains.move(["down"], low, lambda v: back(v, *kept))
    gproj, gsec, up_share = hold(gproj, gsec, up_share)
    chains.start("up", share_steps(up_share))
    net = tuple(chains.move(["down", "up"], gsec, lambda v: network_back(v, layers, mid_weight))) + (gfw,)
    mids = sums_mid[1:13].reshape(3, 4, D)
    vectors = {
        "in_bias": mids[:, 0].reshape(3 * D), "short": mids[:, 1:].swapaxes(0, 1).reshape(3, 3 * D), "skip": sums_mid[0],
        "out_bias": sums_two[2], "second_gain": sums_two[0], "second_shift": sums_two[1], "up_bias": up_bias_sum[0],
        "down_bias": sums_two[3],
    }
    by_owner = lambda name, count: vectors[name].reshape(-1, mp, count * own).swapaxes(0, 1).reshape(mp, -1)
    middle = [(name, 3 if name == "short" else count) for name, count in VECTORS[2:]]
    flats = [jnp.concatenate([by_owner(*item) for item in middle], axis=1).reshape(-1)]
    flats += [n.reshape(-1) for n in net]
    length = sum(f.shape[0] for f in flats)
    group = (2, mp, lax.axis_size("z"), 8)
    count = math.prod(group)
    word = -(-length // (128 * count)) * 128
    flat = jnp.concatenate(flats + [jnp.zeros((count * word - length,), F32)]).reshape(group + (word,))
    kernel = lambda v: finish(flat, full["first_gain"], n1, v, in_matrix, x, gres)
    input_grad, in_sum, flat_sum, firsts = chains.move(["up"], gproj, kernel)
    chains.finish()
    done = chains.done
    down_sum = done["down"]
    up_sum, out_sum = done["up"][:, :FF], done["up"][:, FF:]
    me = lax.axis_index("mp")
    firsts = firsts.reshape(2, D)
    mine = {
        "first_gain": lax.dynamic_slice_in_dim(firsts[0], me * own, own, 0),
        "first_shift": lax.dynamic_slice_in_dim(firsts[1], me * own, own, 0),
    }
    flat_sum = flat_sum.reshape(-1)
    span = sum(count for _, count in VECTORS[2:]) * own
    local = lax.dynamic_slice_in_dim(flat_sum, me * span, span, 0)
    at = 0
    for name, count in VECTORS[2:]:
        mine[name] = local[at:at + count * own]
        at += count * own
    mine["short"] = mine["short"].reshape(3, 3 * own)
    at = mp * span
    pieces = []
    for n in net:
        pieces.append(flat_sum[at:at + n.size])
        at += n.size
    net_sum = [p.reshape(n.shape) for p, n in zip(pieces, (pos_weight, pos_bias, mid_weight, mid_bias, filter_weight))]
    return (
        block_out, input_grad, mine["first_gain"], mine["first_shift"], in_sum, mine["in_bias"], mine["short"], mine["skip"],
        *net_sum, out_sum, mine["out_bias"], mine["second_gain"], mine["second_shift"], up_sum, mine["up_bias"],
        down_sum, mine["down_bias"],
    )


def solution(mesh):
    dp, mp = mesh.devices.shape
    split = jax.sharding.Mesh(mesh.devices.reshape(dp // 2, 2, mp), ("z", "core", "mp"))
    tokens = P(("z", "core", "mp"), None)
    row, vec, rep = P("mp", None), P("mp"), P()
    return jax.shard_map(
        shards,
        mesh=split,
        in_specs=(
            tokens, vec, vec, row, vec, P(None, "mp"), vec, rep, rep, rep, rep, rep, rep, row, vec, vec, vec, row, vec, row,
            vec, tokens,
        ),
        out_specs=(
            tokens, tokens, vec, vec, row, vec, P(None, "mp"), vec, rep, rep, rep, rep, rep, row, vec, vec, vec, row, vec,
            row, vec,
        ),
        check_vma=False,
    )
```

```python
import functools
import math

import jax
import jax.numpy as jnp
import numpy as np
from jax import lax
from jax.experimental import pallas as pl
from jax.experimental.pallas import tpu as pltpu
from jax.sharding import PartitionSpec as P

D = 1024
FF = 4096
BANDS = 16
L = 2048
PH = 4
ML = L // PH
TILE = 256
PAD = 8

HIGH_ACCURACY = lax.Precision.HIGHEST
eps = 1e-05
decay_floor = 0.05
F32 = jnp.float32
BF16 = jnp.bfloat16
VMEM_BYTES = 62 << 20


def dot_nn(a, b):
    return lax.dot_general(a, b, (((1,), (0,)), ((), ())), preferred_element_type=F32)


def dot_nt(a, b):
    return lax.dot_general(a, b, (((1,), (1,)), ((), ())), preferred_element_type=F32)


def dot_tn(a, b):
    return lax.dot_general(a, b, (((0,), (0,)), ((), ())), preferred_element_type=F32)


def dft_tables():
    times = PH * np.arange(ML)[None, None, :] + np.arange(PH)[:, None, None]
    odd = 2 * np.arange(ML)[None, :, None] + 1
    angle = 2.0 * np.pi / (4 * L) * ((times * odd) % (4 * L)).astype(np.float64)
    table = np.concatenate([np.cos(angle), -np.sin(angle)], axis=1)
    forward = table.reshape(PH * 2 * ML, ML).astype(jnp.bfloat16)
    backward = np.swapaxes(table, 1, 2).reshape(PH * ML, 2 * ML).astype(jnp.bfloat16)
    return forward, backward


def whole(shape):
    return pl.BlockSpec(shape, lambda *_: (0,) * len(shape), pipeline_mode=pl.Buffered(1))


def params(**kw):
    return pltpu.CompilerParams(vmem_limit_bytes=VMEM_BYTES, **kw)


def cost(flops, moved):
    return pl.CostEstimate(flops=int(flops), bytes_accessed=int(moved), transcendentals=0)


def forward_dft(tab_ref, src, dst_ref):
    for r in range(PH):
        dst_ref[pl.ds(r * 2 * ML, 2 * ML), :] = dot_nn(tab_ref[pl.ds(r * 2 * ML, 2 * ML), :], src(r)).astype(BF16)


def split_bins(part, rows):
    re = [part(r * 2 * ML + rows) for r in range(PH)]
    im = [part(r * 2 * ML + ML + rows) for r in range(PH)]
    ar, ai, br, bi = re[0] + re[2], im[0] + im[2], re[0] - re[2], im[0] - im[2]
    cr, ci, dr, di = re[1] + re[3], im[1] + im[3], re[1] - re[3], im[1] - im[3]
    return [(ar + cr, ai + ci), (br + di, bi - dr), (ar - cr, ai - ci), (br - di, bi + dr)]


def join_bins(bins, put, rows):
    (r0, i0), (r1, i1), (r2, i2), (r3, i3) = bins
    ar, ai, br, bi = r0 + r2, i0 + i2, r0 - r2, i0 - i2
    cr, ci, dr, di = r1 + r3, i1 + i3, r1 - r3, i1 - i3
    out = [(ar + cr, ai + ci), (br - di, bi + dr), (ar - cr, ai - ci), (br + di, bi - dr)]
    for r in range(PH):
        put(r * 2 * ML + rows, out[r][0])
        put(r * 2 * ML + ML + rows, out[r][1])


def phase_decay(r, rates):
    places = (PH * lax.broadcasted_iota(jnp.int32, (ML, TILE), 0) + r).astype(F32)
    return jnp.exp(-rates * places * (1.0 / L)) + decay_floor


def filter_kernel(tab_ref, second_ref, fw_ref, rates_ref, spec_ref, part_ref, filt_ref, wide_ref):
    width = second_ref.shape[1]

    @pl.when(pl.program_id(0) == 0)
    def _():
        value = second_ref[...]
        high = value.astype(BF16)
        wide_ref[:, 0:width] = high
        wide_ref[:, width:2 * width] = (value - high.astype(F32)).astype(BF16)
        wide_ref[:, 2 * width:3 * width] = high

    weight = fw_ref[...]
    high = weight.astype(BF16)
    rest = (weight - high.astype(F32)).astype(BF16)
    three = jnp.concatenate([high, high, rest], axis=0)
    rates = rates_ref[...]
    for r in range(PH):
        rows = pl.ds(r * ML, ML)
        filt_ref[rows, :] = (dot_nn(wide_ref[rows, :], three) * phase_decay(r, rates)).astype(BF16)
    forward_dft(tab_ref, lambda r: filt_ref[pl.ds(r * ML, ML), :], part_ref)
    step = 32

    @pl.loop(0, ML // step)
    def _(i):
        rows = pl.multiple_of(i * step, step)
        bins = split_bins(lambda at: part_ref[pl.ds(at, step), :], rows)
        for j in range(PH):
            spec_ref[pl.ds(j * 2 * ML + rows, step), :] = bins[j][0] * jnp.bfloat16(1.0 / L)
            spec_ref[pl.ds(j * 2 * ML + ML + rows, step), :] = bins[j][1] * jnp.bfloat16(1.0 / L)


def filter_spectrum(tab, second, filter_weight, rates):
    width = second.shape[1]
    return pl.pallas_call(
        filter_kernel,
        grid=(D // TILE,),
        in_specs=[whole((PH * 2 * ML, ML)), whole((L, width)), pl.BlockSpec((width, TILE), lambda i: (0, i)),
                  pl.BlockSpec((1, TILE), lambda i: (0, i))],
        out_specs=pl.BlockSpec((2 * L, TILE), lambda i: (0, i)),
        out_shape=jax.ShapeDtypeStruct((2 * L, D), BF16),
        scratch_shapes=[pltpu.VMEM((2 * L, TILE), BF16), pltpu.VMEM((L, TILE), BF16), pltpu.VMEM((L, 3 * width), BF16)],
        compiler_params=params(),
        cost_estimate=cost(2 * 2 * L * ML * D, 16 << 20),
        name="filter_spectrum",
    )(tab, second, filter_weight, rates)


def fetch_tables(tab_any, itab_any, tab_ref, itab_ref, sem):
    copies = [pltpu.make_async_copy(tab_any, tab_ref, sem.at[0]), pltpu.make_async_copy(itab_any, itab_ref, sem.at[1])]
    is_first = pl.program_id(0) == 0

    @pl.when(is_first)
    def _():
        for c in copies:
            c.start()

    def ready(n):
        @pl.when(is_first)
        def _():
            copies[n].wait()

    return ready


TABLES = [pltpu.VMEM((PH * 2 * ML, ML), BF16), pltpu.VMEM((PH * ML, 2 * ML), BF16), pltpu.SemaphoreType.DMA((2,))]
FAR = pl.BlockSpec(memory_space=pl.ANY)


def front_kernel(
    n1_ref, wa_ref, wb_ref, wc_ref, ba_ref, bb_ref, bc_ref, ta_ref, tb_ref, tc_ref, skip_ref,
    tab_any, itab_any, spec_ref,
    proj_ref, gate_ref, gated_ref, mixed_ref, branch_ref, sig_ref,
    sa_ref, sb_ref, sc_ref, part_ref, turn_ref, long_ref, tab_ref, itab_ref, tab_sem,
):
    ready = fetch_tables(tab_any, itab_any, tab_ref, itab_ref, tab_sem)
    scr = (sa_ref, sb_ref, sc_ref)
    for ref, w_ref, b_ref in zip(scr, (wa_ref, wb_ref, wc_ref), (ba_ref, bb_ref, bc_ref)):
        for r in range(PH):
            ref[r, pl.ds(0, PAD), :] = jnp.zeros((PAD, TILE), F32)
            ref[r, pl.ds(PAD, ML), :] = dot_nn(n1_ref[pl.ds(r * ML, ML), :], w_ref[...]) + b_ref[...]
    taps = [[t[pl.ds(j, 1), :] for j in range(3)] for t in (ta_ref, tb_ref, tc_ref)]
    step = 32

    @pl.loop(0, ML // step)
    def _(i):
        rows = pl.multiple_of(i * step, step)
        outs = []
        for n in range(3):
            ref = scr[n]
            p = [ref[r, pl.ds(PAD + rows, step), :] for r in range(PH)]
            low = [pltpu.roll(ref[r, pl.ds(rows, step + PAD), :], 1, 0)[PAD:, :] for r in (2, 3)]
            seq = low + p
            w0, w1, w2 = taps[n]
            short = [w0 * seq[r + 2] + w1 * seq[r + 1] + w2 * seq[r] for r in range(PH)]
            for r in range(PH):
                proj_ref[n, pl.ds(r * ML + rows, step), :] = p[r].astype(BF16)
                gate_ref[n, pl.ds(r * ML + rows, step), :] = short[r].astype(BF16)
            outs.append(short)
        for r in range(PH):
            gated_ref[pl.ds(r * ML + rows, step), :] = (outs[1][r] * outs[2][r]).astype(BF16)

    ready(0)
    forward_dft(tab_ref, lambda r: gated_ref[pl.ds(r * ML, ML), :], part_ref)
    step2 = 32

    @pl.loop(0, ML // step2)
    def _(i):
        rows = pl.multiple_of(i * step2, step2)
        bins = split_bins(lambda at: part_ref[pl.ds(at, step2), :], rows)
        out = []
        for j in range(PH):
            xr, xi = bins[j]
            at = j * 2 * ML + rows
            sig_ref[pl.ds(at, step2), :] = xr
            sig_ref[pl.ds(at + ML, step2), :] = xi
            hr = spec_ref[pl.ds(at, step2), :]
            hi = spec_ref[pl.ds(at + ML, step2), :]
            out.append((xr * hr - xi * hi, xr * hi + xi * hr))

        def put(at, value):
            turn_ref[pl.ds(at, step2), :] = value

        join_bins(out, put, rows)

    skip = skip_ref[...]
    ready(1)
    for r in range(PH):
        long_ref[pl.ds(r * ML, ML), :] = dot_nn(
            itab_ref[pl.ds(r * ML, ML), :], turn_ref[pl.ds(r * 2 * ML, 2 * ML), :]
        )

    @pl.loop(0, ML // step)
    def _(i):
        rows = pl.multiple_of(i * step, step)
        for r in range(PH):
            at = pl.ds(r * ML + rows, step)
            mixed = long_ref[at, :] + skip * gated_ref[at, :].astype(F32)
            mixed_ref[at, :] = mixed.astype(BF16)
            branch_ref[at, :] = (gate_ref[0, at, :].astype(F32) * mixed).astype(BF16)


def front(n1, in_w, in_b, taps, skip, tab, itab, spec):
    nt = D // TILE
    cols = lambda k: pl.BlockSpec((D, TILE), lambda i, k=k: (0, k * nt + i))
    row = lambda k, h: pl.BlockSpec((h, TILE), lambda i, k=k: (0, k * nt + i))
    out = pl.BlockSpec((L, TILE), lambda i: (0, i))
    out3 = pl.BlockSpec((3, L, TILE), lambda i: (0, 0, i))
    return pl.pallas_call(
        front_kernel,
        grid=(nt,),
        in_specs=[whole((L, D))] + [cols(k) for k in range(3)] + [row(k, 1) for k in range(3)]
        + [row(k, 3) for k in range(3)] + [row(0, 1), FAR, FAR,
           pl.BlockSpec((2 * L, TILE), lambda i: (0, i))],
        out_specs=[out3, out3, out, out, out, pl.BlockSpec((2 * L, TILE), lambda i: (0, i))],
        out_shape=[
            jax.ShapeDtypeStruct((3, L, D), BF16), jax.ShapeDtypeStruct((3, L, D), BF16),
            jax.ShapeDtypeStruct((L, D), BF16), jax.ShapeDtypeStruct((L, D), BF16),
            jax.ShapeDtypeStruct((L, D), BF16), jax.ShapeDtypeStruct((2 * L, D), BF16),
        ],
        scratch_shapes=[pltpu.VMEM((PH, PAD + ML, TILE), F32)] * 3
        + [pltpu.VMEM((2 * L, TILE), BF16), pltpu.VMEM((2 * L, TILE), BF16), pltpu.VMEM((L, TILE), F32)] + TABLES,
        compiler_params=params(),
        cost_estimate=cost(2 * L * D * 3 * D + 4 * 2 * L * ML * D, 80 << 20),
        name="front",
    )(n1, in_w, in_w, in_w, in_b, in_b, in_b, taps, taps, taps, skip, tab, itab, spec)


def gelu_parts(h):
    c = lambda v: jnp.bfloat16(v)
    h = h.astype(BF16)
    t = c(1.0) / (c(1.0) + c(0.3275911 / math.sqrt(2.0)) * jnp.abs(h))
    bell = jnp.exp(c(-0.5) * h * h)
    poly = c(0.5 * 1.061405429) * t - c(0.5 * 1.453152027)
    for k in (0.5 * 1.421413741, -0.5 * 0.284496736, 0.5 * 0.254829592):
        poly = poly * t + c(k)
    tail = poly * t * bell
    phi = jnp.where(h >= 0, c(1.0) - tail, tail)
    return h * phi, phi + h * (bell * c(1.0 / math.sqrt(2.0 * math.pi)))


def norm_stats(v):
    centre = jnp.mean(v, axis=-1, keepdims=True)
    centred = v - centre
    inv = lax.rsqrt(jnp.mean(centred * centred, axis=-1, keepdims=True) + eps)
    return centred * inv, inv


ROWS = 256
CHUNK = 512


def up_kernel(x_ref, branch_ref, ow_ref, ob_ref, g_ref, s_ref, uw_ref, ub_ref, res_ref, n2_ref, act_ref, slope_ref):
    res = x_ref[...].astype(F32) + dot_nn(branch_ref[...], ow_ref[...]) + ob_ref[...]
    res_ref[...] = res
    hat, _ = norm_stats(res)
    n2_ref[...] = (hat * g_ref[...] + s_ref[...]).astype(BF16)
    n2 = n2_ref[...]
    for c in range(FF // CHUNK):
        at = pl.ds(c * CHUNK, CHUNK)
        h = dot_nn(n2, uw_ref[:, at]) + ub_ref[:, at]
        act, slope = gelu_parts(h)
        act_ref[:, at] = act
        slope_ref[:, at] = slope


def up_part():
    return pl.BlockSpec((D, FF), lambda *_: (0, 0), pipeline_mode=pl.Buffered(1))


def out_part():
    return pl.BlockSpec((D, D), lambda *_: (0, FF // D), pipeline_mode=pl.Buffered(1))


def up_stage(x, branch, upout, ob, g, s, ub):
    rows = lambda n: pl.BlockSpec((2 * ROWS, n), lambda i: (i, 0))
    return pl.pallas_call(
        up_kernel,
        grid=(L // (2 * ROWS),),
        in_specs=[rows(D), rows(D), out_part(), whole((1, D)), whole((1, D)), whole((1, D)), up_part(), whole((1, FF))],
        out_specs=[rows(D), rows(D), rows(FF), rows(FF)],
        out_shape=[
            jax.ShapeDtypeStruct((L, D), F32), jax.ShapeDtypeStruct((L, D), BF16),
            jax.ShapeDtypeStruct((L, FF), BF16), jax.ShapeDtypeStruct((L, FF), BF16),
        ],
        compiler_params=params(),
        cost_estimate=cost(2 * L * D * (D + FF), 60 << 20),
        name="up_stage",
    )(x, branch, upout, ob, g, s, upout, ub)


def interleave(value, mix_ref, out_ref):
    q = ROWS // PH
    for c in range(D // 128):
        lanes = slice(c * 128, (c + 1) * 128)
        for r in range(PH):
            mix_ref[c, pl.ds(r, q, stride=PH), :] = value[r * q:(r + 1) * q, lanes]
        out_ref[:, lanes] = mix_ref[c].astype(BF16)


def down_kernel(act_ref, slope_ref, res_ref, cot_ref, dw_ref, db_ref, uw_ref, g_ref, out_ref, gh_ref, gres_ref, low_ref, sums_ref, ubg_ref, mix_ref):
    i = pl.program_id(0)

    @pl.when(i == 0)
    def _():
        sums_ref[...] = jnp.zeros_like(sums_ref)
        ubg_ref[...] = jnp.zeros_like(ubg_ref)

    res = res_ref[...].reshape(ROWS, D)
    cot = cot_ref[...].reshape(ROWS, D)
    for c in range(FF // CHUNK):
        at = pl.ds(c * CHUNK, CHUNK)
        ga = dot_nt(cot, dw_ref[at, :])
        gh = (ga * slope_ref[:, :, at].reshape(ROWS, CHUNK).astype(F32)).astype(BF16)
        gh_ref[:, :, at] = gh.reshape(PH, ROWS // PH, CHUNK)
        ubg_ref[pl.ds(0, 1), at] += jnp.sum(gh.astype(F32), axis=0, keepdims=True)
    out = res + dot_nn(act_ref[...].reshape(ROWS, FF), dw_ref[...]) + db_ref[...]
    interleave(out, mix_ref, out_ref)
    gn = dot_nt(gh_ref[...].reshape(ROWS, FF), uw_ref[...])
    hat, inv = norm_stats(res)
    e = gn * g_ref[...]
    cot32 = cot.astype(F32)
    gres = cot32 + inv * (e - jnp.mean(e, axis=-1, keepdims=True) - hat * jnp.mean(e * hat, axis=-1, keepdims=True))
    low = gres.astype(BF16)
    gres_ref[...] = gres.reshape(PH, ROWS // PH, D)
    low_ref[...] = low.reshape(PH, ROWS // PH, D)
    sums_ref[pl.ds(0, 1), :] += jnp.sum(gn * hat, axis=0, keepdims=True)
    sums_ref[pl.ds(1, 1), :] += jnp.sum(gn, axis=0, keepdims=True)
    sums_ref[pl.ds(2, 1), :] += jnp.sum(low.astype(F32), axis=0, keepdims=True)
    sums_ref[pl.ds(3, 1), :] += jnp.sum(cot32, axis=0, keepdims=True)


def down_stage(act, slope, res, cot, dw, db, uw, g):
    q = ROWS // PH
    rows = lambda n: pl.BlockSpec((PH, q, n), lambda i: (0, i, 0))
    fold = lambda a: a.reshape(PH, ML, a.shape[-1])
    out, gh, gres, low, sums, ubg = pl.pallas_call(
        down_kernel,
        grid=(L // ROWS,),
        in_specs=[rows(FF), rows(FF), rows(D), rows(D), whole((FF, D)), whole((1, D)), up_part(), whole((1, D))],
        out_specs=[pl.BlockSpec((ROWS, D), lambda i: (i, 0)), rows(FF), rows(D), rows(D),
                   pl.BlockSpec((8, D), lambda i: (0, 0)), pl.BlockSpec((8, FF), lambda i: (0, 0))],
        out_shape=[
            jax.ShapeDtypeStruct((L, D), BF16), jax.ShapeDtypeStruct((PH, ML, FF), BF16),
            jax.ShapeDtypeStruct((PH, ML, D), F32), jax.ShapeDtypeStruct((PH, ML, D), BF16),
            jax.ShapeDtypeStruct((8, D), F32), jax.ShapeDtypeStruct((8, FF), F32),
        ],
        scratch_shapes=[pltpu.VMEM((D // 128, ROWS, 128), F32)],
        compiler_params=params(),
        cost_estimate=cost(2 * L * D * 3 * FF, 100 << 20),
        name="down_stage",
    )(fold(act), fold(slope), fold(res), fold(cot), dw, db, uw, g)
    return out, gh.reshape(L, FF), gres.reshape(L, D), low.reshape(L, D), sums, ubg


def grad_kernel(a_ref, b_ref, o_ref):
    o_ref[...] = dot_tn(a_ref[...], b_ref[...]).astype(o_ref.dtype)


def weight_grad(a, b, bm, bn, name):
    m, n = a.shape[1], b.shape[1]
    return pl.pallas_call(
        grad_kernel,
        grid=(m // bm, n // bn),
        in_specs=[pl.BlockSpec((L, bm), lambda i, j: (0, i)), pl.BlockSpec((L, bn), lambda i, j: (0, j))],
        out_specs=pl.BlockSpec((bm, bn), lambda i, j: (i, j)),
        out_shape=jax.ShapeDtypeStruct((m, n), BF16),
        compiler_params=params(),
        cost_estimate=cost(2 * L * m * n, 2 * (L * (m + n) + m * n)),
        name=name,
    )(a, b)


def short_back(n, step, scr, taps_ref, proj_ref, gproj_ref, sums_ref):
    ref = scr[n]
    w = [taps_ref[n, pl.ds(j, 1), :] for j in range(3)]

    def second(i, acc, ref=ref, w=w, n=n):
        rows = pl.multiple_of(i * step, step)
        seq = [ref[r, pl.ds(rows, step), :] for r in range(PH)]
        seq += [pltpu.roll(ref[r, pl.ds(rows, step + PAD), :], step + PAD - 1, 0)[:step, :] for r in range(2)]
        acc = list(acc)
        for r in range(PH):
            at = pl.ds(r * ML + rows, step)
            g = (w[0] * seq[r] + w[1] * seq[r + 1] + w[2] * seq[r + 2]).astype(BF16)
            gproj_ref[n, at, :] = g
            p = proj_ref[n, at, :].astype(F32)
            terms = (g.astype(F32), seq[r] * p, seq[r + 1] * p, seq[r + 2] * p)
            for q in range(4):
                for k in range(step // 8):
                    acc[q] = acc[q] + terms[q][k * 8:(k + 1) * 8, :]
        return tuple(acc)

    zero = jnp.zeros((8, TILE), F32)
    acc = lax.fori_loop(0, ML // step, second, (zero,) * 4)
    for q in range(4):
        sums_ref[pl.ds(1 + 4 * n + q, 1), :] = jnp.sum(acc[q], axis=0, keepdims=True)


def back_kernel(
    low_ref, ow_ref, gate_ref, proj_ref, gated_ref, mixed_ref, sig_ref, spec_ref, taps_ref, skip_ref, tab_any, itab_any,
    second_ref, fw_ref, rates_ref,
    gproj_ref, gfw_ref, gsec_ref, sums_ref,
    gb_ref, gl_ref, part_ref, turn_ref, cross_ref, long_ref, s1_ref, s2_ref, tab_ref, itab_ref, tab_sem,
):
    ready = fetch_tables(tab_any, itab_any, tab_ref, itab_ref, tab_sem)
    scr = (s1_ref, s1_ref, s2_ref)
    gb_ref[...] = dot_nt(low_ref[...], ow_ref[...])
    step = 32
    skip = skip_ref[...]

    def first(i, acc):
        rows = pl.multiple_of(i * step, step)
        for r in range(PH):
            at = pl.ds(r * ML + rows, step)
            gb = gb_ref[at, :]
            gp = gb * gate_ref[0, at, :].astype(F32)
            gl_ref[at, :] = gp.astype(BF16)
            s1_ref[r, pl.ds(rows, step), :] = gb * mixed_ref[at, :].astype(F32)
            gb_ref[at, :] = gp
            prod = gp * gated_ref[at, :].astype(F32)
            for k in range(step // 8):
                acc = acc + prod[k * 8:(k + 1) * 8, :]
        return acc

    acc = lax.fori_loop(0, ML // step, first, jnp.zeros((8, TILE), F32))
    sums_ref[pl.ds(0, 1), :] = jnp.sum(acc, axis=0, keepdims=True)
    for ref in (s1_ref, s2_ref):
        for r in range(2):
            ref[r, pl.ds(ML, PAD), :] = jnp.zeros((PAD, TILE), F32)
    short_back(0, step, scr, taps_ref, proj_ref, gproj_ref, sums_ref)
    ready(0)
    forward_dft(tab_ref, lambda r: gl_ref[pl.ds(r * ML, ML), :], part_ref)
    step2 = 32

    @pl.loop(0, ML // step2)
    def _(i):
        rows = pl.multiple_of(i * step2, step2)
        bins = split_bins(lambda at: part_ref[pl.ds(at, step2), :], rows)
        for other_ref, into_ref in ((spec_ref, turn_ref), (sig_ref, cross_ref)):
            out = []
            for j in range(PH):
                gr, gi = bins[j]
                at = j * 2 * ML + rows
                hr = other_ref[pl.ds(at, step2), :]
                hi = other_ref[pl.ds(at + ML, step2), :]
                out.append((hr * gr + hi * gi, hr * gi - hi * gr))

            def put(at, value, into_ref=into_ref):
                into_ref[pl.ds(at, step2), :] = value

            join_bins(out, put, rows)

    ready(1)
    rates = rates_ref[...]

    @pl.when(pl.program_id(0) == 0)
    def _():
        gsec_ref[...] = jnp.zeros_like(gsec_ref)

    for r in range(PH):
        rows = pl.ds(r * ML, ML)
        freq = pl.ds(r * 2 * ML, 2 * ML)
        gl_ref[rows, :] = (dot_nn(itab_ref[rows, :], cross_ref[freq, :]) * (phase_decay(r, rates) * (1.0 / L))).astype(BF16)
        long_ref[rows, :] = dot_nn(itab_ref[rows, :], turn_ref[freq, :])

    gfw_ref[...] = dot_tn(second_ref[...], gl_ref[...])
    gsec_ref[...] += dot_nt(gl_ref[...], fw_ref[...])

    @pl.loop(0, ML // step)
    def _(i):
        rows = pl.multiple_of(i * step, step)
        for r in range(PH):
            at = pl.ds(r * ML + rows, step)
            gg = long_ref[at, :] + gb_ref[at, :] * skip
            s1_ref[r, pl.ds(rows, step), :] = gg * gate_ref[2, at, :].astype(F32)
            s2_ref[r, pl.ds(rows, step), :] = gg * gate_ref[1, at, :].astype(F32)

    for n in (1, 2):
        short_back(n, step, scr, taps_ref, proj_ref, gproj_ref, sums_ref)


def back(low, upout, gate, proj, gated, mixed, sig, spec, taps3, skip, tab, itab, second, fw, rates):
    tile = lambda h: pl.BlockSpec((h, TILE), lambda i: (0, i))
    tile3 = lambda h: pl.BlockSpec((3, h, TILE), lambda i: (0, 0, i))
    once = lambda h: pl.BlockSpec((h, TILE), lambda i: (0, i), pipeline_mode=pl.Buffered(1))
    width = second.shape[1]
    return pl.pallas_call(
        back_kernel,
        grid=(D // TILE,),
        in_specs=[whole((L, D)), pl.BlockSpec((TILE, D), lambda i: (i, FF // D)), tile3(L), tile3(L), once(L), once(L),
                  tile(2 * L), tile(2 * L), tile3(3), tile(1), FAR, FAR, whole((L, width)), tile(width), tile(1)],
        out_specs=[tile3(L), tile(width), pl.BlockSpec((L, width), lambda i: (0, 0)), tile(16)],
        out_shape=[
            jax.ShapeDtypeStruct((3, L, D), BF16), jax.ShapeDtypeStruct((width, D), F32),
            jax.ShapeDtypeStruct((L, width), F32), jax.ShapeDtypeStruct((16, D), F32),
        ],
        scratch_shapes=[
            pltpu.VMEM((L, TILE), F32), pltpu.VMEM((L, TILE), BF16), pltpu.VMEM((2 * L, TILE), BF16),
            pltpu.VMEM((2 * L, TILE), BF16), pltpu.VMEM((2 * L, TILE), BF16), pltpu.VMEM((L, TILE), F32),
        ] + [pltpu.VMEM((PH, ML + PAD, TILE), F32)] * 2 + TABLES,
        compiler_params=params(),
        cost_estimate=cost(2 * L * D * D + 12 * L * ML * D, 80 << 20),
        name="back",
    )(low, upout, gate, proj, gated, mixed, sig, spec, taps3, skip, tab, itab, second, fw, rates)


def up_out_kernel(n2_ref, br_ref, gh_ref, low_ref, o_ref):
    j = pl.program_id(0)

    @pl.when(j < FF // D)
    def _():
        o_ref[...] = dot_tn(n2_ref[...], gh_ref[...]).astype(BF16)

    @pl.when(j == FF // D)
    def _():
        o_ref[...] = dot_tn(br_ref[...], low_ref[...]).astype(BF16)


def up_out_grad(n2, branch, gh, low):
    nj = FF // D
    return pl.pallas_call(
        up_out_kernel,
        grid=(nj + 1,),
        in_specs=[whole((L, D)), whole((L, D)), pl.BlockSpec((L, D), lambda j: (0, jnp.minimum(j, nj - 1))), whole((L, D))],
        out_specs=pl.BlockSpec((D, D), lambda j: (0, j)),
        out_shape=jax.ShapeDtypeStruct((D, FF + D), BF16),
        compiler_params=params(),
        cost_estimate=cost(2 * L * D * (FF + D), 40 << 20),
        name="up_out_grad",
    )(n2, branch, gh, low)


def deinterleave(src_ref, mix_ref, put):
    q = ROWS // PH
    for c in range(D // 128):
        lanes = slice(c * 128, (c + 1) * 128)
        mix_ref[c] = src_ref[:, lanes].astype(F32)
        for r in range(PH):
            put(r, lanes, mix_ref[c, pl.ds(r, q, stride=PH), :])


def prep_kernel(x_ref, cot_ref, g_ref, s_ref, xp_ref, cp_ref, n1_ref, mix_ref, flat_ref):
    q = ROWS // PH

    def put_cot(r, lanes, value):
        cp_ref[r, :, lanes] = value.astype(BF16)

    def put_x(r, lanes, value):
        xp_ref[r, :, lanes] = value.astype(BF16)
        flat_ref[pl.ds(r * q, q), lanes] = value

    deinterleave(cot_ref, mix_ref, put_cot)
    deinterleave(x_ref, mix_ref, put_x)
    hat, _ = norm_stats(flat_ref[...])
    n1_ref[...] = (hat * g_ref[...] + s_ref[...]).astype(BF16).reshape(PH, q, D)


def prep(inputs, cotangent, g, s):
    flat = pl.BlockSpec((ROWS, D), lambda i: (i, 0))
    rows = pl.BlockSpec((PH, ROWS // PH, D), lambda i: (0, i, 0))
    out = jax.ShapeDtypeStruct((PH, ML, D), BF16)
    x, cot, n1 = pl.pallas_call(
        prep_kernel,
        grid=(L // ROWS,),
        in_specs=[flat, flat, whole((1, D)), whole((1, D))],
        out_specs=[rows] * 3,
        out_shape=[out] * 3,
        scratch_shapes=[pltpu.VMEM((D // 128, ROWS, 128), F32), pltpu.VMEM((ROWS, D), F32)],
        compiler_params=params(),
        cost_estimate=cost(20 * L * D, 20 << 20),
        name="prep",
    )(inputs, cotangent, g, s)
    return x.reshape(L, D), cot.reshape(L, D), n1.reshape(L, D)


def positions_table(places):
    places = places.astype(F32)
    harmonics = jnp.arange(1, BANDS + 1).astype(F32)
    angles = 2.0 * math.pi / L * places[:, None] * harmonics[None, :]
    return places, jnp.concatenate([places[:, None] / L, jnp.cos(angles), jnp.sin(angles)], axis=1)


def network_layers(places, pos_weight, pos_bias, mid_weight, mid_bias):
    _, features = positions_table(places)
    first = jnp.dot(features, pos_weight, precision=HIGH_ACCURACY) + pos_bias
    layer = jnp.sin(first)
    second = jnp.dot(layer, mid_weight, precision=HIGH_ACCURACY) + mid_bias
    return features, layer, jnp.sin(second), jnp.cos(first), jnp.cos(second)


def network_kernel(grad_ref, feat_ref, layer_ref, slope1_ref, slope2_ref, mid_ref, gpw_ref, gpb_ref, gmw_ref, gmb_ref):
    exact = functools.partial(lax.dot_general, precision=HIGH_ACCURACY, preferred_element_type=F32)
    two = grad_ref[...] * slope2_ref[...]
    gmw_ref[...] = exact(layer_ref[...], two, (((0,), (0,)), ((), ())))
    gmb_ref[...] = jnp.sum(two, axis=0, keepdims=True)
    one = exact(two, mid_ref[...], (((1,), (1,)), ((), ()))) * slope1_ref[...]
    gpw_ref[...] = exact(feat_ref[...], one, (((0,), (0,)), ((), ())))
    gpb_ref[...] = jnp.sum(one, axis=0, keepdims=True)


def network_back(grad, layers, mid_weight):
    features, layer, _, slope1, slope2 = layers
    wide, width = features.shape[1], mid_weight.shape[0]
    shape = lambda n: jax.ShapeDtypeStruct((n, width), F32)
    return pl.pallas_call(
        network_kernel,
        out_shape=[shape(wide), shape(1), shape(width), shape(1)],
        compiler_params=params(),
        cost_estimate=cost(6 * 2 * 3 * L * width * width, 5 << 20),
        name="network_back",
    )(grad, features, layer, slope1, slope2, mid_weight)


def finish_kernel(
    sizes, flat_ref, gain_ref, n1_any, gp_any, iw_any, x_any, gres_any, out_any, rows_ref, total_ref, firsts_ref,
    n1, gp, iw, xs, gres, mix, done_ref, f0, leaving, r1, half, r2, part, r3, sum_ref, f1, g1, f2, g2, g3, u1, u2, u3, sem_s, sem_r, sem_l,
):
    mp, z = sizes
    me = {name: lax.axis_index(name) for name in ("z", "core", "mp")}
    other = {"core": 1 - me["core"]}
    to_mp = [(b, {"mp": lax.rem(me["mp"] + b, mp)}) for b in range(1, mp)]
    to_z = [(b, {"z": lax.rem(me["z"] + b, z)}) for b in range(1, z)]
    q = ROWS // PH
    tiles = L // ROWS

    def load(i, src, dst):
        out = pltpu.make_async_copy(src, dst, sem_l.at[i])
        out.start()
        return out

    chunks, _, rows, width = half.shape
    piece = width // z
    loads, stores = {}, {}

    def fetch_chunk(c):
        if c < chunks:
            at = pl.ds(c * width % D, width)
            loads["g", c] = [load(1 + c, gp_any.at[c * width // D, :, :, at], gp.at[c * width // D, :, :, at])]

    def fetch_tile(i):
        if i < tiles:
            at = pl.ds(i * q, q)
            base = 2 + chunks + 2 * i
            loads["t", i] = [load(base, x_any.at[:, at], xs.at[i % 2]), load(base + 1, gres_any.at[:, at], gres.at[i % 2])]

    def grad_chunk(c):
        for item in ([loads["n1"]] if c == 0 else []) + loads["g", c]:
            item.wait()
        fetch_chunk(c + 2)
        if c + 2 == chunks:
            loads["iw"] = load(1 + chunks, iw_any, iw)
        if c + 1 == chunks:
            fetch_tile(0)
            fetch_tile(1)
        at = c * width % D
        g = gp[c * width // D, :, :, at:at + width].reshape(L, width)
        value = dot_tn(n1[...], g).astype(BF16).reshape(mp, 2, rows, width)
        half[c] = jnp.where(me["core"] == 0, value[:, 0], value[:, 1])
        leaving[c] = jnp.where(me["core"] == 0, value[:, 1], value[:, 0])
        first[c] = copy(leaving.at[c], r1.at[c], other)

    def last_tile(i):
        at = pl.ds(i * q, q)
        for item in ([loads["iw"]] if i == 0 else []) + loads["t", i]:
            item.wait()
        both = jnp.concatenate([gp[n, :, at].reshape(ROWS, D) for n in range(3)], axis=1)
        gn = dot_nt(both, iw[...])
        hat, inv = norm_stats(xs[i % 2].reshape(ROWS, D).astype(F32))
        e = gn * gain_ref[...]
        fix = jnp.mean(e, axis=-1, keepdims=True) + hat * jnp.mean(e * hat, axis=-1, keepdims=True)
        if i >= 2:
            stores[i - 2].wait()
        interleave(gres[i % 2].reshape(ROWS, D) + inv * (e - fix), mix, done_ref.at[i % 2])
        stores[i] = load(2 + chunks + 2 * tiles + i, done_ref.at[i % 2], out_any.at[pl.ds(i * ROWS, ROWS)])
        fetch_tile(i + 2)
        return jnp.sum(gn * hat, axis=0, keepdims=True), jnp.sum(gn, axis=0, keepdims=True)

    loads["n1"] = load(0, n1_any, n1)
    fetch_chunk(0)
    fetch_chunk(1)
    barrier = pltpu.get_barrier_semaphore()
    peers = [other] + [p for _, p in to_mp] + [p for _, p in to_z]
    for peer in peers:
        pl.semaphore_signal(barrier, inc=1, device_id=peer, device_id_type=pl.DeviceIdType.MESH)
    pl.semaphore_wait(barrier, len(peers))

    count = [0]

    def copy(src, dst, peer):
        i = count[0]
        count[0] += 1
        out = pltpu.make_async_remote_copy(
            src_ref=src, dst_ref=dst, send_sem=sem_s.at[i], recv_sem=sem_r.at[i], device_id=peer,
            device_id_type=pl.DeviceIdType.MESH,
        )
        out.start()
        return out

    sent = []

    def wait(copies):
        for c in copies:
            c.wait_recv()
        sent.extend(copies)

    cols = lambda i: pl.ds(pl.multiple_of(i * piece, piece), piece)
    mine = cols(me["z"])
    first = {}
    flat_now = [[copy(flat_ref.at[1 - me["core"]], g1, other)]]
    second, third, fourth, fifth = {}, {}, {}, {}

    def step_one(c):
        wait([first[c]])
        half[c] = (half[c].astype(F32) + r1[c].astype(F32)).astype(BF16)
        second[c] = [copy(half.at[c, p["mp"]], r2.at[c, b - 1], p) for b, p in to_mp]

    def step_two(c):
        total = half[c, me["mp"]].astype(F32)
        for b in range(mp - 1):
            total = total + r2[c, b].astype(F32)
        part[c] = total.astype(BF16)
        third[c] = [copy(part.at[c, :, cols(p["z"])], r3.at[c, b - 1], p) for b, p in to_z]

    def step_three(c):
        wait(third[c])
        total = part[c, :, mine].astype(F32)
        for b in range(z - 1):
            total = total + r3[c, b].astype(F32)
        sum_ref[me["core"], c, :, mine] = total.astype(BF16)
        here = sum_ref.at[me["core"], c, :, mine]
        fourth[c] = [copy(here, here, p) for b, p in to_z]

    def step_four(c):
        wait(fourth[c])
        here = sum_ref.at[me["core"], c]
        fifth[c] = copy(here, here, other)

    def flat_sum(value, got):
        for b in range(got.shape[0]):
            value = value + got[b]
        return value

    def flat_step(i):
        core, at = me["core"], total_ref.at
        if i == 0:
            wait(flat_now[0])
            f1[...] = flat_ref[core] + g1[...]
            flat_now[0] = [copy(f1.at[p["mp"]], g2.at[b - 1], p) for b, p in to_mp]
        elif i == 1:
            wait(flat_now[0])
            f2[...] = flat_sum(f1[me["mp"]], g2)
            flat_now[0] = [copy(f2.at[p["z"]], g3.at[b - 1], p) for b, p in to_z]
        elif i == 2:
            wait(flat_now[0])
            total_ref[core, me["mp"], me["z"]] = flat_sum(f2[me["z"]], g3)
            own = at[core, me["mp"], me["z"]]
            flat_now[0] = [copy(own, own, p) for b, p in to_z]
        elif i == 3:
            wait(flat_now[0])
            own = at[core, me["mp"]]
            flat_now[0] = [copy(own, own, p) for b, p in to_mp]
        elif i == 4:
            wait(flat_now[0])
            own = at[core]
            flat_now[0] = [copy(own, own, other)]

    first_now = [None]

    def first_step(i):
        if i == 0:
            for n, value in enumerate((gain_sum, shift_sum)):
                for j in range(D // 128):
                    f0[0, n * 8 + j:n * 8 + j + 1, :] = value[:, j * 128:(j + 1) * 128]
            first_now[0] = [copy(f0.at[0], u1, other)]
        elif i == 1:
            wait(first_now[0])
            f0[1] = f0[0] + u1[...]
            first_now[0] = [copy(f0.at[1], u2.at[b - 1], p) for b, p in to_mp]
        elif i == 2:
            wait(first_now[0])
            f0[2] = flat_sum(f0[1], u2)
            first_now[0] = [copy(f0.at[2], u3.at[b - 1], p) for b, p in to_z]

    one = two = three = four = flats = 0

    def middle():
        nonlocal one, two, three, flats
        if two < one:
            wait(second[two])
            if one < min(chunks, len(first)):
                step_one(one)
                one += 1
            step_two(two)
            two += 1
        if three < two and (three < two - 1 or two == chunks):
            step_three(three)
            three += 1
        flat_step(flats)
        flats += 1

    def back_to_core():
        nonlocal four
        if four < three and (four < three - 1 or three == chunks):
            step_four(four)
            four += 1

    gain_sum = shift_sum = None
    for k in range(chunks + tiles):
        if k < chunks:
            grad_chunk(k)
        else:
            gain, shift = last_tile(k - chunks)
            gain_sum = gain if gain_sum is None else gain_sum + gain
            shift_sum = shift if shift_sum is None else shift_sum + shift
        if k >= 1 and one < min(2, chunks):
            step_one(one)
            one += 1
        elif k >= 3 and k % 2 == 1:
            middle()
        elif k >= 3:
            back_to_core()
    ends = 0
    while four < chunks or flats < 5 or ends < 3:
        first_step(ends)
        ends += 1
        middle()
        back_to_core()
    for i in (tiles - 2, tiles - 1):
        stores[i].wait()
    wait(first_now[0])
    firsts_ref[...] = flat_sum(f0[2], u3)
    wait(flat_now[0] + [fifth[c] for c in range(chunks)])
    for c in range(chunks):
        for core in range(2):
            rows_ref[core, :, c * width:(c + 1) * width] = sum_ref[core, c].astype(F32)
    for c in sent:
        c.wait_send()


def finish(flat, gain, n1, gproj, in_w, x, gres):
    mp, z = lax.axis_size("mp"), lax.axis_size("z")
    width = 128 * z
    chunks = 3 * D // width
    rows = D // (2 * mp)
    word = flat.shape[-1]
    tiles, q = L // ROWS, ROWS // PH
    copies = chunks * (2 + (mp - 1) + 2 * (z - 1)) + 3 + 3 * (mp - 1) + 3 * (z - 1)
    vm = lambda *shape: pltpu.VMEM(shape, BF16)
    vf = lambda *shape: pltpu.VMEM(shape, F32)
    spec = pl.BlockSpec(memory_space=pltpu.VMEM)
    fold = lambda a: a.reshape(PH, ML, D)
    out, row_sum, total, firsts = pl.pallas_call(
        functools.partial(finish_kernel, (mp, z)),
        in_specs=[spec] * 2 + [FAR] * 5,
        out_specs=[FAR] + [spec] * 3,
        out_shape=[
            jax.ShapeDtypeStruct((L, D), BF16), jax.ShapeDtypeStruct((2, rows, 3 * D), F32),
            jax.ShapeDtypeStruct(flat.shape, F32), jax.ShapeDtypeStruct((16, 128), F32),
        ],
        scratch_shapes=[
            vm(L, D), vm(3, PH, ML, D), vm(D, 3 * D), vm(2, PH, q, D), vf(2, PH, q, D), vf(D // 128, ROWS, 128),
            vm(2, ROWS, D), vf(3, 16, 128), vm(chunks, mp, rows, width), vm(chunks, mp, rows, width),
            vm(chunks, mp, rows, width), vm(chunks, mp - 1, rows, width), vm(chunks, rows, width),
            vm(chunks, z - 1, rows, width // z), vm(2, chunks, rows, width),
            vf(mp, z, 8, word), vf(mp, z, 8, word), vf(z, 8, word), vf(mp - 1, z, 8, word), vf(z - 1, 8, word),
            vf(16, 128), vf(mp - 1, 16, 128), vf(z - 1, 16, 128),
            pltpu.SemaphoreType.DMA((copies,)), pltpu.SemaphoreType.DMA((copies,)),
            pltpu.SemaphoreType.DMA((2 + chunks + 3 * tiles,)),
        ],
        compiler_params=params(collective_id=0, has_side_effects=True),
        cost_estimate=cost(2 * 2 * L * D * 3 * D, 60 << 20),
        name="finish",
    )(flat, gain, n1, gproj.reshape(3, PH, ML, D), in_w, fold(x), fold(gres))
    return out, row_sum.reshape(2 * rows, 3 * D), total, firsts


VECTORS = (
    ("first_gain", 1), ("first_shift", 1), ("in_bias", 3), ("short", 9), ("skip", 1), ("out_bias", 1),
    ("second_gain", 1), ("second_shift", 1), ("up_bias", 4), ("down_bias", 1),
)


def swap_bit(x, axis, bit):
    size = lax.axis_size(axis)
    return lax.ppermute(x, axis, [(i, i ^ bit) for i in range(size)])


def add_low(*parts):
    total = parts[0].astype(F32)
    for part in parts[1:]:
        total = total + part.astype(F32)
    return total.astype(BF16)


def hold(*values):
    return lax.optimization_barrier(values)


def entry(x, i):
    return lax.dynamic_index_in_dim(x, i, 0, False)


def in_order(pieces, axis):
    place = lax.axis_index(axis)
    stacked = jnp.stack(pieces)
    return jnp.concatenate([entry(stacked, place ^ i) for i in range(len(pieces))], axis=0)


def spread_steps(x, axis, add):
    place = lax.axis_index(axis)
    got = yield [(entry(x, place ^ b), axis, b) for b in range(1, x.shape[0])]
    return add(entry(x, place), *got)


def collect_steps(x, axis):
    got = yield [(x, axis, b) for b in range(1, lax.axis_size(axis))]
    return in_order([x] + list(got), axis)


def both_cores(mine, other):
    core = lax.axis_index("core")
    low = jnp.where(core == 0, mine, other)
    high = jnp.where(core == 0, other, mine)
    return jnp.concatenate([low, high], axis=0).astype(F32)


def share_steps(share):
    z = lax.axis_size("z")
    rows, cols = share.shape
    mine = yield from spread_steps(share.reshape(z, rows // z, cols), "z", add_low)
    mine = yield from collect_steps(mine, "z")
    return (yield from collect_steps(mine, "core")).astype(F32)


class Chains:
    def __init__(self):
        self.live, self.done = {}, {}

    def start(self, name, steps):
        self.live[name] = (steps, next(steps))

    def move(self, names, first, kernel):
        names = [n for n in names if n in self.live]
        sends = [send for n in names for send in self.live[n][1]]
        held = hold(first, *(s[0] for s in sends))
        got = [swap_bit(v, s[1], s[2]) for v, s in zip(held[1:], sends)]
        out = kernel(held[0])
        flat, tree = jax.tree.flatten(out)
        held = hold(*flat, *got)
        out = jax.tree.unflatten(tree, held[:len(flat)])
        got = list(held[len(flat):])
        for n in names:
            steps, wanted = self.live.pop(n)
            arrived, got = got[:len(wanted)], got[len(wanted):]
            try:
                self.live[n] = (steps, steps.send(arrived))
            except StopIteration as stop:
                self.done[n] = stop.value
        return out

    def finish(self):
        while self.live:
            self.move(list(self.live), jnp.zeros((8, 128), F32), lambda v: v)


def scatter_rows(grad):
    return lax.psum_scatter(grad, ("mp", "core"), scatter_dimension=0, tiled=True)


def gather_rows(shard):
    rows = shard.shape[0]
    half = lax.dynamic_slice_in_dim(shard, lax.axis_index("core") * (rows // 2), rows // 2, 0)
    return lax.all_gather(half, ("mp", "core"), axis=0, tiled=True)


def shards(
    inputs, first_gain, first_shift, in_weight, in_bias, short_weight, skip_gain, pos_weight, pos_bias,
    mid_weight, mid_bias, filter_weight, decay_rates, out_weight, out_bias, second_gain, second_shift,
    up_weight, up_bias, down_weight, down_bias, cotangent,
):
    mp = lax.axis_size("mp")
    own = D // mp
    local = (first_gain, first_shift, in_bias, short_weight, skip_gain, out_bias, second_gain, second_shift, up_bias, down_bias)
    packed = jnp.concatenate([v.reshape(-1) for v in local]).reshape(1, -1)
    spread = in_order([packed] + [swap_bit(packed, "mp", b) for b in range(1, mp)], "mp").astype(F32)
    full = {}
    at = 0
    for name, count in VECTORS:
        part = spread[:, at:at + count * own]
        at += count * own
        if name == "short":
            part = part.reshape(mp, 3, 3 * own).swapaxes(0, 1)
            full[name] = part.reshape(3, 3 * D)
        else:
            full[name] = part.reshape(1, count * D)
    in_matrix = gather_rows(in_weight)
    upout = gather_rows(jnp.concatenate([up_weight, out_weight], axis=1))
    down_matrix = gather_rows(down_weight)

    tab, itab = (jnp.asarray(t) for t in dft_tables())
    x, cot, n1 = prep(inputs, cotangent, full["first_gain"], full["first_shift"])
    places = (jnp.arange(PH)[:, None] + PH * jnp.arange(ML)[None, :]).reshape(L)
    layers = network_layers(places, pos_weight, pos_bias, mid_weight, mid_bias)
    second = layers[2]
    rates = decay_rates.reshape(1, D)
    spec = filter_spectrum(tab, second, filter_weight, rates)
    proj, gate, gated, mixed, branch, sig = front(n1, in_matrix, full["in_bias"], full["short"], full["skip"], tab, itab, spec)
    res, n2, act, slope = up_stage(x, branch, upout, full["out_bias"], full["second_gain"], full["second_shift"], full["up_bias"])
    down_grad = weight_grad(act, cot, 1024, 1024, "down_weight_grad")
    act, down_grad = hold(act, down_grad)
    block_out, gh, gres, low, sums_two, up_bias_sum = down_stage(act, slope, res, cot, down_matrix, full["down_bias"], upout, full["second_gain"])
    down_share = scatter_rows(down_grad)
    chains = Chains()
    low, down_share = hold(low, down_share)
    chains.start("down", share_steps(down_share))
    up_out = chains.move(["down"], low, lambda v: up_out_grad(n2, branch, gh, v))
    low, up_out = hold(low, up_out)
    up_share = scatter_rows(up_out)
    taps3 = full["short"].reshape(3, 3, D).swapaxes(0, 1)
    kept = (upout, gate, proj, gated, mixed, sig, spec, taps3, full["skip"], tab, itab, second.astype(BF16), filter_weight.astype(BF16), rates)
    gproj, gfw, gsec, sums_mid = chains.move(["down"], low, lambda v: back(v, *kept))
    gproj, gsec, up_share = hold(gproj, gsec, up_share)
    up_half = lax.psum(up_share, "z")
    net = tuple(chains.move(["down"], gsec, lambda v: network_back(v, layers, mid_weight))) + (gfw,)
    mids = sums_mid[1:13].reshape(3, 4, D)
    vectors = {
        "in_bias": mids[:, 0].reshape(3 * D), "short": mids[:, 1:].swapaxes(0, 1).reshape(3, 3 * D), "skip": sums_mid[0],
        "out_bias": sums_two[2], "second_gain": sums_two[0], "second_shift": sums_two[1], "up_bias": up_bias_sum[0],
        "down_bias": sums_two[3],
    }
    by_owner = lambda name, count: vectors[name].reshape(-1, mp, count * own).swapaxes(0, 1).reshape(mp, -1)
    middle = [(name, 3 if name == "short" else count) for name, count in VECTORS[2:]]
    flats = [jnp.concatenate([by_owner(*item) for item in middle], axis=1).reshape(-1)]
    flats += [n.reshape(-1) for n in net]
    length = sum(f.shape[0] for f in flats)
    group = (2, mp, lax.axis_size("z"), 8)
    count = math.prod(group)
    word = -(-length // (128 * count)) * 128
    flat = jnp.concatenate(flats + [jnp.zeros((count * word - length,), F32)]).reshape(group + (word,))
    kernel = lambda v: finish(flat, full["first_gain"], n1, v, in_matrix, x, gres)
    input_grad, in_sum, flat_sum, firsts = kernel(gproj)
    in_sum, up_half = hold(in_sum, up_half)
    up_both = both_cores(up_half, swap_bit(up_half, "core", 1))
    done = chains.done
    down_sum = done["down"]
    up_sum, out_sum = up_both[:, :FF], up_both[:, FF:]
    me = lax.axis_index("mp")
    firsts = firsts.reshape(2, D)
    mine = {
        "first_gain": lax.dynamic_slice_in_dim(firsts[0], me * own, own, 0),
        "first_shift": lax.dynamic_slice_in_dim(firsts[1], me * own, own, 0),
    }
    flat_sum = flat_sum.reshape(-1)
    span = sum(count for _, count in VECTORS[2:]) * own
    local = lax.dynamic_slice_in_dim(flat_sum, me * span, span, 0)
    at = 0
    for name, count in VECTORS[2:]:
        mine[name] = local[at:at + count * own]
        at += count * own
    mine["short"] = mine["short"].reshape(3, 3 * own)
    at = mp * span
    pieces = []
    for n in net:
        pieces.append(flat_sum[at:at + n.size])
        at += n.size
    net_sum = [p.reshape(n.shape) for p, n in zip(pieces, (pos_weight, pos_bias, mid_weight, mid_bias, filter_weight))]
    return (
        block_out, input_grad, mine["first_gain"], mine["first_shift"], in_sum, mine["in_bias"], mine["short"], mine["skip"],
        *net_sum, out_sum, mine["out_bias"], mine["second_gain"], mine["second_shift"], up_sum, mine["up_bias"],
        down_sum, mine["down_bias"],
    )


def solution(mesh):
    dp, mp = mesh.devices.shape
    split = jax.sharding.Mesh(mesh.devices.reshape(dp // 2, 2, mp), ("z", "core", "mp"))
    tokens = P(("z", "core", "mp"), None)
    row, vec, rep = P("mp", None), P("mp"), P()
    return jax.shard_map(
        shards,
        mesh=split,
        in_specs=(
            tokens, vec, vec, row, vec, P(None, "mp"), vec, rep, rep, rep, rep, rep, rep, row, vec, vec, vec, row, vec, row,
            vec, tokens,
        ),
        out_specs=(
            tokens, tokens, vec, vec, row, vec, P(None, "mp"), vec, rep, rep, rep, rep, rep, row, vec, vec, vec, row, vec,
            row, vec,
        ),
        check_vma=False,
    )
```

```python
import functools
import math

import jax
import jax.numpy as jnp
import numpy as np
from jax import lax
from jax.experimental import pallas as pl
from jax.experimental.pallas import tpu as pltpu
from jax.sharding import PartitionSpec as P

D = 1024
FF = 4096
BANDS = 16
L = 2048
PH = 4
ML = L // PH
TILE = 256
PAD = 8

HIGH_ACCURACY = lax.Precision.HIGHEST
eps = 1e-05
decay_floor = 0.05
F32 = jnp.float32
BF16 = jnp.bfloat16
VMEM_BYTES = 62 << 20


def dot_nn(a, b):
    return lax.dot_general(a, b, (((1,), (0,)), ((), ())), preferred_element_type=F32)


def dot_nt(a, b):
    return lax.dot_general(a, b, (((1,), (1,)), ((), ())), preferred_element_type=F32)


def dot_tn(a, b):
    return lax.dot_general(a, b, (((0,), (0,)), ((), ())), preferred_element_type=F32)


def dft_tables():
    times = PH * np.arange(ML)[None, None, :] + np.arange(PH)[:, None, None]
    odd = 2 * np.arange(ML)[None, :, None] + 1
    angle = 2.0 * np.pi / (4 * L) * ((times * odd) % (4 * L)).astype(np.float64)
    table = np.concatenate([np.cos(angle), -np.sin(angle)], axis=1)
    forward = table.reshape(PH * 2 * ML, ML).astype(jnp.bfloat16)
    backward = np.swapaxes(table, 1, 2).reshape(PH * ML, 2 * ML).astype(jnp.bfloat16)
    return forward, backward


def whole(shape):
    return pl.BlockSpec(shape, lambda *_: (0,) * len(shape), pipeline_mode=pl.Buffered(1))


def params(**kw):
    return pltpu.CompilerParams(vmem_limit_bytes=VMEM_BYTES, **kw)


def cost(flops, moved):
    return pl.CostEstimate(flops=int(flops), bytes_accessed=int(moved), transcendentals=0)


def forward_dft(tab_ref, src, dst_ref):
    for r in range(PH):
        dst_ref[pl.ds(r * 2 * ML, 2 * ML), :] = dot_nn(tab_ref[pl.ds(r * 2 * ML, 2 * ML), :], src(r)).astype(BF16)


def split_bins(part, rows):
    re = [part(r * 2 * ML + rows) for r in range(PH)]
    im = [part(r * 2 * ML + ML + rows) for r in range(PH)]
    ar, ai, br, bi = re[0] + re[2], im[0] + im[2], re[0] - re[2], im[0] - im[2]
    cr, ci, dr, di = re[1] + re[3], im[1] + im[3], re[1] - re[3], im[1] - im[3]
    return [(ar + cr, ai + ci), (br + di, bi - dr), (ar - cr, ai - ci), (br - di, bi + dr)]


def join_bins(bins, put, rows):
    (r0, i0), (r1, i1), (r2, i2), (r3, i3) = bins
    ar, ai, br, bi = r0 + r2, i0 + i2, r0 - r2, i0 - i2
    cr, ci, dr, di = r1 + r3, i1 + i3, r1 - r3, i1 - i3
    out = [(ar + cr, ai + ci), (br - di, bi + dr), (ar - cr, ai - ci), (br + di, bi - dr)]
    for r in range(PH):
        put(r * 2 * ML + rows, out[r][0])
        put(r * 2 * ML + ML + rows, out[r][1])


def phase_decay(r, rates):
    places = (PH * lax.broadcasted_iota(jnp.int32, (ML, TILE), 0) + r).astype(F32)
    return jnp.exp(-rates * places * (1.0 / L)) + decay_floor


def filter_kernel(tab_ref, second_ref, fw_ref, rates_ref, spec_ref, part_ref, filt_ref, wide_ref):
    width = second_ref.shape[1]

    @pl.when(pl.program_id(0) == 0)
    def _():
        value = second_ref[...]
        high = value.astype(BF16)
        wide_ref[:, 0:width] = high
        wide_ref[:, width:2 * width] = (value - high.astype(F32)).astype(BF16)
        wide_ref[:, 2 * width:3 * width] = high

    weight = fw_ref[...]
    high = weight.astype(BF16)
    rest = (weight - high.astype(F32)).astype(BF16)
    three = jnp.concatenate([high, high, rest], axis=0)
    rates = rates_ref[...]
    for r in range(PH):
        rows = pl.ds(r * ML, ML)
        filt_ref[rows, :] = (dot_nn(wide_ref[rows, :], three) * phase_decay(r, rates)).astype(BF16)
    forward_dft(tab_ref, lambda r: filt_ref[pl.ds(r * ML, ML), :], part_ref)
    step = 32

    @pl.loop(0, ML // step)
    def _(i):
        rows = pl.multiple_of(i * step, step)
        bins = split_bins(lambda at: part_ref[pl.ds(at, step), :], rows)
        for j in range(PH):
            spec_ref[pl.ds(j * 2 * ML + rows, step), :] = bins[j][0] * jnp.bfloat16(1.0 / L)
            spec_ref[pl.ds(j * 2 * ML + ML + rows, step), :] = bins[j][1] * jnp.bfloat16(1.0 / L)


def filter_spectrum(tab, second, filter_weight, rates):
    width = second.shape[1]
    return pl.pallas_call(
        filter_kernel,
        grid=(D // TILE,),
        in_specs=[whole((PH * 2 * ML, ML)), whole((L, width)), pl.BlockSpec((width, TILE), lambda i: (0, i)),
                  pl.BlockSpec((1, TILE), lambda i: (0, i))],
        out_specs=pl.BlockSpec((2 * L, TILE), lambda i: (0, i)),
        out_shape=jax.ShapeDtypeStruct((2 * L, D), BF16),
        scratch_shapes=[pltpu.VMEM((2 * L, TILE), BF16), pltpu.VMEM((L, TILE), BF16), pltpu.VMEM((L, 3 * width), BF16)],
        compiler_params=params(),
        cost_estimate=cost(2 * 2 * L * ML * D, 16 << 20),
        name="filter_spectrum",
    )(tab, second, filter_weight, rates)


def fetch_tables(tab_any, itab_any, tab_ref, itab_ref, sem):
    copies = [pltpu.make_async_copy(tab_any, tab_ref, sem.at[0]), pltpu.make_async_copy(itab_any, itab_ref, sem.at[1])]
    is_first = pl.program_id(0) == 0

    @pl.when(is_first)
    def _():
        for c in copies:
            c.start()

    def ready(n):
        @pl.when(is_first)
        def _():
            copies[n].wait()

    return ready


TABLES = [pltpu.VMEM((PH * 2 * ML, ML), BF16), pltpu.VMEM((PH * ML, 2 * ML), BF16), pltpu.SemaphoreType.DMA((2,))]
FAR = pl.BlockSpec(memory_space=pl.ANY)


def front_kernel(
    n1_ref, wa_ref, wb_ref, wc_ref, ba_ref, bb_ref, bc_ref, ta_ref, tb_ref, tc_ref, skip_ref,
    tab_any, itab_any, spec_ref,
    proj_ref, gate_ref, gated_ref, mixed_ref, branch_ref, sig_ref,
    sa_ref, sb_ref, sc_ref, part_ref, turn_ref, long_ref, tab_ref, itab_ref, tab_sem,
):
    ready = fetch_tables(tab_any, itab_any, tab_ref, itab_ref, tab_sem)
    scr = (sa_ref, sb_ref, sc_ref)
    for ref, w_ref, b_ref in zip(scr, (wa_ref, wb_ref, wc_ref), (ba_ref, bb_ref, bc_ref)):
        for r in range(PH):
            ref[r, pl.ds(0, PAD), :] = jnp.zeros((PAD, TILE), F32)
            ref[r, pl.ds(PAD, ML), :] = dot_nn(n1_ref[pl.ds(r * ML, ML), :], w_ref[...]) + b_ref[...]
    taps = [[t[pl.ds(j, 1), :] for j in range(3)] for t in (ta_ref, tb_ref, tc_ref)]
    step = 32

    @pl.loop(0, ML // step)
    def _(i):
        rows = pl.multiple_of(i * step, step)
        outs = []
        for n in range(3):
            ref = scr[n]
            p = [ref[r, pl.ds(PAD + rows, step), :] for r in range(PH)]
            low = [pltpu.roll(ref[r, pl.ds(rows, step + PAD), :], 1, 0)[PAD:, :] for r in (2, 3)]
            seq = low + p
            w0, w1, w2 = taps[n]
            short = [w0 * seq[r + 2] + w1 * seq[r + 1] + w2 * seq[r] for r in range(PH)]
            for r in range(PH):
                proj_ref[n, pl.ds(r * ML + rows, step), :] = p[r].astype(BF16)
                gate_ref[n, pl.ds(r * ML + rows, step), :] = short[r].astype(BF16)
            outs.append(short)
        for r in range(PH):
            gated_ref[pl.ds(r * ML + rows, step), :] = (outs[1][r] * outs[2][r]).astype(BF16)

    ready(0)
    forward_dft(tab_ref, lambda r: gated_ref[pl.ds(r * ML, ML), :], part_ref)
    step2 = 32

    @pl.loop(0, ML // step2)
    def _(i):
        rows = pl.multiple_of(i * step2, step2)
        bins = split_bins(lambda at: part_ref[pl.ds(at, step2), :], rows)
        out = []
        for j in range(PH):
            xr, xi = bins[j]
            at = j * 2 * ML + rows
            sig_ref[pl.ds(at, step2), :] = xr
            sig_ref[pl.ds(at + ML, step2), :] = xi
            hr = spec_ref[pl.ds(at, step2), :]
            hi = spec_ref[pl.ds(at + ML, step2), :]
            out.append((xr * hr - xi * hi, xr * hi + xi * hr))

        def put(at, value):
            turn_ref[pl.ds(at, step2), :] = value

        join_bins(out, put, rows)

    skip = skip_ref[...]
    ready(1)
    for r in range(PH):
        long_ref[pl.ds(r * ML, ML), :] = dot_nn(
            itab_ref[pl.ds(r * ML, ML), :], turn_ref[pl.ds(r * 2 * ML, 2 * ML), :]
        )

    @pl.loop(0, ML // step)
    def _(i):
        rows = pl.multiple_of(i * step, step)
        for r in range(PH):
            at = pl.ds(r * ML + rows, step)
            mixed = long_ref[at, :] + skip * gated_ref[at, :].astype(F32)
            mixed_ref[at, :] = mixed.astype(BF16)
            branch_ref[at, :] = (gate_ref[0, at, :].astype(F32) * mixed).astype(BF16)


def front(n1, in_w, in_b, taps, skip, tab, itab, spec):
    nt = D // TILE
    cols = lambda k: pl.BlockSpec((D, TILE), lambda i, k=k: (0, k * nt + i))
    row = lambda k, h: pl.BlockSpec((h, TILE), lambda i, k=k: (0, k * nt + i))
    out = pl.BlockSpec((L, TILE), lambda i: (0, i))
    out3 = pl.BlockSpec((3, L, TILE), lambda i: (0, 0, i))
    return pl.pallas_call(
        front_kernel,
        grid=(nt,),
        in_specs=[whole((L, D))] + [cols(k) for k in range(3)] + [row(k, 1) for k in range(3)]
        + [row(k, 3) for k in range(3)] + [row(0, 1), FAR, FAR,
           pl.BlockSpec((2 * L, TILE), lambda i: (0, i))],
        out_specs=[out3, out3, out, out, out, pl.BlockSpec((2 * L, TILE), lambda i: (0, i))],
        out_shape=[
            jax.ShapeDtypeStruct((3, L, D), BF16), jax.ShapeDtypeStruct((3, L, D), BF16),
            jax.ShapeDtypeStruct((L, D), BF16), jax.ShapeDtypeStruct((L, D), BF16),
            jax.ShapeDtypeStruct((L, D), BF16), jax.ShapeDtypeStruct((2 * L, D), BF16),
        ],
        scratch_shapes=[pltpu.VMEM((PH, PAD + ML, TILE), F32)] * 3
        + [pltpu.VMEM((2 * L, TILE), BF16), pltpu.VMEM((2 * L, TILE), BF16), pltpu.VMEM((L, TILE), F32)] + TABLES,
        compiler_params=params(),
        cost_estimate=cost(2 * L * D * 3 * D + 4 * 2 * L * ML * D, 80 << 20),
        name="front",
    )(n1, in_w, in_w, in_w, in_b, in_b, in_b, taps, taps, taps, skip, tab, itab, spec)


def gelu_parts(h):
    c = lambda v: jnp.bfloat16(v)
    h = h.astype(BF16)
    t = c(1.0) / (c(1.0) + c(0.3275911 / math.sqrt(2.0)) * jnp.abs(h))
    bell = jnp.exp(c(-0.5) * h * h)
    poly = c(0.5 * 1.061405429) * t - c(0.5 * 1.453152027)
    for k in (0.5 * 1.421413741, -0.5 * 0.284496736, 0.5 * 0.254829592):
        poly = poly * t + c(k)
    tail = poly * t * bell
    phi = jnp.where(h >= 0, c(1.0) - tail, tail)
    return h * phi, phi + h * (bell * c(1.0 / math.sqrt(2.0 * math.pi)))


def norm_stats(v):
    centre = jnp.mean(v, axis=-1, keepdims=True)
    centred = v - centre
    inv = lax.rsqrt(jnp.mean(centred * centred, axis=-1, keepdims=True) + eps)
    return centred * inv, inv


ROWS = 256
CHUNK = 512


def mid_kernel(x_ref, branch_ref, ow_ref, ob_ref, g_ref, s_ref, res_ref, n2_ref):
    res = x_ref[...].astype(F32) + dot_nn(branch_ref[...], ow_ref[...]) + ob_ref[...]
    res_ref[...] = res
    hat, _ = norm_stats(res)
    n2_ref[...] = (hat * g_ref[...] + s_ref[...]).astype(BF16)


def up_kernel(n2_ref, uw_ref, ub_ref, act_ref, slope_ref):
    n2 = n2_ref[...]
    for c in range(FF // CHUNK):
        at = pl.ds(c * CHUNK, CHUNK)
        h = dot_nn(n2, uw_ref[:, at]) + ub_ref[:, at]
        act, slope = gelu_parts(h)
        act_ref[:, at] = act
        slope_ref[:, at] = slope


def mid_stage(x, branch, inout, ob, g, s):
    rows = pl.BlockSpec((2 * ROWS, D), lambda i: (i, 0))
    out_part = pl.BlockSpec((D, D), lambda *_: (0, 3), pipeline_mode=pl.Buffered(1))
    return pl.pallas_call(
        mid_kernel,
        grid=(L // (2 * ROWS),),
        in_specs=[rows, rows, out_part, whole((1, D)), whole((1, D)), whole((1, D))],
        out_specs=[rows, rows],
        out_shape=[jax.ShapeDtypeStruct((L, D), F32), jax.ShapeDtypeStruct((L, D), BF16)],
        compiler_params=params(),
        cost_estimate=cost(2 * L * D * D, 24 << 20),
        name="mid_stage",
    )(x, branch, inout, ob, g, s)


def up_stage(n2, uw, ub):
    rows = lambda n: pl.BlockSpec((2 * ROWS, n), lambda i: (i, 0))
    return pl.pallas_call(
        up_kernel,
        grid=(L // (2 * ROWS),),
        in_specs=[rows(D), whole((D, FF)), whole((1, FF))],
        out_specs=[rows(FF), rows(FF)],
        out_shape=[jax.ShapeDtypeStruct((L, FF), BF16), jax.ShapeDtypeStruct((L, FF), BF16)],
        compiler_params=params(),
        cost_estimate=cost(2 * L * D * FF, 48 << 20),
        name="up_stage",
    )(n2, uw, ub)


def interleave(value, mix_ref, out_ref):
    q = ROWS // PH
    for c in range(D // 128):
        lanes = slice(c * 128, (c + 1) * 128)
        for r in range(PH):
            mix_ref[c, pl.ds(r, q, stride=PH), :] = value[r * q:(r + 1) * q, lanes]
        out_ref[:, lanes] = mix_ref[c].astype(BF16)


def down_kernel(act_ref, slope_ref, res_ref, cot_ref, dw_ref, db_ref, uw_ref, g_ref, out_ref, gh_ref, gres_ref, low_ref, sums_ref, ubg_ref, mix_ref):
    i = pl.program_id(0)

    @pl.when(i == 0)
    def _():
        sums_ref[...] = jnp.zeros_like(sums_ref)
        ubg_ref[...] = jnp.zeros_like(ubg_ref)

    res = res_ref[...].reshape(ROWS, D)
    cot = cot_ref[...].reshape(ROWS, D)
    for c in range(FF // CHUNK):
        at = pl.ds(c * CHUNK, CHUNK)
        ga = dot_nt(cot, dw_ref[at, :])
        gh = (ga * slope_ref[:, :, at].reshape(ROWS, CHUNK).astype(F32)).astype(BF16)
        gh_ref[:, :, at] = gh.reshape(PH, ROWS // PH, CHUNK)
        ubg_ref[pl.ds(0, 1), at] += jnp.sum(gh.astype(F32), axis=0, keepdims=True)
    out = res + dot_nn(act_ref[...].reshape(ROWS, FF), dw_ref[...]) + db_ref[...]
    interleave(out, mix_ref, out_ref)
    gn = dot_nt(gh_ref[...].reshape(ROWS, FF), uw_ref[...])
    hat, inv = norm_stats(res)
    e = gn * g_ref[...]
    cot32 = cot.astype(F32)
    gres = cot32 + inv * (e - jnp.mean(e, axis=-1, keepdims=True) - hat * jnp.mean(e * hat, axis=-1, keepdims=True))
    low = gres.astype(BF16)
    gres_ref[...] = gres.reshape(PH, ROWS // PH, D)
    low_ref[...] = low.reshape(PH, ROWS // PH, D)
    sums_ref[pl.ds(0, 1), :] += jnp.sum(gn * hat, axis=0, keepdims=True)
    sums_ref[pl.ds(1, 1), :] += jnp.sum(gn, axis=0, keepdims=True)
    sums_ref[pl.ds(2, 1), :] += jnp.sum(low.astype(F32), axis=0, keepdims=True)
    sums_ref[pl.ds(3, 1), :] += jnp.sum(cot32, axis=0, keepdims=True)


def down_stage(act, slope, res, cot, dw, db, uw, g):
    q = ROWS // PH
    rows = lambda n: pl.BlockSpec((PH, q, n), lambda i: (0, i, 0))
    fold = lambda a: a.reshape(PH, ML, a.shape[-1])
    out, gh, gres, low, sums, ubg = pl.pallas_call(
        down_kernel,
        grid=(L // ROWS,),
        in_specs=[rows(FF), rows(FF), rows(D), rows(D), whole((FF, D)), whole((1, D)), whole((D, FF)), whole((1, D))],
        out_specs=[pl.BlockSpec((ROWS, D), lambda i: (i, 0)), rows(FF), rows(D), rows(D),
                   pl.BlockSpec((8, D), lambda i: (0, 0)), pl.BlockSpec((8, FF), lambda i: (0, 0))],
        out_shape=[
            jax.ShapeDtypeStruct((L, D), BF16), jax.ShapeDtypeStruct((PH, ML, FF), BF16),
            jax.ShapeDtypeStruct((PH, ML, D), F32), jax.ShapeDtypeStruct((PH, ML, D), BF16),
            jax.ShapeDtypeStruct((8, D), F32), jax.ShapeDtypeStruct((8, FF), F32),
        ],
        scratch_shapes=[pltpu.VMEM((D // 128, ROWS, 128), F32)],
        compiler_params=params(),
        cost_estimate=cost(2 * L * D * 3 * FF, 100 << 20),
        name="down_stage",
    )(fold(act), fold(slope), fold(res), fold(cot), dw, db, uw, g)
    return out, gh.reshape(L, FF), gres.reshape(L, D), low.reshape(L, D), sums, ubg


def grad_kernel(a_ref, b_ref, o_ref):
    o_ref[...] = dot_tn(a_ref[...], b_ref[...]).astype(o_ref.dtype)


def weight_grad(a, b, bm, bn, name):
    m, n = a.shape[1], b.shape[1]
    return pl.pallas_call(
        grad_kernel,
        grid=(m // bm, n // bn),
        in_specs=[pl.BlockSpec((L, bm), lambda i, j: (0, i)), pl.BlockSpec((L, bn), lambda i, j: (0, j))],
        out_specs=pl.BlockSpec((bm, bn), lambda i, j: (i, j)),
        out_shape=jax.ShapeDtypeStruct((m, n), BF16),
        compiler_params=params(),
        cost_estimate=cost(2 * L * m * n, 2 * (L * (m + n) + m * n)),
        name=name,
    )(a, b)


def short_back(n, step, scr, taps_ref, proj_ref, gproj_ref, sums_ref):
    ref = scr[n]
    w = [taps_ref[n, pl.ds(j, 1), :] for j in range(3)]

    def second(i, acc, ref=ref, w=w, n=n):
        rows = pl.multiple_of(i * step, step)
        seq = [ref[r, pl.ds(rows, step), :] for r in range(PH)]
        seq += [pltpu.roll(ref[r, pl.ds(rows, step + PAD), :], step + PAD - 1, 0)[:step, :] for r in range(2)]
        acc = list(acc)
        for r in range(PH):
            at = pl.ds(r * ML + rows, step)
            g = (w[0] * seq[r] + w[1] * seq[r + 1] + w[2] * seq[r + 2]).astype(BF16)
            gproj_ref[n, at, :] = g
            p = proj_ref[n, at, :].astype(F32)
            terms = (g.astype(F32), seq[r] * p, seq[r + 1] * p, seq[r + 2] * p)
            for q in range(4):
                for k in range(step // 8):
                    acc[q] = acc[q] + terms[q][k * 8:(k + 1) * 8, :]
        return tuple(acc)

    zero = jnp.zeros((8, TILE), F32)
    acc = lax.fori_loop(0, ML // step, second, (zero,) * 4)
    for q in range(4):
        sums_ref[pl.ds(1 + 4 * n + q, 1), :] = jnp.sum(acc[q], axis=0, keepdims=True)


def back_kernel(
    low_ref, ow_ref, gate_ref, proj_ref, gated_ref, mixed_ref, sig_ref, spec_ref, taps_ref, skip_ref, tab_any, itab_any,
    second_ref, fw_ref, rates_ref,
    gproj_ref, gfw_ref, gsec_ref, sums_ref,
    gb_ref, gl_ref, part_ref, turn_ref, cross_ref, long_ref, s1_ref, s2_ref, tab_ref, itab_ref, tab_sem,
):
    ready = fetch_tables(tab_any, itab_any, tab_ref, itab_ref, tab_sem)
    scr = (s1_ref, s1_ref, s2_ref)
    gb_ref[...] = dot_nt(low_ref[...], ow_ref[...])
    step = 32
    skip = skip_ref[...]

    def first(i, acc):
        rows = pl.multiple_of(i * step, step)
        for r in range(PH):
            at = pl.ds(r * ML + rows, step)
            gb = gb_ref[at, :]
            gp = gb * gate_ref[0, at, :].astype(F32)
            gl_ref[at, :] = gp.astype(BF16)
            s1_ref[r, pl.ds(rows, step), :] = gb * mixed_ref[at, :].astype(F32)
            gb_ref[at, :] = gp
            prod = gp * gated_ref[at, :].astype(F32)
            for k in range(step // 8):
                acc = acc + prod[k * 8:(k + 1) * 8, :]
        return acc

    acc = lax.fori_loop(0, ML // step, first, jnp.zeros((8, TILE), F32))
    sums_ref[pl.ds(0, 1), :] = jnp.sum(acc, axis=0, keepdims=True)
    for ref in (s1_ref, s2_ref):
        for r in range(2):
            ref[r, pl.ds(ML, PAD), :] = jnp.zeros((PAD, TILE), F32)
    short_back(0, step, scr, taps_ref, proj_ref, gproj_ref, sums_ref)
    ready(0)
    forward_dft(tab_ref, lambda r: gl_ref[pl.ds(r * ML, ML), :], part_ref)
    step2 = 32

    @pl.loop(0, ML // step2)
    def _(i):
        rows = pl.multiple_of(i * step2, step2)
        bins = split_bins(lambda at: part_ref[pl.ds(at, step2), :], rows)
        for other_ref, into_ref in ((spec_ref, turn_ref), (sig_ref, cross_ref)):
            out = []
            for j in range(PH):
                gr, gi = bins[j]
                at = j * 2 * ML + rows
                hr = other_ref[pl.ds(at, step2), :]
                hi = other_ref[pl.ds(at + ML, step2), :]
                out.append((hr * gr + hi * gi, hr * gi - hi * gr))

            def put(at, value, into_ref=into_ref):
                into_ref[pl.ds(at, step2), :] = value

            join_bins(out, put, rows)

    ready(1)
    rates = rates_ref[...]

    @pl.when(pl.program_id(0) == 0)
    def _():
        gsec_ref[...] = jnp.zeros_like(gsec_ref)

    for r in range(PH):
        rows = pl.ds(r * ML, ML)
        freq = pl.ds(r * 2 * ML, 2 * ML)
        gl_ref[rows, :] = (dot_nn(itab_ref[rows, :], cross_ref[freq, :]) * (phase_decay(r, rates) * (1.0 / L))).astype(BF16)
        long_ref[rows, :] = dot_nn(itab_ref[rows, :], turn_ref[freq, :])

    gfw_ref[...] = dot_tn(second_ref[...], gl_ref[...])
    gsec_ref[...] += dot_nt(gl_ref[...], fw_ref[...])

    @pl.loop(0, ML // step)
    def _(i):
        rows = pl.multiple_of(i * step, step)
        for r in range(PH):
            at = pl.ds(r * ML + rows, step)
            gg = long_ref[at, :] + gb_ref[at, :] * skip
            s1_ref[r, pl.ds(rows, step), :] = gg * gate_ref[2, at, :].astype(F32)
            s2_ref[r, pl.ds(rows, step), :] = gg * gate_ref[1, at, :].astype(F32)

    for n in (1, 2):
        short_back(n, step, scr, taps_ref, proj_ref, gproj_ref, sums_ref)


def back(low, inout, gate, proj, gated, mixed, sig, spec, taps3, skip, tab, itab, second, fw, rates):
    tile = lambda h: pl.BlockSpec((h, TILE), lambda i: (0, i))
    tile3 = lambda h: pl.BlockSpec((3, h, TILE), lambda i: (0, 0, i))
    once = lambda h: pl.BlockSpec((h, TILE), lambda i: (0, i), pipeline_mode=pl.Buffered(1))
    width = second.shape[1]
    return pl.pallas_call(
        back_kernel,
        grid=(D // TILE,),
        in_specs=[whole((L, D)), pl.BlockSpec((TILE, D), lambda i: (i, 3)), tile3(L), tile3(L), once(L), once(L),
                  tile(2 * L), tile(2 * L), tile3(3), tile(1), FAR, FAR, whole((L, width)), tile(width), tile(1)],
        out_specs=[tile3(L), tile(width), pl.BlockSpec((L, width), lambda i: (0, 0)), tile(16)],
        out_shape=[
            jax.ShapeDtypeStruct((3, L, D), BF16), jax.ShapeDtypeStruct((width, D), F32),
            jax.ShapeDtypeStruct((L, width), F32), jax.ShapeDtypeStruct((16, D), F32),
        ],
        scratch_shapes=[
            pltpu.VMEM((L, TILE), F32), pltpu.VMEM((L, TILE), BF16), pltpu.VMEM((2 * L, TILE), BF16),
            pltpu.VMEM((2 * L, TILE), BF16), pltpu.VMEM((2 * L, TILE), BF16), pltpu.VMEM((L, TILE), F32),
        ] + [pltpu.VMEM((PH, ML + PAD, TILE), F32)] * 2 + TABLES,
        compiler_params=params(),
        cost_estimate=cost(2 * L * D * D + 12 * L * ML * D, 80 << 20),
        name="back",
    )(low, inout, gate, proj, gated, mixed, sig, spec, taps3, skip, tab, itab, second, fw, rates)


def up_out_kernel(n2_ref, br_ref, gh_ref, low_ref, o_ref):
    j = pl.program_id(0)

    @pl.when(j < FF // D)
    def _():
        o_ref[...] = dot_tn(n2_ref[...], gh_ref[...]).astype(BF16)

    @pl.when(j == FF // D)
    def _():
        o_ref[...] = dot_tn(br_ref[...], low_ref[...]).astype(BF16)


def up_out_grad(n2, branch, gh, low):
    nj = FF // D
    return pl.pallas_call(
        up_out_kernel,
        grid=(nj + 1,),
        in_specs=[whole((L, D)), whole((L, D)), pl.BlockSpec((L, D), lambda j: (0, jnp.minimum(j, nj - 1))), whole((L, D))],
        out_specs=pl.BlockSpec((D, D), lambda j: (0, j)),
        out_shape=jax.ShapeDtypeStruct((D, FF + D), BF16),
        compiler_params=params(),
        cost_estimate=cost(2 * L * D * (FF + D), 40 << 20),
        name="up_out_grad",
    )(n2, branch, gh, low)


def deinterleave(src_ref, mix_ref, put):
    q = ROWS // PH
    for c in range(D // 128):
        lanes = slice(c * 128, (c + 1) * 128)
        mix_ref[c] = src_ref[:, lanes].astype(F32)
        for r in range(PH):
            put(r, lanes, mix_ref[c, pl.ds(r, q, stride=PH), :])


def prep_kernel(x_ref, cot_ref, g_ref, s_ref, xp_ref, cp_ref, n1_ref, mix_ref, flat_ref):
    q = ROWS // PH

    def put_cot(r, lanes, value):
        cp_ref[r, :, lanes] = value.astype(BF16)

    def put_x(r, lanes, value):
        xp_ref[r, :, lanes] = value.astype(BF16)
        flat_ref[pl.ds(r * q, q), lanes] = value

    deinterleave(cot_ref, mix_ref, put_cot)
    deinterleave(x_ref, mix_ref, put_x)
    hat, _ = norm_stats(flat_ref[...])
    n1_ref[...] = (hat * g_ref[...] + s_ref[...]).astype(BF16).reshape(PH, q, D)


def prep(inputs, cotangent, g, s):
    flat = pl.BlockSpec((ROWS, D), lambda i: (i, 0))
    rows = pl.BlockSpec((PH, ROWS // PH, D), lambda i: (0, i, 0))
    out = jax.ShapeDtypeStruct((PH, ML, D), BF16)
    x, cot, n1 = pl.pallas_call(
        prep_kernel,
        grid=(L // ROWS,),
        in_specs=[flat, flat, whole((1, D)), whole((1, D))],
        out_specs=[rows] * 3,
        out_shape=[out] * 3,
        scratch_shapes=[pltpu.VMEM((D // 128, ROWS, 128), F32), pltpu.VMEM((ROWS, D), F32)],
        compiler_params=params(),
        cost_estimate=cost(20 * L * D, 20 << 20),
        name="prep",
    )(inputs, cotangent, g, s)
    return x.reshape(L, D), cot.reshape(L, D), n1.reshape(L, D)


def positions_table(places):
    places = places.astype(F32)
    harmonics = jnp.arange(1, BANDS + 1).astype(F32)
    angles = 2.0 * math.pi / L * places[:, None] * harmonics[None, :]
    return places, jnp.concatenate([places[:, None] / L, jnp.cos(angles), jnp.sin(angles)], axis=1)


def network_layers(places, pos_weight, pos_bias, mid_weight, mid_bias):
    _, features = positions_table(places)
    first = jnp.dot(features, pos_weight, precision=HIGH_ACCURACY) + pos_bias
    layer = jnp.sin(first)
    second = jnp.dot(layer, mid_weight, precision=HIGH_ACCURACY) + mid_bias
    return features, layer, jnp.sin(second), jnp.cos(first), jnp.cos(second)


def network_kernel(grad_ref, feat_ref, layer_ref, slope1_ref, slope2_ref, mid_ref, gpw_ref, gpb_ref, gmw_ref, gmb_ref):
    exact = functools.partial(lax.dot_general, precision=HIGH_ACCURACY, preferred_element_type=F32)
    two = grad_ref[...] * slope2_ref[...]
    gmw_ref[...] = exact(layer_ref[...], two, (((0,), (0,)), ((), ())))
    gmb_ref[...] = jnp.sum(two, axis=0, keepdims=True)
    one = exact(two, mid_ref[...], (((1,), (1,)), ((), ()))) * slope1_ref[...]
    gpw_ref[...] = exact(feat_ref[...], one, (((0,), (0,)), ((), ())))
    gpb_ref[...] = jnp.sum(one, axis=0, keepdims=True)


def network_back(grad, layers, mid_weight):
    features, layer, _, slope1, slope2 = layers
    wide, width = features.shape[1], mid_weight.shape[0]
    shape = lambda n: jax.ShapeDtypeStruct((n, width), F32)
    return pl.pallas_call(
        network_kernel,
        out_shape=[shape(wide), shape(1), shape(width), shape(1)],
        compiler_params=params(),
        cost_estimate=cost(6 * 2 * 3 * L * width * width, 5 << 20),
        name="network_back",
    )(grad, features, layer, slope1, slope2, mid_weight)


def finish_kernel(
    sizes, flat_ref, gain_ref, n1_any, gp_any, iw_any, x_any, gres_any, out_any, rows_ref, total_ref, firsts_ref,
    n1, gp, iw, xs, gres, mix, done_ref, f0, leaving, r1, half, r2, part, r3, sum_ref, f1, g1, f2, g2, g3, u1, u2, u3, sem_s, sem_r, sem_l,
):
    mp, z = sizes
    me = {name: lax.axis_index(name) for name in ("z", "core", "mp")}
    other = {"core": 1 - me["core"]}
    to_mp = [(b, {"mp": lax.rem(me["mp"] + b, mp)}) for b in range(1, mp)]
    to_z = [(b, {"z": lax.rem(me["z"] + b, z)}) for b in range(1, z)]
    q = ROWS // PH
    tiles = L // ROWS

    def load(i, src, dst):
        out = pltpu.make_async_copy(src, dst, sem_l.at[i])
        out.start()
        return out

    chunks, _, rows, width = half.shape
    piece = width // z
    loads, stores = {}, {}

    def fetch_chunk(c):
        if c < chunks:
            at = pl.ds(c * width % D, width)
            loads["g", c] = [load(1 + c, gp_any.at[c * width // D, :, :, at], gp.at[c * width // D, :, :, at])]

    def fetch_tile(i):
        if i < tiles:
            at = pl.ds(i * q, q)
            base = 2 + chunks + 2 * i
            loads["t", i] = [load(base, x_any.at[:, at], xs.at[i % 2]), load(base + 1, gres_any.at[:, at], gres.at[i % 2])]

    def grad_chunk(c):
        for item in ([loads["n1"]] if c == 0 else []) + loads["g", c]:
            item.wait()
        fetch_chunk(c + 2)
        if c + 2 == chunks:
            loads["iw"] = load(1 + chunks, iw_any.at[:, pl.ds(0, 3 * D)], iw)
        if c + 1 == chunks:
            fetch_tile(0)
            fetch_tile(1)
        at = c * width % D
        g = gp[c * width // D, :, :, at:at + width].reshape(L, width)
        value = dot_tn(n1[...], g).astype(BF16).reshape(mp, 2, rows, width)
        half[c] = jnp.where(me["core"] == 0, value[:, 0], value[:, 1])
        leaving[c] = jnp.where(me["core"] == 0, value[:, 1], value[:, 0])
        first[c] = copy(leaving.at[c], r1.at[c], other)

    def last_tile(i):
        at = pl.ds(i * q, q)
        for item in ([loads["iw"]] if i == 0 else []) + loads["t", i]:
            item.wait()
        both = jnp.concatenate([gp[n, :, at].reshape(ROWS, D) for n in range(3)], axis=1)
        gn = dot_nt(both, iw[...])
        hat, inv = norm_stats(xs[i % 2].reshape(ROWS, D).astype(F32))
        e = gn * gain_ref[...]
        fix = jnp.mean(e, axis=-1, keepdims=True) + hat * jnp.mean(e * hat, axis=-1, keepdims=True)
        if i >= 2:
            stores[i - 2].wait()
        interleave(gres[i % 2].reshape(ROWS, D) + inv * (e - fix), mix, done_ref.at[i % 2])
        stores[i] = load(2 + chunks + 2 * tiles + i, done_ref.at[i % 2], out_any.at[pl.ds(i * ROWS, ROWS)])
        fetch_tile(i + 2)
        return jnp.sum(gn * hat, axis=0, keepdims=True), jnp.sum(gn, axis=0, keepdims=True)

    loads["n1"] = load(0, n1_any, n1)
    fetch_chunk(0)
    fetch_chunk(1)
    barrier = pltpu.get_barrier_semaphore()
    peers = [other] + [p for _, p in to_mp] + [p for _, p in to_z]
    for peer in peers:
        pl.semaphore_signal(barrier, inc=1, device_id=peer, device_id_type=pl.DeviceIdType.MESH)
    pl.semaphore_wait(barrier, len(peers))

    count = [0]

    def copy(src, dst, peer):
        i = count[0]
        count[0] += 1
        out = pltpu.make_async_remote_copy(
            src_ref=src, dst_ref=dst, send_sem=sem_s.at[i], recv_sem=sem_r.at[i], device_id=peer,
            device_id_type=pl.DeviceIdType.MESH,
        )
        out.start()
        return out

    sent = []

    def wait(copies):
        for c in copies:
            c.wait_recv()
        sent.extend(copies)

    cols = lambda i: pl.ds(pl.multiple_of(i * piece, piece), piece)
    mine = cols(me["z"])
    first = {}
    flat_now = [[copy(flat_ref.at[1 - me["core"]], g1, other)]]
    second, third, fourth, fifth = {}, {}, {}, {}

    def step_one(c):
        wait([first[c]])
        half[c] = (half[c].astype(F32) + r1[c].astype(F32)).astype(BF16)
        second[c] = [copy(half.at[c, p["mp"]], r2.at[c, b - 1], p) for b, p in to_mp]

    def step_two(c):
        total = half[c, me["mp"]].astype(F32)
        for b in range(mp - 1):
            total = total + r2[c, b].astype(F32)
        part[c] = total.astype(BF16)
        third[c] = [copy(part.at[c, :, cols(p["z"])], r3.at[c, b - 1], p) for b, p in to_z]

    def step_three(c):
        wait(third[c])
        total = part[c, :, mine].astype(F32)
        for b in range(z - 1):
            total = total + r3[c, b].astype(F32)
        sum_ref[me["core"], c, :, mine] = total.astype(BF16)
        here = sum_ref.at[me["core"], c, :, mine]
        fourth[c] = [copy(here, here, p) for b, p in to_z]

    def step_four(c):
        wait(fourth[c])
        here = sum_ref.at[me["core"], c]
        fifth[c] = copy(here, here, other)

    def flat_sum(value, got):
        for b in range(got.shape[0]):
            value = value + got[b]
        return value

    def flat_step(i):
        core, at = me["core"], total_ref.at
        if i == 0:
            wait(flat_now[0])
            f1[...] = flat_ref[core] + g1[...]
            flat_now[0] = [copy(f1.at[p["mp"]], g2.at[b - 1], p) for b, p in to_mp]
        elif i == 1:
            wait(flat_now[0])
            f2[...] = flat_sum(f1[me["mp"]], g2)
            flat_now[0] = [copy(f2.at[p["z"]], g3.at[b - 1], p) for b, p in to_z]
        elif i == 2:
            wait(flat_now[0])
            total_ref[core, me["mp"], me["z"]] = flat_sum(f2[me["z"]], g3)
            own = at[core, me["mp"], me["z"]]
            flat_now[0] = [copy(own, own, p) for b, p in to_z]
        elif i == 3:
            wait(flat_now[0])
            own = at[core, me["mp"]]
            flat_now[0] = [copy(own, own, p) for b, p in to_mp]
        elif i == 4:
            wait(flat_now[0])
            own = at[core]
            flat_now[0] = [copy(own, own, other)]

    first_now = [None]

    def first_step(i):
        if i == 0:
            for n, value in enumerate((gain_sum, shift_sum)):
                for j in range(D // 128):
                    f0[0, n * 8 + j:n * 8 + j + 1, :] = value[:, j * 128:(j + 1) * 128]
            first_now[0] = [copy(f0.at[0], u1, other)]
        elif i == 1:
            wait(first_now[0])
            f0[1] = f0[0] + u1[...]
            first_now[0] = [copy(f0.at[1], u2.at[b - 1], p) for b, p in to_mp]
        elif i == 2:
            wait(first_now[0])
            f0[2] = flat_sum(f0[1], u2)
            first_now[0] = [copy(f0.at[2], u3.at[b - 1], p) for b, p in to_z]

    one = two = three = four = flats = 0

    def middle():
        nonlocal one, two, three, flats
        if two < one:
            wait(second[two])
            if one < min(chunks, len(first)):
                step_one(one)
                one += 1
            step_two(two)
            two += 1
        if three < two and (three < two - 1 or two == chunks):
            step_three(three)
            three += 1
        flat_step(flats)
        flats += 1

    def back_to_core():
        nonlocal four
        if four < three and (four < three - 1 or three == chunks):
            step_four(four)
            four += 1

    gain_sum = shift_sum = None
    for k in range(chunks + tiles):
        if k < chunks:
            grad_chunk(k)
        else:
            gain, shift = last_tile(k - chunks)
            gain_sum = gain if gain_sum is None else gain_sum + gain
            shift_sum = shift if shift_sum is None else shift_sum + shift
        if k >= 1 and one < min(2, chunks):
            step_one(one)
            one += 1
        elif k >= 3 and k % 2 == 1:
            middle()
        elif k >= 3:
            back_to_core()
    ends = 0
    while four < chunks or flats < 5 or ends < 3:
        first_step(ends)
        ends += 1
        middle()
        back_to_core()
    for i in (tiles - 2, tiles - 1):
        stores[i].wait()
    wait(first_now[0])
    firsts_ref[...] = flat_sum(f0[2], u3)
    wait(flat_now[0] + [fifth[c] for c in range(chunks)])
    for c in range(chunks):
        for core in range(2):
            rows_ref[core, :, c * width:(c + 1) * width] = sum_ref[core, c].astype(F32)
    for c in sent:
        c.wait_send()


def finish(flat, gain, n1, gproj, in_w, x, gres):
    mp, z = lax.axis_size("mp"), lax.axis_size("z")
    width = 128 * z
    chunks = 3 * D // width
    rows = D // (2 * mp)
    word = flat.shape[-1]
    tiles, q = L // ROWS, ROWS // PH
    copies = chunks * (2 + (mp - 1) + 2 * (z - 1)) + 3 + 3 * (mp - 1) + 3 * (z - 1)
    vm = lambda *shape: pltpu.VMEM(shape, BF16)
    vf = lambda *shape: pltpu.VMEM(shape, F32)
    spec = pl.BlockSpec(memory_space=pltpu.VMEM)
    fold = lambda a: a.reshape(PH, ML, D)
    out, row_sum, total, firsts = pl.pallas_call(
        functools.partial(finish_kernel, (mp, z)),
        in_specs=[spec] * 2 + [FAR] * 5,
        out_specs=[FAR] + [spec] * 3,
        out_shape=[
            jax.ShapeDtypeStruct((L, D), BF16), jax.ShapeDtypeStruct((2, rows, 3 * D), F32),
            jax.ShapeDtypeStruct(flat.shape, F32), jax.ShapeDtypeStruct((16, 128), F32),
        ],
        scratch_shapes=[
            vm(L, D), vm(3, PH, ML, D), vm(D, 3 * D), vm(2, PH, q, D), vf(2, PH, q, D), vf(D // 128, ROWS, 128),
            vm(2, ROWS, D), vf(3, 16, 128), vm(chunks, mp, rows, width), vm(chunks, mp, rows, width),
            vm(chunks, mp, rows, width), vm(chunks, mp - 1, rows, width), vm(chunks, rows, width),
            vm(chunks, z - 1, rows, width // z), vm(2, chunks, rows, width),
            vf(mp, z, 8, word), vf(mp, z, 8, word), vf(z, 8, word), vf(mp - 1, z, 8, word), vf(z - 1, 8, word),
            vf(16, 128), vf(mp - 1, 16, 128), vf(z - 1, 16, 128),
            pltpu.SemaphoreType.DMA((copies,)), pltpu.SemaphoreType.DMA((copies,)),
            pltpu.SemaphoreType.DMA((2 + chunks + 3 * tiles,)),
        ],
        compiler_params=params(collective_id=0, has_side_effects=True),
        cost_estimate=cost(2 * 2 * L * D * 3 * D, 60 << 20),
        name="finish",
    )(flat, gain, n1, gproj.reshape(3, PH, ML, D), in_w, fold(x), fold(gres))
    return out, row_sum.reshape(2 * rows, 3 * D), total, firsts


VECTORS = (
    ("first_gain", 1), ("first_shift", 1), ("in_bias", 3), ("short", 9), ("skip", 1), ("out_bias", 1),
    ("second_gain", 1), ("second_shift", 1), ("up_bias", 4), ("down_bias", 1),
)


def swap_bit(x, axis, bit):
    size = lax.axis_size(axis)
    return lax.ppermute(x, axis, [(i, i ^ bit) for i in range(size)])


def add_low(*parts):
    total = parts[0].astype(F32)
    for part in parts[1:]:
        total = total + part.astype(F32)
    return total.astype(BF16)


def hold(*values):
    return lax.optimization_barrier(values)


def entry(x, i):
    return lax.dynamic_index_in_dim(x, i, 0, False)


def in_order(pieces, axis):
    place = lax.axis_index(axis)
    stacked = jnp.stack(pieces)
    return jnp.concatenate([entry(stacked, place ^ i) for i in range(len(pieces))], axis=0)


def spread_steps(x, axis, add):
    place = lax.axis_index(axis)
    got = yield [(entry(x, place ^ b), axis, b) for b in range(1, x.shape[0])]
    return add(entry(x, place), *got)


def collect_steps(x, axis):
    got = yield [(x, axis, b) for b in range(1, lax.axis_size(axis))]
    return in_order([x] + list(got), axis)


def both_cores(mine, other):
    core = lax.axis_index("core")
    low = jnp.where(core == 0, mine, other)
    high = jnp.where(core == 0, other, mine)
    return jnp.concatenate([low, high], axis=0).astype(F32)


def share_steps(share):
    z = lax.axis_size("z")
    rows, cols = share.shape
    mine = yield from spread_steps(share.reshape(z, rows // z, cols), "z", add_low)
    mine = yield from collect_steps(mine, "z")
    return (yield from collect_steps(mine, "core")).astype(F32)


class Chains:
    def __init__(self):
        self.live, self.done = {}, {}

    def start(self, name, steps):
        self.live[name] = (steps, next(steps))

    def move(self, names, first, kernel):
        names = [n for n in names if n in self.live]
        sends = [send for n in names for send in self.live[n][1]]
        held = hold(first, *(s[0] for s in sends))
        got = [swap_bit(v, s[1], s[2]) for v, s in zip(held[1:], sends)]
        out = kernel(held[0])
        flat, tree = jax.tree.flatten(out)
        held = hold(*flat, *got)
        out = jax.tree.unflatten(tree, held[:len(flat)])
        got = list(held[len(flat):])
        for n in names:
            steps, wanted = self.live.pop(n)
            arrived, got = got[:len(wanted)], got[len(wanted):]
            try:
                self.live[n] = (steps, steps.send(arrived))
            except StopIteration as stop:
                self.done[n] = stop.value
        return out

    def finish(self):
        while self.live:
            self.move(list(self.live), jnp.zeros((8, 128), F32), lambda v: v)


def scatter_rows(grad):
    return lax.psum_scatter(grad, ("mp", "core"), scatter_dimension=0, tiled=True)


def gather_rows(shard):
    rows = shard.shape[0]
    half = lax.dynamic_slice_in_dim(shard, lax.axis_index("core") * (rows // 2), rows // 2, 0)
    return lax.all_gather(half, ("mp", "core"), axis=0, tiled=True)


def shards(
    inputs, first_gain, first_shift, in_weight, in_bias, short_weight, skip_gain, pos_weight, pos_bias,
    mid_weight, mid_bias, filter_weight, decay_rates, out_weight, out_bias, second_gain, second_shift,
    up_weight, up_bias, down_weight, down_bias, cotangent,
):
    mp = lax.axis_size("mp")
    own = D // mp
    local = (first_gain, first_shift, in_bias, short_weight, skip_gain, out_bias, second_gain, second_shift, up_bias, down_bias)
    packed = jnp.concatenate([v.reshape(-1) for v in local]).reshape(1, -1)
    spread = in_order([packed] + [swap_bit(packed, "mp", b) for b in range(1, mp)], "mp").astype(F32)
    full = {}
    at = 0
    for name, count in VECTORS:
        part = spread[:, at:at + count * own]
        at += count * own
        if name == "short":
            part = part.reshape(mp, 3, 3 * own).swapaxes(0, 1)
            full[name] = part.reshape(3, 3 * D)
        else:
            full[name] = part.reshape(1, count * D)
    inout = gather_rows(jnp.concatenate([in_weight, out_weight], axis=1))
    up_matrix = gather_rows(up_weight)
    down_matrix = gather_rows(down_weight)

    tab, itab = (jnp.asarray(t) for t in dft_tables())
    x, cot, n1 = prep(inputs, cotangent, full["first_gain"], full["first_shift"])
    places = (jnp.arange(PH)[:, None] + PH * jnp.arange(ML)[None, :]).reshape(L)
    layers = network_layers(places, pos_weight, pos_bias, mid_weight, mid_bias)
    second = layers[2]
    rates = decay_rates.reshape(1, D)
    spec = filter_spectrum(tab, second, filter_weight, rates)
    proj, gate, gated, mixed, branch, sig = front(n1, inout, full["in_bias"], full["short"], full["skip"], tab, itab, spec)
    res, n2 = mid_stage(x, branch, inout, full["out_bias"], full["second_gain"], full["second_shift"])
    act, slope = up_stage(n2, up_matrix, full["up_bias"])
    down_grad = weight_grad(act, cot, 1024, 1024, "down_weight_grad")
    act, down_grad = hold(act, down_grad)
    block_out, gh, gres, low, sums_two, up_bias_sum = down_stage(act, slope, res, cot, down_matrix, full["down_bias"], up_matrix, full["second_gain"])
    down_share = scatter_rows(down_grad)
    chains = Chains()
    low, down_share = hold(low, down_share)
    chains.start("down", share_steps(down_share))
    up_out = chains.move(["down"], low, lambda v: up_out_grad(n2, branch, gh, v))
    low, up_out = hold(low, up_out)
    up_share = scatter_rows(up_out)
    taps3 = full["short"].reshape(3, 3, D).swapaxes(0, 1)
    kept = (inout, gate, proj, gated, mixed, sig, spec, taps3, full["skip"], tab, itab, second.astype(BF16), filter_weight.astype(BF16), rates)
    gproj, gfw, gsec, sums_mid = chains.move(["down"], low, lambda v: back(v, *kept))
    gproj, gsec, up_share = hold(gproj, gsec, up_share)
    up_half = lax.psum(up_share, "z")
    net = tuple(chains.move(["down"], gsec, lambda v: network_back(v, layers, mid_weight))) + (gfw,)
    mids = sums_mid[1:13].reshape(3, 4, D)
    vectors = {
        "in_bias": mids[:, 0].reshape(3 * D), "short": mids[:, 1:].swapaxes(0, 1).reshape(3, 3 * D), "skip": sums_mid[0],
        "out_bias": sums_two[2], "second_gain": sums_two[0], "second_shift": sums_two[1], "up_bias": up_bias_sum[0],
        "down_bias": sums_two[3],
    }
    by_owner = lambda name, count: vectors[name].reshape(-1, mp, count * own).swapaxes(0, 1).reshape(mp, -1)
    middle = [(name, 3 if name == "short" else count) for name, count in VECTORS[2:]]
    flats = [jnp.concatenate([by_owner(*item) for item in middle], axis=1).reshape(-1)]
    flats += [n.reshape(-1) for n in net]
    length = sum(f.shape[0] for f in flats)
    group = (2, mp, lax.axis_size("z"), 8)
    count = math.prod(group)
    word = -(-length // (128 * count)) * 128
    flat = jnp.concatenate(flats + [jnp.zeros((count * word - length,), F32)]).reshape(group + (word,))
    kernel = lambda v: finish(flat, full["first_gain"], n1, v, inout, x, gres)
    input_grad, in_sum, flat_sum, firsts = kernel(gproj)
    in_sum, up_half = hold(in_sum, up_half)
    up_both = both_cores(up_half, swap_bit(up_half, "core", 1))
    done = chains.done
    down_sum = done["down"]
    up_sum, out_sum = up_both[:, :FF], up_both[:, FF:]
    me = lax.axis_index("mp")
    firsts = firsts.reshape(2, D)
    mine = {
        "first_gain": lax.dynamic_slice_in_dim(firsts[0], me * own, own, 0),
        "first_shift": lax.dynamic_slice_in_dim(firsts[1], me * own, own, 0),
    }
    flat_sum = flat_sum.reshape(-1)
    span = sum(count for _, count in VECTORS[2:]) * own
    local = lax.dynamic_slice_in_dim(flat_sum, me * span, span, 0)
    at = 0
    for name, count in VECTORS[2:]:
        mine[name] = local[at:at + count * own]
        at += count * own
    mine["short"] = mine["short"].reshape(3, 3 * own)
    at = mp * span
    pieces = []
    for n in net:
        pieces.append(flat_sum[at:at + n.size])
        at += n.size
    net_sum = [p.reshape(n.shape) for p, n in zip(pieces, (pos_weight, pos_bias, mid_weight, mid_bias, filter_weight))]
    return (
        block_out, input_grad, mine["first_gain"], mine["first_shift"], in_sum, mine["in_bias"], mine["short"], mine["skip"],
        *net_sum, out_sum, mine["out_bias"], mine["second_gain"], mine["second_shift"], up_sum, mine["up_bias"],
        down_sum, mine["down_bias"],
    )


def solution(mesh):
    dp, mp = mesh.devices.shape
    split = jax.sharding.Mesh(mesh.devices.reshape(dp // 2, 2, mp), ("z", "core", "mp"))
    tokens = P(("z", "core", "mp"), None)
    row, vec, rep = P("mp", None), P("mp"), P()
    return jax.shard_map(
        shards,
        mesh=split,
        in_specs=(
            tokens, vec, vec, row, vec, P(None, "mp"), vec, rep, rep, rep, rep, rep, rep, row, vec, vec, vec, row, vec, row,
            vec, tokens,
        ),
        out_specs=(
            tokens, tokens, vec, vec, row, vec, P(None, "mp"), vec, rep, rep, rep, rep, rep, row, vec, vec, vec, row, vec,
            row, vec,
        ),
        check_vma=False,
    )
```

```python
import functools
import math

import jax
import jax.numpy as jnp
import numpy as np
from jax import lax
from jax.experimental import pallas as pl
from jax.experimental.pallas import tpu as pltpu
from jax.sharding import PartitionSpec as P

D = 1024
FF = 4096
BANDS = 16
L = 2048
PH = 4
ML = L // PH
TILE = 256
PAD = 8

HIGH_ACCURACY = lax.Precision.HIGHEST
eps = 1e-05
decay_floor = 0.05
F32 = jnp.float32
BF16 = jnp.bfloat16
VMEM_BYTES = 62 << 20


def dot_nn(a, b):
    return lax.dot_general(a, b, (((1,), (0,)), ((), ())), preferred_element_type=F32)


def dot_nt(a, b):
    return lax.dot_general(a, b, (((1,), (1,)), ((), ())), preferred_element_type=F32)


def dot_tn(a, b):
    return lax.dot_general(a, b, (((0,), (0,)), ((), ())), preferred_element_type=F32)


def dft_tables():
    times = PH * np.arange(ML)[None, None, :] + np.arange(PH)[:, None, None]
    odd = 2 * np.arange(ML)[None, :, None] + 1
    angle = 2.0 * np.pi / (4 * L) * ((times * odd) % (4 * L)).astype(np.float64)
    table = np.concatenate([np.cos(angle), -np.sin(angle)], axis=1)
    forward = table.reshape(PH * 2 * ML, ML).astype(jnp.bfloat16)
    backward = np.swapaxes(table, 1, 2).reshape(PH * ML, 2 * ML).astype(jnp.bfloat16)
    return forward, backward


def whole(shape):
    return pl.BlockSpec(shape, lambda *_: (0,) * len(shape), pipeline_mode=pl.Buffered(1))


def params(**kw):
    return pltpu.CompilerParams(vmem_limit_bytes=VMEM_BYTES, **kw)


def cost(flops, moved):
    return pl.CostEstimate(flops=int(flops), bytes_accessed=int(moved), transcendentals=0)


def forward_dft(tab_ref, src, dst_ref):
    for r in range(PH):
        dst_ref[pl.ds(r * 2 * ML, 2 * ML), :] = dot_nn(tab_ref[pl.ds(r * 2 * ML, 2 * ML), :], src(r)).astype(BF16)


def split_bins(part, rows):
    re = [part(r * 2 * ML + rows) for r in range(PH)]
    im = [part(r * 2 * ML + ML + rows) for r in range(PH)]
    ar, ai, br, bi = re[0] + re[2], im[0] + im[2], re[0] - re[2], im[0] - im[2]
    cr, ci, dr, di = re[1] + re[3], im[1] + im[3], re[1] - re[3], im[1] - im[3]
    return [(ar + cr, ai + ci), (br + di, bi - dr), (ar - cr, ai - ci), (br - di, bi + dr)]


def join_bins(bins, put, rows):
    (r0, i0), (r1, i1), (r2, i2), (r3, i3) = bins
    ar, ai, br, bi = r0 + r2, i0 + i2, r0 - r2, i0 - i2
    cr, ci, dr, di = r1 + r3, i1 + i3, r1 - r3, i1 - i3
    out = [(ar + cr, ai + ci), (br - di, bi + dr), (ar - cr, ai - ci), (br + di, bi - dr)]
    for r in range(PH):
        put(r * 2 * ML + rows, out[r][0])
        put(r * 2 * ML + ML + rows, out[r][1])


def phase_decay(r, rates):
    places = (PH * lax.broadcasted_iota(jnp.int32, (ML, TILE), 0) + r).astype(F32)
    return jnp.exp(-rates * places * (1.0 / L)) + decay_floor


def filter_kernel(tab_ref, second_ref, fw_ref, rates_ref, spec_ref, part_ref, filt_ref, wide_ref):
    width = second_ref.shape[1]

    @pl.when(pl.program_id(0) == 0)
    def _():
        value = second_ref[...]
        high = value.astype(BF16)
        wide_ref[:, 0:width] = high
        wide_ref[:, width:2 * width] = (value - high.astype(F32)).astype(BF16)
        wide_ref[:, 2 * width:3 * width] = high

    weight = fw_ref[...]
    high = weight.astype(BF16)
    rest = (weight - high.astype(F32)).astype(BF16)
    three = jnp.concatenate([high, high, rest], axis=0)
    rates = rates_ref[...]
    for r in range(PH):
        rows = pl.ds(r * ML, ML)
        filt_ref[rows, :] = (dot_nn(wide_ref[rows, :], three) * phase_decay(r, rates)).astype(BF16)
    forward_dft(tab_ref, lambda r: filt_ref[pl.ds(r * ML, ML), :], part_ref)
    step = 64

    @pl.loop(0, ML // step)
    def _(i):
        rows = pl.multiple_of(i * step, step)
        bins = split_bins(lambda at: part_ref[pl.ds(at, step), :], rows)
        for j in range(PH):
            spec_ref[pl.ds(j * 2 * ML + rows, step), :] = bins[j][0] * jnp.bfloat16(1.0 / L)
            spec_ref[pl.ds(j * 2 * ML + ML + rows, step), :] = bins[j][1] * jnp.bfloat16(1.0 / L)


def filter_spectrum(tab, second, filter_weight, rates):
    width = second.shape[1]
    return pl.pallas_call(
        filter_kernel,
        grid=(D // TILE,),
        in_specs=[whole((PH * 2 * ML, ML)), whole((L, width)), pl.BlockSpec((width, TILE), lambda i: (0, i)),
                  pl.BlockSpec((1, TILE), lambda i: (0, i))],
        out_specs=pl.BlockSpec((2 * L, TILE), lambda i: (0, i)),
        out_shape=jax.ShapeDtypeStruct((2 * L, D), BF16),
        scratch_shapes=[pltpu.VMEM((2 * L, TILE), BF16), pltpu.VMEM((L, TILE), BF16), pltpu.VMEM((L, 3 * width), BF16)],
        compiler_params=params(),
        cost_estimate=cost(2 * 2 * L * ML * D, 16 << 20),
        name="filter_spectrum",
    )(tab, second, filter_weight, rates)


def fetch_tables(tab_any, itab_any, tab_ref, itab_ref, sem):
    copies = [pltpu.make_async_copy(tab_any, tab_ref, sem.at[0]), pltpu.make_async_copy(itab_any, itab_ref, sem.at[1])]
    is_first = pl.program_id(0) == 0

    @pl.when(is_first)
    def _():
        for c in copies:
            c.start()

    def ready(n):
        @pl.when(is_first)
        def _():
            copies[n].wait()

    return ready


TABLES = [pltpu.VMEM((PH * 2 * ML, ML), BF16), pltpu.VMEM((PH * ML, 2 * ML), BF16), pltpu.SemaphoreType.DMA((2,))]
FAR = pl.BlockSpec(memory_space=pl.ANY)


def front_kernel(
    n1_ref, wa_ref, wb_ref, wc_ref, ba_ref, bb_ref, bc_ref, ta_ref, tb_ref, tc_ref, skip_ref,
    tab_any, itab_any, spec_ref,
    proj_ref, gate_ref, gated_ref, mixed_ref, branch_ref, sig_ref,
    sa_ref, sb_ref, sc_ref, part_ref, turn_ref, long_ref, tab_ref, itab_ref, tab_sem,
):
    ready = fetch_tables(tab_any, itab_any, tab_ref, itab_ref, tab_sem)
    scr = (sa_ref, sb_ref, sc_ref)
    for ref, w_ref, b_ref in zip(scr, (wa_ref, wb_ref, wc_ref), (ba_ref, bb_ref, bc_ref)):
        for r in range(PH):
            ref[r, pl.ds(0, PAD), :] = jnp.zeros((PAD, TILE), F32)
            ref[r, pl.ds(PAD, ML), :] = dot_nn(n1_ref[pl.ds(r * ML, ML), :], w_ref[...]) + b_ref[...]
    taps = [[t[pl.ds(j, 1), :] for j in range(3)] for t in (ta_ref, tb_ref, tc_ref)]
    step = 64

    @pl.loop(0, ML // step)
    def _(i):
        rows = pl.multiple_of(i * step, step)
        outs = []
        for n in range(3):
            ref = scr[n]
            p = [ref[r, pl.ds(PAD + rows, step), :] for r in range(PH)]
            low = [pltpu.roll(ref[r, pl.ds(rows, step + PAD), :], 1, 0)[PAD:, :] for r in (2, 3)]
            seq = low + p
            w0, w1, w2 = taps[n]
            short = [w0 * seq[r + 2] + w1 * seq[r + 1] + w2 * seq[r] for r in range(PH)]
            for r in range(PH):
                proj_ref[n, pl.ds(r * ML + rows, step), :] = p[r].astype(BF16)
                gate_ref[n, pl.ds(r * ML + rows, step), :] = short[r].astype(BF16)
            outs.append(short)
        for r in range(PH):
            gated_ref[pl.ds(r * ML + rows, step), :] = (outs[1][r] * outs[2][r]).astype(BF16)

    ready(0)
    forward_dft(tab_ref, lambda r: gated_ref[pl.ds(r * ML, ML), :], part_ref)
    step2 = 64

    @pl.loop(0, ML // step2)
    def _(i):
        rows = pl.multiple_of(i * step2, step2)
        bins = split_bins(lambda at: part_ref[pl.ds(at, step2), :], rows)
        out = []
        for j in range(PH):
            xr, xi = bins[j]
            at = j * 2 * ML + rows
            sig_ref[pl.ds(at, step2), :] = xr
            sig_ref[pl.ds(at + ML, step2), :] = xi
            hr = spec_ref[pl.ds(at, step2), :]
            hi = spec_ref[pl.ds(at + ML, step2), :]
            out.append((xr * hr - xi * hi, xr * hi + xi * hr))

        def put(at, value):
            turn_ref[pl.ds(at, step2), :] = value

        join_bins(out, put, rows)

    skip = skip_ref[...]
    ready(1)
    for r in range(PH):
        long_ref[pl.ds(r * ML, ML), :] = dot_nn(
            itab_ref[pl.ds(r * ML, ML), :], turn_ref[pl.ds(r * 2 * ML, 2 * ML), :]
        )

    @pl.loop(0, ML // step)
    def _(i):
        rows = pl.multiple_of(i * step, step)
        for r in range(PH):
            at = pl.ds(r * ML + rows, step)
            mixed = long_ref[at, :] + skip * gated_ref[at, :].astype(F32)
            mixed_ref[at, :] = mixed.astype(BF16)
            branch_ref[at, :] = (gate_ref[0, at, :].astype(F32) * mixed).astype(BF16)


def front(n1, in_w, in_b, taps, skip, tab, itab, spec):
    nt = D // TILE
    cols = lambda k: pl.BlockSpec((D, TILE), lambda i, k=k: (0, k * nt + i))
    row = lambda k, h: pl.BlockSpec((h, TILE), lambda i, k=k: (0, k * nt + i))
    out = pl.BlockSpec((L, TILE), lambda i: (0, i))
    out3 = pl.BlockSpec((3, L, TILE), lambda i: (0, 0, i))
    return pl.pallas_call(
        front_kernel,
        grid=(nt,),
        in_specs=[whole((L, D))] + [cols(k) for k in range(3)] + [row(k, 1) for k in range(3)]
        + [row(k, 3) for k in range(3)] + [row(0, 1), FAR, FAR,
           pl.BlockSpec((2 * L, TILE), lambda i: (0, i))],
        out_specs=[out3, out3, out, out, out, pl.BlockSpec((2 * L, TILE), lambda i: (0, i))],
        out_shape=[
            jax.ShapeDtypeStruct((3, L, D), BF16), jax.ShapeDtypeStruct((3, L, D), BF16),
            jax.ShapeDtypeStruct((L, D), BF16), jax.ShapeDtypeStruct((L, D), BF16),
            jax.ShapeDtypeStruct((L, D), BF16), jax.ShapeDtypeStruct((2 * L, D), BF16),
        ],
        scratch_shapes=[pltpu.VMEM((PH, PAD + ML, TILE), F32)] * 3
        + [pltpu.VMEM((2 * L, TILE), BF16), pltpu.VMEM((2 * L, TILE), BF16), pltpu.VMEM((L, TILE), F32)] + TABLES,
        compiler_params=params(),
        cost_estimate=cost(2 * L * D * 3 * D + 4 * 2 * L * ML * D, 80 << 20),
        name="front",
    )(n1, in_w, in_w, in_w, in_b, in_b, in_b, taps, taps, taps, skip, tab, itab, spec)


def gelu_parts(h):
    c = lambda v: jnp.bfloat16(v)
    h = h.astype(BF16)
    t = c(1.0) / (c(1.0) + c(0.3275911 / math.sqrt(2.0)) * jnp.abs(h))
    bell = jnp.exp(c(-0.5) * h * h)
    poly = c(0.5 * 1.061405429) * t - c(0.5 * 1.453152027)
    for k in (0.5 * 1.421413741, -0.5 * 0.284496736, 0.5 * 0.254829592):
        poly = poly * t + c(k)
    tail = poly * t * bell
    phi = jnp.where(h >= 0, c(1.0) - tail, tail)
    return h * phi, phi + h * (bell * c(1.0 / math.sqrt(2.0 * math.pi)))


def norm_stats(v):
    centre = jnp.mean(v, axis=-1, keepdims=True)
    centred = v - centre
    inv = lax.rsqrt(jnp.mean(centred * centred, axis=-1, keepdims=True) + eps)
    return centred * inv, inv


ROWS = 256
CHUNK = 512


def mid_kernel(x_ref, branch_ref, ow_ref, ob_ref, g_ref, s_ref, res_ref, n2_ref):
    res = x_ref[...].astype(F32) + dot_nn(branch_ref[...], ow_ref[...]) + ob_ref[...]
    res_ref[...] = res
    hat, _ = norm_stats(res)
    n2_ref[...] = (hat * g_ref[...] + s_ref[...]).astype(BF16)


def up_kernel(n2_ref, uw_ref, ub_ref, act_ref, slope_ref):
    n2 = n2_ref[...]
    for c in range(FF // CHUNK):
        at = pl.ds(c * CHUNK, CHUNK)
        h = dot_nn(n2, uw_ref[:, at]) + ub_ref[:, at]
        act, slope = gelu_parts(h)
        act_ref[:, at] = act
        slope_ref[:, at] = slope


def mid_stage(x, branch, inout, ob, g, s):
    rows = pl.BlockSpec((2 * ROWS, D), lambda i: (i, 0))
    out_part = pl.BlockSpec((D, D), lambda *_: (0, 3), pipeline_mode=pl.Buffered(1))
    return pl.pallas_call(
        mid_kernel,
        grid=(L // (2 * ROWS),),
        in_specs=[rows, rows, out_part, whole((1, D)), whole((1, D)), whole((1, D))],
        out_specs=[rows, rows],
        out_shape=[jax.ShapeDtypeStruct((L, D), F32), jax.ShapeDtypeStruct((L, D), BF16)],
        compiler_params=params(),
        cost_estimate=cost(2 * L * D * D, 24 << 20),
        name="mid_stage",
    )(x, branch, inout, ob, g, s)


def up_stage(n2, uw, ub):
    rows = lambda n: pl.BlockSpec((2 * ROWS, n), lambda i: (i, 0))
    return pl.pallas_call(
        up_kernel,
        grid=(L // (2 * ROWS),),
        in_specs=[rows(D), whole((D, FF)), whole((1, FF))],
        out_specs=[rows(FF), rows(FF)],
        out_shape=[jax.ShapeDtypeStruct((L, FF), BF16), jax.ShapeDtypeStruct((L, FF), BF16)],
        compiler_params=params(),
        cost_estimate=cost(2 * L * D * FF, 48 << 20),
        name="up_stage",
    )(n2, uw, ub)


def interleave(value, mix_ref, out_ref):
    q = ROWS // PH
    for c in range(D // 128):
        lanes = slice(c * 128, (c + 1) * 128)
        for r in range(PH):
            mix_ref[c, pl.ds(r, q, stride=PH), :] = value[r * q:(r + 1) * q, lanes]
        out_ref[:, lanes] = mix_ref[c].astype(BF16)


def down_kernel(act_ref, slope_ref, res_ref, cot_ref, dw_ref, db_ref, uw_ref, g_ref, out_ref, gh_ref, gres_ref, low_ref, sums_ref, ubg_ref, mix_ref):
    i = pl.program_id(0)

    @pl.when(i == 0)
    def _():
        sums_ref[...] = jnp.zeros_like(sums_ref)
        ubg_ref[...] = jnp.zeros_like(ubg_ref)

    res = res_ref[...].reshape(ROWS, D)
    cot = cot_ref[...].reshape(ROWS, D)
    for c in range(FF // CHUNK):
        at = pl.ds(c * CHUNK, CHUNK)
        ga = dot_nt(cot, dw_ref[at, :])
        gh = (ga * slope_ref[:, :, at].reshape(ROWS, CHUNK).astype(F32)).astype(BF16)
        gh_ref[:, :, at] = gh.reshape(PH, ROWS // PH, CHUNK)
        ubg_ref[pl.ds(0, 1), at] += jnp.sum(gh.astype(F32), axis=0, keepdims=True)
    out = res + dot_nn(act_ref[...].reshape(ROWS, FF), dw_ref[...]) + db_ref[...]
    interleave(out, mix_ref, out_ref)
    gn = dot_nt(gh_ref[...].reshape(ROWS, FF), uw_ref[...])
    hat, inv = norm_stats(res)
    e = gn * g_ref[...]
    cot32 = cot.astype(F32)
    gres = cot32 + inv * (e - jnp.mean(e, axis=-1, keepdims=True) - hat * jnp.mean(e * hat, axis=-1, keepdims=True))
    low = gres.astype(BF16)
    gres_ref[...] = gres.reshape(PH, ROWS // PH, D)
    low_ref[...] = low.reshape(PH, ROWS // PH, D)
    sums_ref[pl.ds(0, 1), :] += jnp.sum(gn * hat, axis=0, keepdims=True)
    sums_ref[pl.ds(1, 1), :] += jnp.sum(gn, axis=0, keepdims=True)
    sums_ref[pl.ds(2, 1), :] += jnp.sum(low.astype(F32), axis=0, keepdims=True)
    sums_ref[pl.ds(3, 1), :] += jnp.sum(cot32, axis=0, keepdims=True)


def down_stage(act, slope, res, cot, dw, db, uw, g):
    q = ROWS // PH
    rows = lambda n: pl.BlockSpec((PH, q, n), lambda i: (0, i, 0))
    fold = lambda a: a.reshape(PH, ML, a.shape[-1])
    out, gh, gres, low, sums, ubg = pl.pallas_call(
        down_kernel,
        grid=(L // ROWS,),
        in_specs=[rows(FF), rows(FF), rows(D), rows(D), whole((FF, D)), whole((1, D)), whole((D, FF)), whole((1, D))],
        out_specs=[pl.BlockSpec((ROWS, D), lambda i: (i, 0)), rows(FF), rows(D), rows(D),
                   pl.BlockSpec((8, D), lambda i: (0, 0)), pl.BlockSpec((8, FF), lambda i: (0, 0))],
        out_shape=[
            jax.ShapeDtypeStruct((L, D), BF16), jax.ShapeDtypeStruct((PH, ML, FF), BF16),
            jax.ShapeDtypeStruct((PH, ML, D), F32), jax.ShapeDtypeStruct((PH, ML, D), BF16),
            jax.ShapeDtypeStruct((8, D), F32), jax.ShapeDtypeStruct((8, FF), F32),
        ],
        scratch_shapes=[pltpu.VMEM((D // 128, ROWS, 128), F32)],
        compiler_params=params(),
        cost_estimate=cost(2 * L * D * 3 * FF, 100 << 20),
        name="down_stage",
    )(fold(act), fold(slope), fold(res), fold(cot), dw, db, uw, g)
    return out, gh.reshape(L, FF), gres.reshape(L, D), low.reshape(L, D), sums, ubg


def grad_kernel(a_ref, b_ref, o_ref):
    o_ref[...] = dot_tn(a_ref[...], b_ref[...]).astype(o_ref.dtype)


def weight_grad(a, b, bm, bn, name):
    m, n = a.shape[1], b.shape[1]
    return pl.pallas_call(
        grad_kernel,
        grid=(m // bm, n // bn),
        in_specs=[pl.BlockSpec((L, bm), lambda i, j: (0, i)), pl.BlockSpec((L, bn), lambda i, j: (0, j))],
        out_specs=pl.BlockSpec((bm, bn), lambda i, j: (i, j)),
        out_shape=jax.ShapeDtypeStruct((m, n), BF16),
        compiler_params=params(),
        cost_estimate=cost(2 * L * m * n, 2 * (L * (m + n) + m * n)),
        name=name,
    )(a, b)


def short_back(n, step, scr, taps_ref, proj_ref, gproj_ref, sums_ref):
    ref = scr[n]
    w = [taps_ref[n, pl.ds(j, 1), :] for j in range(3)]

    def second(i, acc, ref=ref, w=w, n=n):
        rows = pl.multiple_of(i * step, step)
        seq = [ref[r, pl.ds(rows, step), :] for r in range(PH)]
        seq += [pltpu.roll(ref[r, pl.ds(rows, step + PAD), :], step + PAD - 1, 0)[:step, :] for r in range(2)]
        acc = list(acc)
        for r in range(PH):
            at = pl.ds(r * ML + rows, step)
            g = (w[0] * seq[r] + w[1] * seq[r + 1] + w[2] * seq[r + 2]).astype(BF16)
            gproj_ref[n, at, :] = g
            p = proj_ref[n, at, :].astype(F32)
            terms = (g.astype(F32), seq[r] * p, seq[r + 1] * p, seq[r + 2] * p)
            for q in range(4):
                for k in range(step // 8):
                    acc[q] = acc[q] + terms[q][k * 8:(k + 1) * 8, :]
        return tuple(acc)

    zero = jnp.zeros((8, TILE), F32)
    acc = lax.fori_loop(0, ML // step, second, (zero,) * 4)
    for q in range(4):
        sums_ref[pl.ds(1 + 4 * n + q, 1), :] = jnp.sum(acc[q], axis=0, keepdims=True)


def back_kernel(
    low_ref, ow_ref, gate_ref, proj_ref, gated_ref, mixed_ref, sig_ref, spec_ref, taps_ref, skip_ref, tab_any, itab_any,
    second_ref, fw_ref, rates_ref,
    gproj_ref, gfw_ref, gsec_ref, sums_ref,
    gb_ref, gl_ref, part_ref, turn_ref, cross_ref, long_ref, s1_ref, s2_ref, tab_ref, itab_ref, tab_sem,
):
    ready = fetch_tables(tab_any, itab_any, tab_ref, itab_ref, tab_sem)
    scr = (s1_ref, s1_ref, s2_ref)
    gb_ref[...] = dot_nt(low_ref[...], ow_ref[...])
    step = 64
    skip = skip_ref[...]

    def first(i, acc):
        rows = pl.multiple_of(i * step, step)
        for r in range(PH):
            at = pl.ds(r * ML + rows, step)
            gb = gb_ref[at, :]
            gp = gb * gate_ref[0, at, :].astype(F32)
            gl_ref[at, :] = gp.astype(BF16)
            s1_ref[r, pl.ds(rows, step), :] = gb * mixed_ref[at, :].astype(F32)
            gb_ref[at, :] = gp
            prod = gp * gated_ref[at, :].astype(F32)
            for k in range(step // 8):
                acc = acc + prod[k * 8:(k + 1) * 8, :]
        return acc

    acc = lax.fori_loop(0, ML // step, first, jnp.zeros((8, TILE), F32))
    sums_ref[pl.ds(0, 1), :] = jnp.sum(acc, axis=0, keepdims=True)
    for ref in (s1_ref, s2_ref):
        for r in range(2):
            ref[r, pl.ds(ML, PAD), :] = jnp.zeros((PAD, TILE), F32)
    short_back(0, step, scr, taps_ref, proj_ref, gproj_ref, sums_ref)
    ready(0)
    forward_dft(tab_ref, lambda r: gl_ref[pl.ds(r * ML, ML), :], part_ref)
    step2 = 64

    @pl.loop(0, ML // step2)
    def _(i):
        rows = pl.multiple_of(i * step2, step2)
        bins = split_bins(lambda at: part_ref[pl.ds(at, step2), :], rows)
        for other_ref, into_ref in ((spec_ref, turn_ref), (sig_ref, cross_ref)):
            out = []
            for j in range(PH):
                gr, gi = bins[j]
                at = j * 2 * ML + rows
                hr = other_ref[pl.ds(at, step2), :]
                hi = other_ref[pl.ds(at + ML, step2), :]
                out.append((hr * gr + hi * gi, hr * gi - hi * gr))

            def put(at, value, into_ref=into_ref):
                into_ref[pl.ds(at, step2), :] = value

            join_bins(out, put, rows)

    ready(1)
    rates = rates_ref[...]

    @pl.when(pl.program_id(0) == 0)
    def _():
        gsec_ref[...] = jnp.zeros_like(gsec_ref)

    for r in range(PH):
        rows = pl.ds(r * ML, ML)
        freq = pl.ds(r * 2 * ML, 2 * ML)
        gl_ref[rows, :] = (dot_nn(itab_ref[rows, :], cross_ref[freq, :]) * (phase_decay(r, rates) * (1.0 / L))).astype(BF16)
        long_ref[rows, :] = dot_nn(itab_ref[rows, :], turn_ref[freq, :])

    gfw_ref[...] = dot_tn(second_ref[...], gl_ref[...])
    gsec_ref[...] += dot_nt(gl_ref[...], fw_ref[...])

    @pl.loop(0, ML // step)
    def _(i):
        rows = pl.multiple_of(i * step, step)
        for r in range(PH):
            at = pl.ds(r * ML + rows, step)
            gg = long_ref[at, :] + gb_ref[at, :] * skip
            s1_ref[r, pl.ds(rows, step), :] = gg * gate_ref[2, at, :].astype(F32)
            s2_ref[r, pl.ds(rows, step), :] = gg * gate_ref[1, at, :].astype(F32)

    for n in (1, 2):
        short_back(n, step, scr, taps_ref, proj_ref, gproj_ref, sums_ref)


def back(low, inout, gate, proj, gated, mixed, sig, spec, taps3, skip, tab, itab, second, fw, rates):
    tile = lambda h: pl.BlockSpec((h, TILE), lambda i: (0, i))
    tile3 = lambda h: pl.BlockSpec((3, h, TILE), lambda i: (0, 0, i))
    once = lambda h: pl.BlockSpec((h, TILE), lambda i: (0, i), pipeline_mode=pl.Buffered(1))
    width = second.shape[1]
    return pl.pallas_call(
        back_kernel,
        grid=(D // TILE,),
        in_specs=[whole((L, D)), pl.BlockSpec((TILE, D), lambda i: (i, 3)), tile3(L), tile3(L), once(L), once(L),
                  tile(2 * L), tile(2 * L), tile3(3), tile(1), FAR, FAR, whole((L, width)), tile(width), tile(1)],
        out_specs=[tile3(L), tile(width), pl.BlockSpec((L, width), lambda i: (0, 0)), tile(16)],
        out_shape=[
            jax.ShapeDtypeStruct((3, L, D), BF16), jax.ShapeDtypeStruct((width, D), F32),
            jax.ShapeDtypeStruct((L, width), F32), jax.ShapeDtypeStruct((16, D), F32),
        ],
        scratch_shapes=[
            pltpu.VMEM((L, TILE), F32), pltpu.VMEM((L, TILE), BF16), pltpu.VMEM((2 * L, TILE), BF16),
            pltpu.VMEM((2 * L, TILE), BF16), pltpu.VMEM((2 * L, TILE), BF16), pltpu.VMEM((L, TILE), F32),
        ] + [pltpu.VMEM((PH, ML + PAD, TILE), F32)] * 2 + TABLES,
        compiler_params=params(),
        cost_estimate=cost(2 * L * D * D + 12 * L * ML * D, 80 << 20),
        name="back",
    )(low, inout, gate, proj, gated, mixed, sig, spec, taps3, skip, tab, itab, second, fw, rates)


def up_out_kernel(n2_ref, br_ref, gh_ref, low_ref, o_ref):
    j = pl.program_id(0)

    @pl.when(j < FF // D)
    def _():
        o_ref[...] = dot_tn(n2_ref[...], gh_ref[...]).astype(BF16)

    @pl.when(j == FF // D)
    def _():
        o_ref[...] = dot_tn(br_ref[...], low_ref[...]).astype(BF16)


def up_out_grad(n2, branch, gh, low):
    nj = FF // D
    return pl.pallas_call(
        up_out_kernel,
        grid=(nj + 1,),
        in_specs=[whole((L, D)), whole((L, D)), pl.BlockSpec((L, D), lambda j: (0, jnp.minimum(j, nj - 1))), whole((L, D))],
        out_specs=pl.BlockSpec((D, D), lambda j: (0, j)),
        out_shape=jax.ShapeDtypeStruct((D, FF + D), BF16),
        compiler_params=params(),
        cost_estimate=cost(2 * L * D * (FF + D), 40 << 20),
        name="up_out_grad",
    )(n2, branch, gh, low)


def deinterleave(src_ref, mix_ref, put):
    q = ROWS // PH
    for c in range(D // 128):
        lanes = slice(c * 128, (c + 1) * 128)
        mix_ref[c] = src_ref[:, lanes].astype(F32)
        for r in range(PH):
            put(r, lanes, mix_ref[c, pl.ds(r, q, stride=PH), :])


def prep_kernel(x_ref, cot_ref, g_ref, s_ref, xp_ref, cp_ref, n1_ref, mix_ref, flat_ref):
    q = ROWS // PH

    def put_cot(r, lanes, value):
        cp_ref[r, :, lanes] = value.astype(BF16)

    def put_x(r, lanes, value):
        xp_ref[r, :, lanes] = value.astype(BF16)
        flat_ref[pl.ds(r * q, q), lanes] = value

    deinterleave(cot_ref, mix_ref, put_cot)
    deinterleave(x_ref, mix_ref, put_x)
    hat, _ = norm_stats(flat_ref[...])
    n1_ref[...] = (hat * g_ref[...] + s_ref[...]).astype(BF16).reshape(PH, q, D)


def prep(inputs, cotangent, g, s):
    flat = pl.BlockSpec((ROWS, D), lambda i: (i, 0))
    rows = pl.BlockSpec((PH, ROWS // PH, D), lambda i: (0, i, 0))
    out = jax.ShapeDtypeStruct((PH, ML, D), BF16)
    x, cot, n1 = pl.pallas_call(
        prep_kernel,
        grid=(L // ROWS,),
        in_specs=[flat, flat, whole((1, D)), whole((1, D))],
        out_specs=[rows] * 3,
        out_shape=[out] * 3,
        scratch_shapes=[pltpu.VMEM((D // 128, ROWS, 128), F32), pltpu.VMEM((ROWS, D), F32)],
        compiler_params=params(),
        cost_estimate=cost(20 * L * D, 20 << 20),
        name="prep",
    )(inputs, cotangent, g, s)
    return x.reshape(L, D), cot.reshape(L, D), n1.reshape(L, D)


def positions_table(places):
    places = places.astype(F32)
    harmonics = jnp.arange(1, BANDS + 1).astype(F32)
    angles = 2.0 * math.pi / L * places[:, None] * harmonics[None, :]
    return places, jnp.concatenate([places[:, None] / L, jnp.cos(angles), jnp.sin(angles)], axis=1)


def network_layers(places, pos_weight, pos_bias, mid_weight, mid_bias):
    _, features = positions_table(places)
    first = jnp.dot(features, pos_weight, precision=HIGH_ACCURACY) + pos_bias
    layer = jnp.sin(first)
    second = jnp.dot(layer, mid_weight, precision=HIGH_ACCURACY) + mid_bias
    return features, layer, jnp.sin(second), jnp.cos(first), jnp.cos(second)


def network_kernel(grad_ref, feat_ref, layer_ref, slope1_ref, slope2_ref, mid_ref, gpw_ref, gpb_ref, gmw_ref, gmb_ref):
    exact = functools.partial(lax.dot_general, precision=HIGH_ACCURACY, preferred_element_type=F32)
    two = grad_ref[...] * slope2_ref[...]
    gmw_ref[...] = exact(layer_ref[...], two, (((0,), (0,)), ((), ())))
    gmb_ref[...] = jnp.sum(two, axis=0, keepdims=True)
    one = exact(two, mid_ref[...], (((1,), (1,)), ((), ()))) * slope1_ref[...]
    gpw_ref[...] = exact(feat_ref[...], one, (((0,), (0,)), ((), ())))
    gpb_ref[...] = jnp.sum(one, axis=0, keepdims=True)


def network_back(grad, layers, mid_weight):
    features, layer, _, slope1, slope2 = layers
    wide, width = features.shape[1], mid_weight.shape[0]
    shape = lambda n: jax.ShapeDtypeStruct((n, width), F32)
    return pl.pallas_call(
        network_kernel,
        out_shape=[shape(wide), shape(1), shape(width), shape(1)],
        compiler_params=params(),
        cost_estimate=cost(6 * 2 * 3 * L * width * width, 5 << 20),
        name="network_back",
    )(grad, features, layer, slope1, slope2, mid_weight)


def finish_kernel(
    sizes, flat_ref, gain_ref, n1_any, gp_any, iw_any, x_any, gres_any, out_any, rows_ref, total_ref, firsts_ref,
    n1, gp, iw, xs, gres, mix, done_ref, f0, leaving, r1, half, r2, part, r3, sum_ref, f1, g1, f2, g2, g3, u1, u2, u3, sem_s, sem_r, sem_l,
):
    mp, z = sizes
    me = {name: lax.axis_index(name) for name in ("z", "core", "mp")}
    other = {"core": 1 - me["core"]}
    to_mp = [(b, {"mp": lax.rem(me["mp"] + b, mp)}) for b in range(1, mp)]
    to_z = [(b, {"z": lax.rem(me["z"] + b, z)}) for b in range(1, z)]
    q = ROWS // PH
    tiles = L // ROWS

    def load(i, src, dst):
        out = pltpu.make_async_copy(src, dst, sem_l.at[i])
        out.start()
        return out

    chunks, _, rows, width = half.shape
    piece = width // z
    loads, stores = {}, {}

    def fetch_chunk(c):
        if c < chunks:
            at = pl.ds(c * width % D, width)
            loads["g", c] = [load(1 + c, gp_any.at[c * width // D, :, :, at], gp.at[c * width // D, :, :, at])]

    def fetch_tile(i):
        if i < tiles:
            at = pl.ds(i * q, q)
            base = 2 + chunks + 2 * i
            loads["t", i] = [load(base, x_any.at[:, at], xs.at[i % 2]), load(base + 1, gres_any.at[:, at], gres.at[i % 2])]

    def grad_chunk(c):
        for item in ([loads["n1"]] if c == 0 else []) + loads["g", c]:
            item.wait()
        fetch_chunk(c + 2)
        if c + 2 == chunks:
            loads["iw"] = load(1 + chunks, iw_any.at[:, pl.ds(0, 3 * D)], iw)
        if c + 1 == chunks:
            fetch_tile(0)
            fetch_tile(1)
        at = c * width % D
        g = gp[c * width // D, :, :, at:at + width].reshape(L, width)
        value = dot_tn(n1[...], g).astype(BF16).reshape(mp, 2, rows, width)
        half[c] = jnp.where(me["core"] == 0, value[:, 0], value[:, 1])
        leaving[c] = jnp.where(me["core"] == 0, value[:, 1], value[:, 0])
        first[c] = copy(leaving.at[c], r1.at[c], other)

    def last_tile(i):
        at = pl.ds(i * q, q)
        for item in ([loads["iw"]] if i == 0 else []) + loads["t", i]:
            item.wait()
        both = jnp.concatenate([gp[n, :, at].reshape(ROWS, D) for n in range(3)], axis=1)
        gn = dot_nt(both, iw[...])
        hat, inv = norm_stats(xs[i % 2].reshape(ROWS, D).astype(F32))
        e = gn * gain_ref[...]
        fix = jnp.mean(e, axis=-1, keepdims=True) + hat * jnp.mean(e * hat, axis=-1, keepdims=True)
        if i >= 2:
            stores[i - 2].wait()
        interleave(gres[i % 2].reshape(ROWS, D) + inv * (e - fix), mix, done_ref.at[i % 2])
        stores[i] = load(2 + chunks + 2 * tiles + i, done_ref.at[i % 2], out_any.at[pl.ds(i * ROWS, ROWS)])
        fetch_tile(i + 2)
        return jnp.sum(gn * hat, axis=0, keepdims=True), jnp.sum(gn, axis=0, keepdims=True)

    loads["n1"] = load(0, n1_any, n1)
    fetch_chunk(0)
    fetch_chunk(1)
    barrier = pltpu.get_barrier_semaphore()
    peers = [other] + [p for _, p in to_mp] + [p for _, p in to_z]
    for peer in peers:
        pl.semaphore_signal(barrier, inc=1, device_id=peer, device_id_type=pl.DeviceIdType.MESH)
    pl.semaphore_wait(barrier, len(peers))

    count = [0]

    def copy(src, dst, peer):
        i = count[0]
        count[0] += 1
        out = pltpu.make_async_remote_copy(
            src_ref=src, dst_ref=dst, send_sem=sem_s.at[i], recv_sem=sem_r.at[i], device_id=peer,
            device_id_type=pl.DeviceIdType.MESH,
        )
        out.start()
        return out

    sent = []

    def wait(copies):
        for c in copies:
            c.wait_recv()
        sent.extend(copies)

    cols = lambda i: pl.ds(pl.multiple_of(i * piece, piece), piece)
    mine = cols(me["z"])
    first = {}
    flat_now = [[copy(flat_ref.at[1 - me["core"]], g1, other)]]
    second, third, fourth, fifth = {}, {}, {}, {}

    def step_one(c):
        wait([first[c]])
        half[c] = (half[c].astype(F32) + r1[c].astype(F32)).astype(BF16)
        second[c] = [copy(half.at[c, p["mp"]], r2.at[c, b - 1], p) for b, p in to_mp]

    def step_two(c):
        total = half[c, me["mp"]].astype(F32)
        for b in range(mp - 1):
            total = total + r2[c, b].astype(F32)
        part[c] = total.astype(BF16)
        third[c] = [copy(part.at[c, :, cols(p["z"])], r3.at[c, b - 1], p) for b, p in to_z]

    def step_three(c):
        wait(third[c])
        total = part[c, :, mine].astype(F32)
        for b in range(z - 1):
            total = total + r3[c, b].astype(F32)
        sum_ref[me["core"], c, :, mine] = total.astype(BF16)
        here = sum_ref.at[me["core"], c, :, mine]
        fourth[c] = [copy(here, here, p) for b, p in to_z]

    def step_four(c):
        wait(fourth[c])
        here = sum_ref.at[me["core"], c]
        fifth[c] = copy(here, here, other)

    def flat_sum(value, got):
        for b in range(got.shape[0]):
            value = value + got[b]
        return value

    def flat_step(i):
        core, at = me["core"], total_ref.at
        if i == 0:
            wait(flat_now[0])
            f1[...] = flat_ref[core] + g1[...]
            flat_now[0] = [copy(f1.at[p["mp"]], g2.at[b - 1], p) for b, p in to_mp]
        elif i == 1:
            wait(flat_now[0])
            f2[...] = flat_sum(f1[me["mp"]], g2)
            flat_now[0] = [copy(f2.at[p["z"]], g3.at[b - 1], p) for b, p in to_z]
        elif i == 2:
            wait(flat_now[0])
            total_ref[core, me["mp"], me["z"]] = flat_sum(f2[me["z"]], g3)
            own = at[core, me["mp"], me["z"]]
            flat_now[0] = [copy(own, own, p) for b, p in to_z]
        elif i == 3:
            wait(flat_now[0])
            own = at[core, me["mp"]]
            flat_now[0] = [copy(own, own, p) for b, p in to_mp]
        elif i == 4:
            wait(flat_now[0])
            own = at[core]
            flat_now[0] = [copy(own, own, other)]

    first_now = [None]

    def first_step(i):
        if i == 0:
            for n, value in enumerate((gain_sum, shift_sum)):
                for j in range(D // 128):
                    f0[0, n * 8 + j:n * 8 + j + 1, :] = value[:, j * 128:(j + 1) * 128]
            first_now[0] = [copy(f0.at[0], u1, other)]
        elif i == 1:
            wait(first_now[0])
            f0[1] = f0[0] + u1[...]
            first_now[0] = [copy(f0.at[1], u2.at[b - 1], p) for b, p in to_mp]
        elif i == 2:
            wait(first_now[0])
            f0[2] = flat_sum(f0[1], u2)
            first_now[0] = [copy(f0.at[2], u3.at[b - 1], p) for b, p in to_z]

    one = two = three = four = flats = 0

    def middle():
        nonlocal one, two, three, flats
        if two < one:
            wait(second[two])
            if one < min(chunks, len(first)):
                step_one(one)
                one += 1
            step_two(two)
            two += 1
        if three < two and (three < two - 1 or two == chunks):
            step_three(three)
            three += 1
        flat_step(flats)
        flats += 1

    def back_to_core():
        nonlocal four
        if four < three and (four < three - 1 or three == chunks):
            step_four(four)
            four += 1

    gain_sum = shift_sum = None
    for k in range(chunks + tiles):
        if k < chunks:
            grad_chunk(k)
        else:
            gain, shift = last_tile(k - chunks)
            gain_sum = gain if gain_sum is None else gain_sum + gain
            shift_sum = shift if shift_sum is None else shift_sum + shift
        if k >= 1 and one < min(2, chunks):
            step_one(one)
            one += 1
        elif k >= 3 and k % 2 == 1:
            middle()
        elif k >= 3:
            back_to_core()
    ends = 0
    while four < chunks or flats < 5 or ends < 3:
        first_step(ends)
        ends += 1
        middle()
        back_to_core()
    for i in (tiles - 2, tiles - 1):
        stores[i].wait()
    wait(first_now[0])
    firsts_ref[...] = flat_sum(f0[2], u3)
    wait(flat_now[0] + [fifth[c] for c in range(chunks)])
    for c in range(chunks):
        for core in range(2):
            rows_ref[core, :, c * width:(c + 1) * width] = sum_ref[core, c].astype(F32)
    for c in sent:
        c.wait_send()


def finish(flat, gain, n1, gproj, in_w, x, gres):
    mp, z = lax.axis_size("mp"), lax.axis_size("z")
    width = 128 * z
    chunks = 3 * D // width
    rows = D // (2 * mp)
    word = flat.shape[-1]
    tiles, q = L // ROWS, ROWS // PH
    copies = chunks * (2 + (mp - 1) + 2 * (z - 1)) + 3 + 3 * (mp - 1) + 3 * (z - 1)
    vm = lambda *shape: pltpu.VMEM(shape, BF16)
    vf = lambda *shape: pltpu.VMEM(shape, F32)
    spec = pl.BlockSpec(memory_space=pltpu.VMEM)
    fold = lambda a: a.reshape(PH, ML, D)
    out, row_sum, total, firsts = pl.pallas_call(
        functools.partial(finish_kernel, (mp, z)),
        in_specs=[spec] * 2 + [FAR] * 5,
        out_specs=[FAR] + [spec] * 3,
        out_shape=[
            jax.ShapeDtypeStruct((L, D), BF16), jax.ShapeDtypeStruct((2, rows, 3 * D), F32),
            jax.ShapeDtypeStruct(flat.shape, F32), jax.ShapeDtypeStruct((16, 128), F32),
        ],
        scratch_shapes=[
            vm(L, D), vm(3, PH, ML, D), vm(D, 3 * D), vm(2, PH, q, D), vf(2, PH, q, D), vf(D // 128, ROWS, 128),
            vm(2, ROWS, D), vf(3, 16, 128), vm(chunks, mp, rows, width), vm(chunks, mp, rows, width),
            vm(chunks, mp, rows, width), vm(chunks, mp - 1, rows, width), vm(chunks, rows, width),
            vm(chunks, z - 1, rows, width // z), vm(2, chunks, rows, width),
            vf(mp, z, 8, word), vf(mp, z, 8, word), vf(z, 8, word), vf(mp - 1, z, 8, word), vf(z - 1, 8, word),
            vf(16, 128), vf(mp - 1, 16, 128), vf(z - 1, 16, 128),
            pltpu.SemaphoreType.DMA((copies,)), pltpu.SemaphoreType.DMA((copies,)),
            pltpu.SemaphoreType.DMA((2 + chunks + 3 * tiles,)),
        ],
        compiler_params=params(collective_id=0, has_side_effects=True),
        cost_estimate=cost(2 * 2 * L * D * 3 * D, 60 << 20),
        name="finish",
    )(flat, gain, n1, gproj.reshape(3, PH, ML, D), in_w, fold(x), fold(gres))
    return out, row_sum.reshape(2 * rows, 3 * D), total, firsts


VECTORS = (
    ("first_gain", 1), ("first_shift", 1), ("in_bias", 3), ("short", 9), ("skip", 1), ("out_bias", 1),
    ("second_gain", 1), ("second_shift", 1), ("up_bias", 4), ("down_bias", 1),
)


def swap_bit(x, axis, bit):
    size = lax.axis_size(axis)
    return lax.ppermute(x, axis, [(i, i ^ bit) for i in range(size)])


def add_low(*parts):
    total = parts[0].astype(F32)
    for part in parts[1:]:
        total = total + part.astype(F32)
    return total.astype(BF16)


def hold(*values):
    return lax.optimization_barrier(values)


def entry(x, i):
    return lax.dynamic_index_in_dim(x, i, 0, False)


def in_order(pieces, axis):
    place = lax.axis_index(axis)
    stacked = jnp.stack(pieces)
    return jnp.concatenate([entry(stacked, place ^ i) for i in range(len(pieces))], axis=0)


def spread_steps(x, axis, add):
    place = lax.axis_index(axis)
    got = yield [(entry(x, place ^ b), axis, b) for b in range(1, x.shape[0])]
    return add(entry(x, place), *got)


def collect_steps(x, axis):
    got = yield [(x, axis, b) for b in range(1, lax.axis_size(axis))]
    return in_order([x] + list(got), axis)


def both_cores(mine, other):
    core = lax.axis_index("core")
    low = jnp.where(core == 0, mine, other)
    high = jnp.where(core == 0, other, mine)
    return jnp.concatenate([low, high], axis=0).astype(F32)


def share_steps(share):
    z = lax.axis_size("z")
    rows, cols = share.shape
    mine = yield from spread_steps(share.reshape(z, rows // z, cols), "z", add_low)
    mine = yield from collect_steps(mine, "z")
    return (yield from collect_steps(mine, "core")).astype(F32)


class Chains:
    def __init__(self):
        self.live, self.done = {}, {}

    def start(self, name, steps):
        self.live[name] = (steps, next(steps))

    def move(self, names, first, kernel):
        names = [n for n in names if n in self.live]
        sends = [send for n in names for send in self.live[n][1]]
        held = hold(first, *(s[0] for s in sends))
        got = [swap_bit(v, s[1], s[2]) for v, s in zip(held[1:], sends)]
        out = kernel(held[0])
        flat, tree = jax.tree.flatten(out)
        held = hold(*flat, *got)
        out = jax.tree.unflatten(tree, held[:len(flat)])
        got = list(held[len(flat):])
        for n in names:
            steps, wanted = self.live.pop(n)
            arrived, got = got[:len(wanted)], got[len(wanted):]
            try:
                self.live[n] = (steps, steps.send(arrived))
            except StopIteration as stop:
                self.done[n] = stop.value
        return out

    def finish(self):
        while self.live:
            self.move(list(self.live), jnp.zeros((8, 128), F32), lambda v: v)


def scatter_rows(grad):
    return lax.psum_scatter(grad, ("mp", "core"), scatter_dimension=0, tiled=True)


def gather_rows(shard):
    rows = shard.shape[0]
    half = lax.dynamic_slice_in_dim(shard, lax.axis_index("core") * (rows // 2), rows // 2, 0)
    return lax.all_gather(half, ("mp", "core"), axis=0, tiled=True)


def shards(
    inputs, first_gain, first_shift, in_weight, in_bias, short_weight, skip_gain, pos_weight, pos_bias,
    mid_weight, mid_bias, filter_weight, decay_rates, out_weight, out_bias, second_gain, second_shift,
    up_weight, up_bias, down_weight, down_bias, cotangent,
):
    mp = lax.axis_size("mp")
    own = D // mp
    local = (first_gain, first_shift, in_bias, short_weight, skip_gain, out_bias, second_gain, second_shift, up_bias, down_bias)
    packed = jnp.concatenate([v.reshape(-1) for v in local]).reshape(1, -1)
    spread = in_order([packed] + [swap_bit(packed, "mp", b) for b in range(1, mp)], "mp").astype(F32)
    full = {}
    at = 0
    for name, count in VECTORS:
        part = spread[:, at:at + count * own]
        at += count * own
        if name == "short":
            part = part.reshape(mp, 3, 3 * own).swapaxes(0, 1)
            full[name] = part.reshape(3, 3 * D)
        else:
            full[name] = part.reshape(1, count * D)
    inout = gather_rows(jnp.concatenate([in_weight, out_weight], axis=1))
    up_matrix = gather_rows(up_weight)
    down_matrix = gather_rows(down_weight)

    tab, itab = (jnp.asarray(t) for t in dft_tables())
    x, cot, n1 = prep(inputs, cotangent, full["first_gain"], full["first_shift"])
    places = (jnp.arange(PH)[:, None] + PH * jnp.arange(ML)[None, :]).reshape(L)
    layers = network_layers(places, pos_weight, pos_bias, mid_weight, mid_bias)
    second = layers[2]
    rates = decay_rates.reshape(1, D)
    spec = filter_spectrum(tab, second, filter_weight, rates)
    proj, gate, gated, mixed, branch, sig = front(n1, inout, full["in_bias"], full["short"], full["skip"], tab, itab, spec)
    res, n2 = mid_stage(x, branch, inout, full["out_bias"], full["second_gain"], full["second_shift"])
    act, slope = up_stage(n2, up_matrix, full["up_bias"])
    down_grad = weight_grad(act, cot, 1024, 1024, "down_weight_grad")
    act, down_grad = hold(act, down_grad)
    block_out, gh, gres, low, sums_two, up_bias_sum = down_stage(act, slope, res, cot, down_matrix, full["down_bias"], up_matrix, full["second_gain"])
    down_share = scatter_rows(down_grad)
    chains = Chains()
    low, down_share = hold(low, down_share)
    chains.start("down", share_steps(down_share))
    up_out = chains.move(["down"], low, lambda v: up_out_grad(n2, branch, gh, v))
    low, up_out = hold(low, up_out)
    up_share = scatter_rows(up_out)
    taps3 = full["short"].reshape(3, 3, D).swapaxes(0, 1)
    kept = (inout, gate, proj, gated, mixed, sig, spec, taps3, full["skip"], tab, itab, second.astype(BF16), filter_weight.astype(BF16), rates)
    gproj, gfw, gsec, sums_mid = chains.move(["down"], low, lambda v: back(v, *kept))
    gproj, gsec, up_share = hold(gproj, gsec, up_share)
    up_half = lax.psum(up_share, "z")
    net = tuple(chains.move(["down"], gsec, lambda v: network_back(v, layers, mid_weight))) + (gfw,)
    mids = sums_mid[1:13].reshape(3, 4, D)
    vectors = {
        "in_bias": mids[:, 0].reshape(3 * D), "short": mids[:, 1:].swapaxes(0, 1).reshape(3, 3 * D), "skip": sums_mid[0],
        "out_bias": sums_two[2], "second_gain": sums_two[0], "second_shift": sums_two[1], "up_bias": up_bias_sum[0],
        "down_bias": sums_two[3],
    }
    by_owner = lambda name, count: vectors[name].reshape(-1, mp, count * own).swapaxes(0, 1).reshape(mp, -1)
    middle = [(name, 3 if name == "short" else count) for name, count in VECTORS[2:]]
    flats = [jnp.concatenate([by_owner(*item) for item in middle], axis=1).reshape(-1)]
    flats += [n.reshape(-1) for n in net]
    length = sum(f.shape[0] for f in flats)
    group = (2, mp, lax.axis_size("z"), 8)
    count = math.prod(group)
    word = -(-length // (128 * count)) * 128
    flat = jnp.concatenate(flats + [jnp.zeros((count * word - length,), F32)]).reshape(group + (word,))
    kernel = lambda v: finish(flat, full["first_gain"], n1, v, inout, x, gres)
    input_grad, in_sum, flat_sum, firsts = kernel(gproj)
    in_sum, up_half = hold(in_sum, up_half)
    up_both = both_cores(up_half, swap_bit(up_half, "core", 1))
    done = chains.done
    down_sum = done["down"]
    up_sum, out_sum = up_both[:, :FF], up_both[:, FF:]
    me = lax.axis_index("mp")
    firsts = firsts.reshape(2, D)
    mine = {
        "first_gain": lax.dynamic_slice_in_dim(firsts[0], me * own, own, 0),
        "first_shift": lax.dynamic_slice_in_dim(firsts[1], me * own, own, 0),
    }
    flat_sum = flat_sum.reshape(-1)
    span = sum(count for _, count in VECTORS[2:]) * own
    local = lax.dynamic_slice_in_dim(flat_sum, me * span, span, 0)
    at = 0
    for name, count in VECTORS[2:]:
        mine[name] = local[at:at + count * own]
        at += count * own
    mine["short"] = mine["short"].reshape(3, 3 * own)
    at = mp * span
    pieces = []
    for n in net:
        pieces.append(flat_sum[at:at + n.size])
        at += n.size
    net_sum = [p.reshape(n.shape) for p, n in zip(pieces, (pos_weight, pos_bias, mid_weight, mid_bias, filter_weight))]
    return (
        block_out, input_grad, mine["first_gain"], mine["first_shift"], in_sum, mine["in_bias"], mine["short"], mine["skip"],
        *net_sum, out_sum, mine["out_bias"], mine["second_gain"], mine["second_shift"], up_sum, mine["up_bias"],
        down_sum, mine["down_bias"],
    )


def solution(mesh):
    dp, mp = mesh.devices.shape
    split = jax.sharding.Mesh(mesh.devices.reshape(dp // 2, 2, mp), ("z", "core", "mp"))
    tokens = P(("z", "core", "mp"), None)
    row, vec, rep = P("mp", None), P("mp"), P()
    return jax.shard_map(
        shards,
        mesh=split,
        in_specs=(
            tokens, vec, vec, row, vec, P(None, "mp"), vec, rep, rep, rep, rep, rep, rep, row, vec, vec, vec, row, vec, row,
            vec, tokens,
        ),
        out_specs=(
            tokens, tokens, vec, vec, row, vec, P(None, "mp"), vec, rep, rep, rep, rep, rep, row, vec, vec, vec, row, vec,
            row, vec,
        ),
        check_vma=False,
    )
```
